32 devices in a mesh: batch: 8 (over z, y), mp: 4 (over x, core).
Axes of the slice: x: 2, y: 2, z: 4, core: 2. Of those that a mesh axis runs over, the one named last changes fastest.
Arguments:
- tokens: bfloat16 [784, 16, 768], P('mp', 'batch'), may hold values from -6 to 6
- segment_ids: int32 [16, 784], P('batch'), may hold values from 0 to 3, never falling along the last dimension, each value on 1 to 392 neighbouring positions
- bucket_ids: int32 [1567], replicated, may hold values from 0 to 255
- memory: bfloat16 [256, 16, 768], P('batch'), may hold values from -80 to 80
- memory_mask: int32 [16, 256], P('batch'), may hold values from 0 to 1, as said below
- cotangent: bfloat16 [784, 16, 768], P('mp', 'batch'), may hold values from -6 to 6
- self_gain: float32 [768], replicated, may hold values from 0.1 to 1.9
- self_bias: float32 [768], replicated, may hold values from -1.5 to 1.5
- query_weight: bfloat16 [768, 768], P(None, 'mp'), may hold values from -0.21875 to 0.21875
- key_weight: bfloat16 [768, 768], P(None, 'mp'), may hold values from -0.21875 to 0.21875
- value_weight: bfloat16 [768, 768], P(None, 'mp'), may hold values from -0.21875 to 0.21875
- rel_table: float32 [256, 12], P(None, 'mp'), may hold values from -4 to 4
- head_scale: float32 [12], P('mp'), may hold values from 0.1 to 1.9
- output_weight: bfloat16 [768, 768], P('mp'), may hold values from -0.21875 to 0.21875
- after_gain: float32 [768], replicated, may hold values from 0.1 to 1.9
- after_bias: float32 [768], replicated, may hold values from -1.5 to 1.5
- cross_gain: float32 [768], replicated, may hold values from 0.1 to 1.9
- cross_bias: float32 [768], replicated, may hold values from -1.5 to 1.5
- batch_gain: float32 [768], replicated, may hold values from 0.1 to 1.9
- batch_bias: float32 [768], replicated, may hold values from -1.5 to 1.5
- cross_query: bfloat16 [768, 768], P(None, 'mp'), may hold values from -0.21875 to 0.21875
- cross_key: bfloat16 [768, 768], P(None, 'mp'), may hold values from -0.21875 to 0.21875
- cross_value: bfloat16 [768, 768], P(None, 'mp'), may hold values from -0.21875 to 0.21875
- cross_output: bfloat16 [768, 768], P('mp'), may hold values from -0.21875 to 0.21875
- crossout_gain: float32 [768], replicated, may hold values from 0.1 to 1.9
- crossout_bias: float32 [768], replicated, may hold values from -1.5 to 1.5
- ffn_gain: float32 [768], replicated, may hold values from 0.1 to 1.9
- ffn_bias: float32 [768], replicated, may hold values from -1.5 to 1.5
- up_weight: bfloat16 [768, 3072], P(None, 'mp'), may hold values from -2 to 2
- middle_gain: float32 [3072], P('mp'), may hold values from 0.1 to 1.9
- middle_bias: float32 [3072], P('mp'), may hold values from -1.5 to 1.5
- down_weight: bfloat16 [3072, 768], P('mp'), may hold values from -0.109375 to 0.109375
Outputs:
- output: bfloat16 [784, 16, 768], P('mp', 'batch')
- grad_tokens: float32 [784, 16, 768], P('mp', 'batch')
- grad_memory: float32 [256, 16, 768], P('batch', None, 'mp')
- grad_self_gain: float32 [768], replicated
- grad_self_bias: float32 [768], replicated
- grad_query_weight: float32 [768, 768], P(None, 'mp')
- grad_key_weight: float32 [768, 768], P(None, 'mp')
- grad_value_weight: float32 [768, 768], P(None, 'mp')
- grad_rel_table: float32 [256, 12], P(None, 'mp')
- grad_head_scale: float32 [12], P('mp')
- grad_output_weight: float32 [768, 768], P('mp')
- grad_after_gain: float32 [768], replicated
- grad_after_bias: float32 [768], replicated
- grad_cross_gain: float32 [768], replicated
- grad_cross_bias: float32 [768], replicated
- grad_batch_gain: float32 [768], P('mp')
- grad_batch_bias: float32 [768], P('mp')
- grad_cross_query: float32 [768, 768], P(None, 'mp')
- grad_cross_key: float32 [768, 768], P(None, 'mp')
- grad_cross_value: float32 [768, 768], P(None, 'mp')
- grad_cross_output: float32 [768, 768], P('mp')
- grad_crossout_gain: float32 [768], replicated
- grad_crossout_bias: float32 [768], replicated
- grad_ffn_gain: float32 [768], replicated
- grad_ffn_bias: float32 [768], replicated
- grad_up_weight: float32 [768, 3072], P(None, 'mp')
- grad_middle_gain: float32 [3072], P('mp')
- grad_middle_bias: float32 [3072], P('mp')
- grad_down_weight: float32 [3072, 768], P('mp')
The draws below stay inside these ranges and needn't reach their ends.
Inputs may be any that keep to these rules, and one draw needn't show every extreme that they name: `segment_ids`: ids of a row never fall. `memory_mask`: the valid positions of each sample form a prefix of at least 64 positions.
All inputs are finite; a program needn't handle non-finite values.
Results may differ from the reference program's by a relative error of at most 0.02.
The reference program's roundings to bfloat16 on the way count: a program that leaves them out, or rounds other values in their place, can miss the bound.
Values may be sent and summed in bfloat16 or wider, within the bound.
No kernel may reach another device: no remote copies, remote signals or barrier semaphores. Data moves between devices by JAX's collectives and lax.ppermute only.
A program may use at most 256 MiB of HBM per device.

```python
import math
from functools import partial
import jax
import jax.numpy as jnp
import numpy as np
from jax import lax

D = 768
HEADS = 12
HEAD_DIM = 64
FF = 3072
BUCKETS = 256
SEQ = 784
MEM = 256
ROWS = 16


def draw_memory(key, part):
    noise_key, center_key, sample_key = jax.random.split(jax.random.fold_in(key, 11), 3)
    places = jnp.arange(MEM).astype(jnp.float32) / (MEM - 1)
    noise = jax.random.normal(noise_key, (MEM, ROWS, D), jnp.float32)
    center = jax.random.uniform(center_key, (D,), jnp.float32, -1.0, 1.0)
    sample = jnp.exp(jax.random.uniform(sample_key, (ROWS,), jnp.float32, 0.0, math.log(3.5)))
    rising = jnp.exp(math.log(3.0) * places)
    return (center[None, None, :] + noise * rising[:, None, None] * sample[None, :, None]).astype(jnp.bfloat16)


def draw_memory_mask(key, part):
    filled = jax.random.randint(jax.random.fold_in(key, 23), (ROWS,), MEM // 4, MEM + 1)
    filled = jnp.where(jnp.arange(ROWS) == 0, MEM, filled)
    return (jnp.arange(MEM)[None, :] < filled[:, None]).astype(jnp.int32)


def draw_up_weight(key, part):
    base_key, column_key = jax.random.split(jax.random.fold_in(key, 37))
    columns = jnp.arange(FF).astype(jnp.float32) / (FF - 1)
    base = jax.random.normal(base_key, (D, FF), jnp.float32)
    extra = jnp.exp(jax.random.uniform(column_key, (FF,), jnp.float32, 0.0, math.log(3.0)))
    rising = jnp.exp(math.log(3.0) * columns)
    return jnp.clip(base * D ** (-0.5) * (rising * extra / 3.0)[None, :], -1.98, 1.98).astype(jnp.bfloat16)


def with_ends(values, stream_key, smallest, largest):
    shape = values.shape
    place = [jax.random.randint(jax.random.fold_in(stream_key, axis), (), 0, shape[axis]) for axis in range(len(shape))]
    values = values.at[tuple(place)].set(smallest)
    longest = shape.index(max(shape))
    place[longest] = (place[longest] + 1) % shape[longest]
    return values.at[tuple(place)].set(largest)


def block_scale(key, extent, cuts, least, top_value):
    level = 1.0
    for position, shards_of in cuts:
        draws = jax.random.uniform(jax.random.fold_in(jax.random.fold_in(key, 6), position), (shards_of,), jnp.float32, least / len(cuts), top_value / len(cuts))
        level = level * jnp.repeat(jnp.exp(draws), extent[position] // shards_of).reshape((-1,) + (1,) * (len(extent) - 1 - position))
    return level


def split_up(amount, total, most, slope):
    loads = [(1 << 20) // math.isqrt(standing ** slope) + 1 for standing in range(2, amount + 1)]
    rest, counts = total - most - (amount - 1), [1] * (amount - 1)
    while rest > 0:
        free = [i for i in range(amount - 1) if counts[i] < most]
        mass, left = sum([loads[i] for i in free]), rest
        for i in free:
            more = min(most - counts[i], max(1, left * loads[i] // mass), rest)
            counts[i] = counts[i] + more
            rest = rest - more
    return np.array([most] + counts)


def ragged_sizes(rng, amount, total, reach, skew):
    if amount == 2:
        one = jax.random.randint(rng, (), max(1, total - reach), min(reach, total - 1) + 1)
        return jnp.stack([one, total - one])
    tallies = jnp.asarray(split_up(amount, total, reach, skew), jnp.int32)
    pairs = (amount - 1) // 2
    donor, receiver = tallies[1:1 + 2 * pairs:2], tallies[2:2 + 2 * pairs:2]
    margin = jnp.minimum(donor - 1, reach - receiver)
    shifted = jax.random.randint(jax.random.fold_in(rng, 1), (pairs,), 0, 1 << 20) % (margin + 1)
    tallies = tallies.at[1:1 + 2 * pairs:2].set(donor - shifted).at[2:2 + 2 * pairs:2].set(receiver + shifted)
    return tallies[jax.random.permutation(jax.random.fold_in(rng, 2), amount)]


def centred(key, dims, scale, most, cuts=(), dtype=jnp.bfloat16):
    entries = jax.random.normal(key, dims, jnp.float32) * scale
    if len(cuts) > 0:
        entries = block_scale(key, dims, cuts, -0.22, 0.18) * entries
    return jnp.clip(entries, min=-most, max=most).astype(dtype)


def setup_inputs(seed: int = 0) -> dict:
    arg_keys = jax.random.split(jax.random.key(seed), 33)
    tokens = centred(arg_keys[0], (SEQ, ROWS, D), 1.0, 6.0, ((0, 4), (1, 8)))
    segment_ids = jax.vmap(lambda own: jnp.searchsorted(jnp.cumsum(ragged_sizes(own, 4, SEQ, SEQ // 2, 1)), jnp.arange(SEQ), side="right"))(jax.random.split(arg_keys[1], ROWS)).reshape((ROWS, SEQ)).astype(jnp.int32)
    bucket_ids = with_ends(jax.random.randint(arg_keys[2], (2 * SEQ - 1,), 0, BUCKETS), jax.random.fold_in(arg_keys[2], 1), 0, BUCKETS - 1).astype(jnp.int32)
    memory = draw_memory(jax.random.fold_in(arg_keys[32], 71), 0)
    memory_mask = draw_memory_mask(jax.random.fold_in(arg_keys[32], 71), 0)
    cotangent = centred(arg_keys[5], (SEQ, ROWS, D), 1.0, 6.0, ((0, 4), (1, 8)))
    self_gain = jnp.clip(1.0 + 0.18 * jax.random.normal(arg_keys[6], (D,), jnp.float32), 0.1, 1.9)
    self_bias = centred(arg_keys[7], (D,), 0.3, 1.5, (), jnp.float32)
    query_weight = centred(arg_keys[8], (D, D), D ** -0.5, 0.21875, ((1, 4),))
    key_weight = centred(arg_keys[9], (D, D), D ** -0.5, 0.21875, ((1, 4),))
    value_weight = centred(arg_keys[10], (D, D), D ** -0.5, 0.21875, ((1, 4),))
    rel_table = centred(arg_keys[11], (BUCKETS, HEADS), 1.0, 4.0, ((1, 4),), jnp.float32)
    head_scale = jnp.clip(1.0 + 0.18 * jax.random.normal(arg_keys[12], (HEADS,), jnp.float32), 0.1, 1.9)
    output_weight = centred(arg_keys[13], (D, D), D ** -0.5, 0.21875, ((0, 4),))
    after_gain = jnp.clip(1.0 + 0.18 * jax.random.normal(arg_keys[14], (D,), jnp.float32), 0.1, 1.9)
    after_bias = centred(arg_keys[15], (D,), 0.3, 1.5, (), jnp.float32)
    cross_gain = jnp.clip(1.0 + 0.18 * jax.random.normal(arg_keys[16], (D,), jnp.float32), 0.1, 1.9)
    cross_bias = centred(arg_keys[17], (D,), 0.3, 1.5, (), jnp.float32)
    batch_gain = jnp.clip(1.0 + 0.18 * jax.random.normal(arg_keys[18], (D,), jnp.float32), 0.1, 1.9)
    batch_bias = centred(arg_keys[19], (D,), 0.3, 1.5, (), jnp.float32)
    cross_query = centred(arg_keys[20], (D, D), D ** -0.5, 0.21875, ((1, 4),))
    cross_key = centred(arg_keys[21], (D, D), D ** -0.5, 0.21875, ((1, 4),))
    cross_value = centred(arg_keys[22], (D, D), D ** -0.5, 0.21875, ((1, 4),))
    cross_output = centred(arg_keys[23], (D, D), D ** -0.5, 0.21875, ((0, 4),))
    crossout_gain = jnp.clip(1.0 + 0.18 * jax.random.normal(arg_keys[24], (D,), jnp.float32), 0.1, 1.9)
    crossout_bias = centred(arg_keys[25], (D,), 0.3, 1.5, (), jnp.float32)
    ffn_gain = jnp.clip(1.0 + 0.18 * jax.random.normal(arg_keys[26], (D,), jnp.float32), 0.1, 1.9)
    ffn_bias = centred(arg_keys[27], (D,), 0.3, 1.5, (), jnp.float32)
    up_weight = draw_up_weight(jax.random.fold_in(arg_keys[32], 71), 0)
    middle_gain = jnp.clip(1.0 + 0.18 * jax.random.normal(arg_keys[29], (FF,), jnp.float32), 0.1, 1.9)
    middle_bias = centred(arg_keys[30], (FF,), 0.3, 1.5, ((0, 4),), jnp.float32)
    down_weight = centred(arg_keys[31], (FF, D), FF ** -0.5, 0.109375, ((0, 4),))
    return dict(tokens=tokens, segment_ids=segment_ids, bucket_ids=bucket_ids, memory=memory, memory_mask=memory_mask, cotangent=cotangent, self_gain=self_gain, self_bias=self_bias, query_weight=query_weight, key_weight=key_weight, value_weight=value_weight, rel_table=rel_table, head_scale=head_scale, output_weight=output_weight, after_gain=after_gain, after_bias=after_bias, cross_gain=cross_gain, cross_bias=cross_bias, batch_gain=batch_gain, batch_bias=batch_bias, cross_query=cross_query, cross_key=cross_key, cross_value=cross_value, cross_output=cross_output, crossout_gain=crossout_gain, crossout_bias=crossout_bias, ffn_gain=ffn_gain, ffn_bias=ffn_bias, up_weight=up_weight, middle_gain=middle_gain, middle_bias=middle_bias, down_weight=down_weight)


@jax.custom_vjp
def low(v):
    return lax.optimization_barrier(v.astype(jnp.bfloat16)).astype(jnp.float32)

@jax.custom_vjp
def low_back(v):
    return v

def low_keep(v):
    return (low(v), None)

def low_pass(kept, grad):
    return (grad,)

def back_keep(v):
    return (v, None)

def back_low(kept, grad):
    return (low(grad),)
low.defvjp(low_keep, low_pass)
low_back.defvjp(back_keep, back_low)
EPSILON = 1e-05
MASKED = -1e+30
HIGHEST = lax.Precision.HIGHEST

def both_ways(value):
    return low_back(low(value))

def project(left, weight):
    return jnp.einsum('srd,dc->src', left, weight, precision=HIGHEST)

def layer_norm(values, gain, bias):
    center = values - lax.optimization_barrier(jnp.mean(values, -1, keepdims=True))
    spread = lax.optimization_barrier(jnp.mean(center * center, -1, keepdims=True))
    return center * lax.rsqrt(spread + EPSILON) * gain + bias

def position_bias(table, bucket_ids):
    length = (bucket_ids.shape[0] + 1) // 2
    places = jnp.arange(length).astype(jnp.int32)
    offsets = (places[None, :] - places[:, None] + length - 1).astype(jnp.int32)
    return jnp.moveaxis(table[bucket_ids[offsets]], -1, 0)

def self_row(query, key, value, segment, bias):
    length = query.shape[0]
    products = jnp.einsum('ihe,jhe->hij', query, key, precision=HIGHEST)
    scores = low_back(products * HEAD_DIM ** (-0.5) + bias)
    places = jnp.arange(length).astype(jnp.int32)
    allowed = (places[None, :] <= places[:, None]) & (segment[None, :] == segment[:, None])
    weights = low(jax.nn.softmax(jnp.where(allowed[None], scores, MASKED), axis=-1))
    return low_back(jnp.einsum('hij,jhe->ihe', weights, value, precision=HIGHEST))

def cross_row(query, key, value, valid):
    products = jnp.einsum('ihe,jhe->hij', query, key, precision=HIGHEST)
    scores = low_back(products * HEAD_DIM ** (-0.5))
    weights = low(jax.nn.softmax(jnp.where(valid[None, None, :] > 0, scores, MASKED), axis=-1))
    return both_ways(jnp.einsum('hij,jhe->ihe', weights, value, precision=HIGHEST))

def forward(segment_ids, bucket_ids, memory_mask, tokens, memory, self_gain, self_bias, query_weight, key_weight, value_weight, rel_table, head_scale, output_weight, after_gain, after_bias, cross_gain, cross_bias, batch_gain, batch_bias, cross_query, cross_key, cross_value, cross_output, crossout_gain, crossout_bias, ffn_gain, ffn_bias, up_weight, middle_gain, middle_bias, down_weight):
    length, rows, width = tokens.shape
    heads = rel_table.shape[1]
    split = (length, rows, heads, width // heads)
    self_in = low(layer_norm(tokens, self_gain, self_bias))
    queries = both_ways(project(self_in, query_weight)).reshape(split)
    keys = both_ways(project(self_in, key_weight)).reshape(split)
    values = both_ways(project(self_in, value_weight)).reshape(split)
    bias = position_bias(rel_table, bucket_ids)

    def self_block(items):
        return self_row(items[0], items[1], items[2], items[3], bias)
    mixed = lax.map(jax.checkpoint(self_block), (jnp.moveaxis(queries, 1, 0), jnp.moveaxis(keys, 1, 0), jnp.moveaxis(values, 1, 0), segment_ids))
    mixed = jnp.moveaxis(mixed, 0, 1)
    scaled = low(mixed * head_scale[:, None]).reshape(length, rows, width)
    attn = low_back(project(scaled, output_weight))
    first = tokens + layer_norm(attn, after_gain, after_bias)
    cross_in = low(layer_norm(first, cross_gain, cross_bias))
    cross_queries = both_ways(project(cross_in, cross_query)).reshape(split)
    mem_mean = lax.optimization_barrier(jnp.mean(memory, axis=(0, 1)))
    centered = memory - mem_mean
    mem_var = lax.optimization_barrier(jnp.mean(centered * centered, axis=(0, 1)))
    normed = low(centered * lax.rsqrt(mem_var + EPSILON) * batch_gain + batch_bias)
    mem_split = (memory.shape[0], rows, heads, width // heads)
    mem_keys = both_ways(project(normed, cross_key)).reshape(mem_split)
    mem_values = both_ways(project(normed, cross_value)).reshape(mem_split)

    def cross_block(items):
        return cross_row(items[0], items[1], items[2], items[3])
    cross_mixed = lax.map(jax.checkpoint(cross_block), (jnp.moveaxis(cross_queries, 1, 0), jnp.moveaxis(mem_keys, 1, 0), jnp.moveaxis(mem_values, 1, 0), memory_mask))
    cross_mixed = jnp.moveaxis(cross_mixed, 0, 1).reshape(length, rows, width)
    cross_attn = low_back(project(cross_mixed, cross_output))
    second = first + layer_norm(cross_attn, crossout_gain, crossout_bias)
    ffn_in = low(layer_norm(second, ffn_gain, ffn_bias))
    gate = low_back(project(ffn_in, up_weight))
    active = jax.nn.gelu(gate, approximate=False)
    middle = low(layer_norm(active, middle_gain, middle_bias))
    return second + project(middle, down_weight)

def reference(tokens, segment_ids, bucket_ids, memory, memory_mask, cotangent, self_gain, self_bias, query_weight, key_weight, value_weight, rel_table, head_scale, output_weight, after_gain, after_bias, cross_gain, cross_bias, batch_gain, batch_bias, cross_query, cross_key, cross_value, cross_output, crossout_gain, crossout_bias, ffn_gain, ffn_bias, up_weight, middle_gain, middle_bias, down_weight):
    operands = [operand.astype(jnp.float32) for operand in (tokens, memory, self_gain, self_bias, query_weight, key_weight, value_weight, rel_table, head_scale, output_weight, after_gain, after_bias, cross_gain, cross_bias, batch_gain, batch_bias, cross_query, cross_key, cross_value, cross_output, crossout_gain, crossout_bias, ffn_gain, ffn_bias, up_weight, middle_gain, middle_bias, down_weight)]
    result, pullback = jax.vjp(partial(forward, segment_ids, bucket_ids, memory_mask), *operands)
    gradients = pullback(cotangent.astype(jnp.float32))
    return (result.astype(jnp.bfloat16), gradients[0], gradients[1], gradients[2], gradients[3], gradients[4], gradients[5], gradients[6], gradients[7], gradients[8], gradients[9], gradients[10], gradients[11], gradients[12], gradients[13], gradients[14], gradients[15], gradients[16], gradients[17], gradients[18], gradients[19], gradients[20], gradients[21], gradients[22], gradients[23], gradients[24], gradients[25], gradients[26], gradients[27])
```

```python
import jax
import jax.numpy as jnp
from jax import lax
from jax.experimental import pallas as pl
from jax.experimental.pallas import tpu as pltpu
from jax.sharding import PartitionSpec as P

HEAD_DIM = 64
EPSILON = 1e-05
MASKED = -1e30
LANES = 128
BF = jnp.bfloat16
F32 = jnp.float32
SCALE = HEAD_DIM ** (-0.5)
VMEM_LIMIT = 50 * 1024 * 1024


def contract(left, right, left_dim, right_dim, precision=None):
    return lax.dot_general(
        left,
        right,
        (((left_dim,), (right_dim,)), ((), ())),
        precision=precision,
        preferred_element_type=F32,
    )


def kernel_params():
    return pltpu.CompilerParams(vmem_limit_bytes=VMEM_LIMIT)


def choice_of(ids, buckets):
    places = lax.broadcasted_iota(jnp.int32, (buckets, ids.shape[1]), 0)
    return jnp.where(places == ids, 1.0, 0.0).astype(F32)


def bias_kernel(ids_ref, table_ref, ext_ref):
    heads, width = 2 * ext_ref.shape[0], ext_ref.shape[2]
    choose = choice_of(ids_ref[...], table_ref.shape[1])
    by_offset = contract(table_ref[...], choose, 1, 0, lax.Precision.HIGHEST)
    sub = lax.broadcasted_iota(jnp.int32, (8, width), 0)
    for head in range(heads):
        rolled = jnp.broadcast_to(by_offset[head : head + 1, :], (8, width))
        for bit in (1, 2, 4):
            rolled = jnp.where((sub & bit) > 0, pltpu.roll(rolled, bit, 1), rolled)
        for group in range(LANES // 8):
            start = (head % 2) * LANES + group * 8
            moved = rolled if group == 0 else pltpu.roll(rolled, group * 8, 1)
            ext_ref[head // 2, start : start + 8, :] = moved


def halves(block, low):
    zero = jnp.zeros_like(block)
    return jnp.concatenate([jnp.where(low, block, zero), jnp.where(low, zero, block)], 0)


def merge(block, low):
    rows = block.shape[0] // 2
    return jnp.where(low, block[:rows], block[rows:])


def pair_columns(pair, base=0):
    return pl.ds(pl.multiple_of(base + pair * LANES, LANES), LANES)


def penalty_of(rows, first_row, count, seg_col, seg_row):
    i = lax.broadcasted_iota(jnp.int32, (rows, count), 0) + first_row
    j = lax.broadcasted_iota(jnp.int32, (rows, count), 1)
    one = jnp.where((j <= i) & (seg_col == seg_row), 0.0, MASKED).astype(F32)
    return jnp.concatenate([one, one], 0)


def ext_block(ext_ref, pair, rows, shift, count):
    if rows == LANES:
        return ext_ref[pair, :, shift : shift + count]
    return jnp.concatenate(
        [
            ext_ref[pair, 0:rows, shift : shift + count],
            ext_ref[pair, LANES : LANES + rows, shift : shift + count],
        ],
        0,
    )


def self_forward_kernel(qkv_ref, ext_ref, seg_col_ref, seg_row_ref, scale_ref, out_ref, stats_ref):
    length, width = out_ref.shape
    pairs = width // LANES
    blocks = -(-length // LANES)
    lane = lax.broadcasted_iota(jnp.int32, (1, LANES), 1)
    low = lane < HEAD_DIM
    stats_ref[...] = jnp.zeros_like(stats_ref)
    for block in range(blocks):
        start = block * LANES
        rows = min(LANES, length - start)
        count = start + rows
        shift = (blocks - 1 - block) * LANES
        penalty = penalty_of(
            rows, start, count, seg_col_ref[start : start + rows, :], seg_row_ref[:, 0:count]
        )

        def one_pair(pair, carry):
            columns = pair_columns(pair)
            query = halves(qkv_ref[start : start + rows, columns].astype(F32) * SCALE, low).astype(BF)
            key = qkv_ref[0:count, pair_columns(pair, width)]
            value = qkv_ref[0:count, pair_columns(pair, 2 * width)]
            scores = contract(query, key, 1, 1) + (
                ext_block(ext_ref, pair, rows, shift, count) + penalty
            )
            peak = jnp.max(scores, -1, keepdims=True)
            shifted = jnp.exp(scores - peak)
            total = jnp.sum(shifted, -1, keepdims=True)
            weights = (shifted * (1.0 / total)).astype(BF)
            mixed = merge(contract(weights, value, 1, 0), low)
            out_ref[start : start + rows, columns] = (mixed * scale_ref[:, columns]).astype(BF)
            level = peak + jnp.log(total)
            stats_ref[start : start + rows, :] += jnp.where(
                lane == 2 * pair, level[:rows], 0.0
            ) + jnp.where(lane == 2 * pair + 1, level[rows:], 0.0)
            return carry

        lax.fori_loop(0, pairs, one_pair, 0)


def level_of(stats, lane, pair):
    return jnp.concatenate(
        [
            jnp.sum(jnp.where(lane == 2 * pair + side, stats, 0.0), -1, keepdims=True)
            for side in (0, 1)
        ],
        0,
    )


def self_backward_kernel(
    qkv_ref,
    upstream_ref,
    ext_ref,
    seg_col_ref,
    seg_row_ref,
    stats_ref,
    ids_ref,
    grad_ref,
    table_ref,
    head_ref,
    key_sum,
    value_sum,
    offset_sum,
):
    length, width = upstream_ref.shape
    pairs = width // LANES
    blocks = -(-length // LANES)
    lane = lax.broadcasted_iota(jnp.int32, (1, LANES), 1)
    low = lane < HEAD_DIM
    key_sum[...] = jnp.zeros_like(key_sum)
    value_sum[...] = jnp.zeros_like(value_sum)
    offset_sum[...] = jnp.zeros_like(offset_sum)
    head_ref[...] = jnp.zeros_like(head_ref)
    for block in range(blocks):
        start = block * LANES
        rows = min(LANES, length - start)
        count = start + rows
        shift = (blocks - 1 - block) * LANES
        penalty = penalty_of(
            rows, start, count, seg_col_ref[start : start + rows, :], seg_row_ref[:, 0:count]
        )

        def one_pair(pair, carry):
            columns = pair_columns(pair)
            query = halves(qkv_ref[start : start + rows, columns].astype(F32) * SCALE, low).astype(BF)
            key = qkv_ref[0:count, pair_columns(pair, width)]
            value = qkv_ref[0:count, pair_columns(pair, 2 * width)]
            upstream = halves(upstream_ref[start : start + rows, columns].astype(F32), low).astype(BF)
            level = level_of(stats_ref[start : start + rows, :], lane, pair)
            scores = contract(query, key, 1, 1) + (
                ext_block(ext_ref, pair, rows, shift, count) + penalty
            )
            probs = jnp.exp(scores - level)
            grad_probs = contract(upstream, value, 1, 1)
            inner = jnp.sum(probs * grad_probs, -1, keepdims=True)
            grad_scores = (probs * (grad_probs - inner)).astype(BF)
            weights = probs.astype(BF)
            grad_query = merge(contract(grad_scores, key, 1, 0), low) * SCALE
            grad_ref[start : start + rows, columns] = grad_query.astype(BF)
            key_sum[0:count, columns] += contract(grad_scores, query, 0, 0)
            value_sum[0:count, columns] += contract(weights, upstream, 0, 0)
            wide = grad_scores.astype(F32)
            if rows == LANES:
                offset_sum[pair, :, shift : shift + count] += wide
            else:
                offset_sum[pair, 0:rows, shift : shift + count] += wide[:rows]
                offset_sum[pair, LANES : LANES + rows, shift : shift + count] += wide[rows:]
            for side in (0, 1):
                part = jnp.sum(inner[side * rows : (side + 1) * rows], 0, keepdims=True)
                head_ref[pl.ds(2 * pair + side, 1), :] += jnp.broadcast_to(part, (1, LANES))
            return carry

        lax.fori_loop(0, pairs, one_pair, 0)
    grad_ref[:, width : 2 * width] = key_sum[...].astype(BF)
    grad_ref[:, 2 * width : 3 * width] = value_sum[...].astype(BF)
    span = offset_sum.shape[2]
    sub = lax.broadcasted_iota(jnp.int32, (8, span), 0)
    head_places = lax.broadcasted_iota(jnp.int32, (table_ref.shape[0], span), 0)
    by_offset = jnp.zeros((table_ref.shape[0], span), F32)
    for head in range(2 * pairs):
        total = None
        for group in range(LANES // 8):
            first = (head % 2) * LANES + group * 8
            piece = offset_sum[head // 2, first : first + 8, :]
            moved = piece if group == 0 else pltpu.roll(piece, span - group * 8, 1)
            total = moved if total is None else total + moved
        for bit in (1, 2, 4):
            total = jnp.where((sub & bit) > 0, pltpu.roll(total, span - bit, 1), total)
        line = jnp.sum(total, 0, keepdims=True)
        by_offset = by_offset + jnp.where(head_places == head, line, 0.0)
    choose = choice_of(ids_ref[...], table_ref.shape[1])
    table_ref[...] = contract(by_offset, choose, 1, 1, lax.Precision.HIGHEST)


def cross_forward_kernel(query_ref, key_ref, value_ref, valid_ref, out_ref, stats_ref):
    pairs = query_ref.shape[1] // LANES
    lane = lax.broadcasted_iota(jnp.int32, (1, LANES), 1)
    low = lane < HEAD_DIM
    penalty = jnp.where(valid_ref[...] > 0, 0.0, MASKED).astype(F32)
    stats_ref[...] = jnp.zeros_like(stats_ref)

    def one_pair(pair, carry):
        columns = pair_columns(pair)
        query = query_ref[:, columns].astype(F32) * SCALE
        key = key_ref[:, columns]
        value = value_ref[:, columns]
        mixed = None
        for side in (0, 1):
            mine = low if side == 0 else jnp.logical_not(low)
            scores = contract(jnp.where(mine, query, 0.0).astype(BF), key, 1, 1) + penalty
            peak = jnp.max(scores, -1, keepdims=True)
            shifted = jnp.exp(scores - peak)
            total = jnp.sum(shifted, -1, keepdims=True)
            weights = (shifted * (1.0 / total)).astype(BF)
            part = contract(weights, value, 1, 0)
            mixed = part if mixed is None else jnp.where(low, mixed, part)
            stats_ref[...] += jnp.where(lane == 2 * pair + side, peak + jnp.log(total), 0.0)
        out_ref[:, columns] = mixed.astype(BF)
        return carry

    lax.fori_loop(0, pairs, one_pair, 0)


def cross_backward_kernel(
    query_ref,
    key_ref,
    value_ref,
    valid_ref,
    stats_ref,
    upstream_ref,
    grad_query_ref,
    grad_key_ref,
    grad_value_ref,
):
    pairs = query_ref.shape[1] // LANES
    lane = lax.broadcasted_iota(jnp.int32, (1, LANES), 1)
    low = lane < HEAD_DIM
    penalty = jnp.where(valid_ref[...] > 0, 0.0, MASKED).astype(F32)

    def one_pair(pair, carry):
        columns = pair_columns(pair)
        query = query_ref[:, columns].astype(F32) * SCALE
        upstream = upstream_ref[:, columns].astype(F32)
        key = key_ref[:, columns]
        value = value_ref[:, columns]
        grad_query = grad_key = grad_value = None
        for side in (0, 1):
            mine = low if side == 0 else jnp.logical_not(low)
            my_query = jnp.where(mine, query, 0.0).astype(BF)
            my_upstream = jnp.where(mine, upstream, 0.0).astype(BF)
            level = jnp.sum(
                jnp.where(lane == 2 * pair + side, stats_ref[...], 0.0), -1, keepdims=True
            )
            probs = jnp.exp(contract(my_query, key, 1, 1) + penalty - level)
            grad_probs = contract(my_upstream, value, 1, 1)
            inner = jnp.sum(probs * grad_probs, -1, keepdims=True)
            grad_scores = (probs * (grad_probs - inner)).astype(BF)
            part_query = contract(grad_scores, key, 1, 0)
            part_key = contract(grad_scores, my_query, 0, 0)
            part_value = contract(probs.astype(BF), my_upstream, 0, 0)
            if side == 0:
                grad_query, grad_key, grad_value = part_query, part_key, part_value
            else:
                grad_query = jnp.where(low, grad_query, part_query)
                grad_key, grad_value = grad_key + part_key, grad_value + part_value
        grad_query_ref[:, columns] = (grad_query * SCALE).astype(BF)
        grad_key_ref[:, columns] = grad_key
        grad_value_ref[:, columns] = grad_value
        return carry

    lax.fori_loop(0, pairs, one_pair, 0)


def flip_over(axis, bit):
    def send(block):
        size = lax.axis_size(axis)
        return lax.ppermute(block, axis, [(i, i ^ bit) for i in range(size)])

    return send


def mate(block):
    return flip_over("mp", 1)(block)


def peer(block):
    return flip_over("mp", 2)(block)


def in_order(index, own, other, axis=0):
    first = jnp.where(index == 0, own, other)
    second = jnp.where(index == 0, other, own)
    return jnp.concatenate([first, second], axis)


def cut(block, index, size, axis=0):
    return lax.dynamic_slice_in_dim(block, index * size, size, axis)


def dot(left, right):
    return jnp.dot(left, right, preferred_element_type=F32)


def dot_right(left, right):
    return contract(left, right, 1, 1)


def dot_left(left, right):
    return contract(left, right, 0, 0)


def norm_parts(values):
    center = values - jnp.mean(values, -1, keepdims=True)
    factor = lax.rsqrt(jnp.mean(center * center, -1, keepdims=True) + EPSILON)
    return center * factor, factor


def norm_back(values, gain, upstream):
    hat, factor = norm_parts(values)
    leaned = upstream * gain
    grad = factor * (
        leaned
        - jnp.mean(leaned, -1, keepdims=True)
        - hat * jnp.mean(leaned * hat, -1, keepdims=True)
    )
    return grad, jnp.sum(upstream * hat, 0), jnp.sum(upstream, 0)


def batch_bits():
    size = lax.axis_size("batch")
    bits = []
    while (1 << len(bits)) < size:
        bits.append(1 << len(bits))
    return bits


def sum_rows(block, axis_bits):
    for axis, bit in axis_bits:
        index = (lax.axis_index(axis) // bit) % 2
        size = block.shape[0] // 2
        keep = cut(block, index, size)
        send = cut(block, 1 - index, size).astype(BF)
        block = keep + flip_over(axis, bit)(send).astype(F32)
    block = block.astype(BF)
    for axis, bit in reversed(axis_bits):
        index = (lax.axis_index(axis) // bit) % 2
        block = in_order(index, block, flip_over(axis, bit)(block))
    return block.astype(F32)


def sum_small(block, axis_bits):
    for axis, bit in axis_bits:
        block = block + flip_over(axis, bit)(block)
    return block


def pack_small(parts):
    flat = jnp.concatenate([part.reshape(-1) for part in parts])
    size = -(-flat.shape[0] // (8 * LANES)) * 8 * LANES
    return jnp.pad(flat, (0, size - flat.shape[0])).reshape(-1, LANES)


def unpack_small(packed, shapes):
    flat = packed.reshape(-1)
    parts, start = [], 0
    for shape in shapes:
        size = 1
        for extent in shape:
            size *= extent
        parts.append(flat[start : start + size].reshape(shape))
        start += size
    return parts


def shape_of(shape, dtype):
    return jax.ShapeDtypeStruct(shape, dtype)


def on_device(
    tokens,
    segment_ids,
    bucket_ids,
    memory,
    memory_mask,
    cotangent,
    self_gain,
    self_bias,
    query_weight,
    key_weight,
    value_weight,
    rel_table,
    head_scale,
    output_weight,
    after_gain,
    after_bias,
    cross_gain,
    cross_bias,
    batch_gain,
    batch_bias,
    cross_query,
    cross_key,
    cross_value,
    cross_output,
    crossout_gain,
    crossout_bias,
    ffn_gain,
    ffn_bias,
    up_weight,
    middle_gain,
    middle_bias,
    down_weight,
):
    place = lax.axis_index("mp")
    core, side = place % 2, place // 2
    batch = lax.axis_size("batch")
    bits = batch_bits()
    over_batch = [("batch", bit) for bit in bits]
    quarter, _, width = tokens.shape
    length = 4 * quarter
    half = 2 * quarter
    heads = 2 * rel_table.shape[1]
    lanes = heads * HEAD_DIM
    own_lanes = lanes // 2
    hidden = 2 * up_weight.shape[1]
    all_hidden = 2 * hidden

    def own_row(array):
        keep = lax.dynamic_index_in_dim(array, core, 1, keepdims=False)
        give = lax.dynamic_index_in_dim(array, 1 - core, 1, keepdims=False)
        near = mate(give)
        far = peer(keep)
        cross = flip_over("mp", 3)(give)
        return in_order(core, keep, near), in_order(core, far, cross)

    own_tokens, far_tokens = own_row(tokens)
    row_tokens = in_order(side, own_tokens, far_tokens).astype(F32)
    stream = own_tokens.astype(F32)

    rows_here = memory.reshape(memory.shape[0], batch, 2, width)
    my_rows = lax.dynamic_index_in_dim(rows_here, core, 2, keepdims=False)
    row_memory = lax.all_to_all(my_rows, "batch", split_axis=1, concat_axis=0, tiled=True)
    row_memory = row_memory.reshape(-1, width)
    mem_float = memory.astype(F32)
    mem_totals = sum_small(
        pack_small([jnp.sum(mem_float, (0, 1)), jnp.sum(mem_float * mem_float, (0, 1))]), over_batch
    )
    mem_sum, mem_square = unpack_small(mem_totals, [(width,), (width,)])

    blocks = -(-length // LANES)
    span = blocks * LANES
    split = length - 1 - (blocks - 1) * LANES
    ids = jnp.concatenate(
        [
            bucket_ids[split:length],
            jnp.full((span - length,), -1, bucket_ids.dtype),
            bucket_ids[:split],
        ]
    )[None, :]
    table = jnp.concatenate([rel_table, mate(rel_table)], 1).T
    table = jnp.pad(table, ((0, 8 - heads % 8), (0, 0)))
    ext = pl.pallas_call(
        bias_kernel,
        out_shape=shape_of((heads // 2, 2 * LANES, span), F32),
        compiler_params=kernel_params(),
        name="bias",
    )(ids, table)

    near_weights = mate(jnp.stack([query_weight, key_weight, value_weight]))
    qkv_weight = jnp.concatenate(
        [
            query_weight,
            near_weights[0],
            key_weight,
            near_weights[1],
            value_weight,
            near_weights[2],
        ],
        1,
    )
    token_hat, _ = norm_parts(row_tokens)
    self_in = (token_hat * self_gain + self_bias).astype(BF)
    qkv = dot(self_in, qkv_weight).astype(BF)
    segment = lax.dynamic_index_in_dim(segment_ids, core, 0, keepdims=False)
    seg_col, seg_row = segment[:, None], segment[None, :]
    both_scale = jnp.concatenate([head_scale, mate(head_scale)])
    scale_lanes = jnp.repeat(both_scale, HEAD_DIM)[None, :]
    scaled, stats = pl.pallas_call(
        self_forward_kernel,
        out_shape=(shape_of((length, lanes), BF), shape_of((length, LANES), F32)),
        compiler_params=kernel_params(),
        name="self_forward",
    )(qkv, ext, seg_col, seg_row, scale_lanes)
    own_scaled = jnp.concatenate([cut(scaled, side, half), peer(cut(scaled, 1 - side, half))], 1)

    def whole(weight, axis):
        near = mate(weight)
        far = peer(weight)
        return jnp.concatenate([weight, near, far, mate(far)], axis)

    output_all = whole(output_weight, 0)
    attn = dot(own_scaled, output_all)
    attn_hat, _ = norm_parts(attn)
    first = stream + attn_hat * after_gain + after_bias
    first_hat, _ = norm_parts(first)
    cross_in = (first_hat * cross_gain + cross_bias).astype(BF)
    cross_query_all = whole(cross_query, 1)
    cross_queries = dot(cross_in, cross_query_all).astype(BF)

    count = memory.shape[0] * batch * memory.shape[1]
    mem_mean = mem_sum / count
    mem_scale = lax.rsqrt(mem_square / count - mem_mean * mem_mean + EPSILON)
    normed = (((row_memory.astype(F32) - mem_mean) * mem_scale) * batch_gain + batch_bias).astype(BF)
    kv_weight = jnp.concatenate([cross_key, mate(cross_key), cross_value, mate(cross_value)], 1)
    own_kv = dot(normed, kv_weight).astype(BF)
    far_kv = peer(own_kv)
    mem_keys = jnp.concatenate([own_kv[:, :own_lanes * 2], far_kv[:, :own_lanes * 2]], 1)
    mem_values = jnp.concatenate([own_kv[:, own_lanes * 2 :], far_kv[:, own_lanes * 2 :]], 1)
    valid = lax.dynamic_index_in_dim(memory_mask, core, 0, keepdims=True)
    cross_mixed, cross_stats = pl.pallas_call(
        cross_forward_kernel,
        out_shape=(shape_of((half, width), BF), shape_of((half, LANES), F32)),
        compiler_params=kernel_params(),
        name="cross_forward",
    )(cross_queries, mem_keys, mem_values, valid)
    cross_output_all = whole(cross_output, 0)
    cross_attn = dot(cross_mixed, cross_output_all)
    cross_hat, _ = norm_parts(cross_attn)
    second = first + cross_hat * crossout_gain + crossout_bias
    second_hat, _ = norm_parts(second)
    ffn_own = (second_hat * ffn_gain + ffn_bias).astype(BF)

    ffn_in = jnp.concatenate([ffn_own, peer(ffn_own)], 0)
    own_cotangent, far_cotangent = own_row(cotangent)
    row_cotangent = jnp.concatenate([own_cotangent, far_cotangent], 0)
    up_pair = jnp.concatenate([up_weight, mate(up_weight)], 1)
    down_pair = jnp.concatenate([down_weight, mate(down_weight)], 0)
    near_middle = mate(jnp.stack([middle_gain, middle_bias]))
    gain_pair = jnp.concatenate([middle_gain, near_middle[0]])
    bias_pair = jnp.concatenate([middle_bias, near_middle[1]])
    gate = dot(ffn_in, up_pair)
    chance = 0.5 * (1.0 + lax.erf(gate * (0.5**0.5)))
    active = gate * chance
    grad_middle = dot_right(row_cotangent, down_pair)
    leaned = grad_middle * gain_pair
    sums = jnp.stack(
        [
            jnp.sum(active, -1),
            jnp.sum(active * active, -1),
            jnp.sum(leaned, -1),
            jnp.sum(leaned * active, -1),
        ]
    )
    far_sums = peer(sums)
    sums = sums + jnp.concatenate([far_sums[:, half:], far_sums[:, :half]], 1)
    sums = sums / all_hidden
    act_mean = sums[0][:, None]
    act_scale = lax.rsqrt(sums[1][:, None] - act_mean * act_mean + EPSILON)
    act_hat = (active - act_mean) * act_scale
    middle = (act_hat * gain_pair + bias_pair).astype(BF)
    leaned_mean = sums[2][:, None]
    leaned_hat = act_scale * (sums[3][:, None] - act_mean * leaned_mean)
    grad_active = act_scale * (leaned - leaned_mean - act_hat * leaned_hat)
    density = jnp.exp(-0.5 * gate * gate) * ((2.0 * jnp.pi) ** -0.5)
    grad_gate = (grad_active * (chance + gate * density)).astype(BF)
    grad_mid_gain = jnp.sum(grad_middle * act_hat, 0)
    grad_mid_bias = jnp.sum(grad_middle, 0)
    back_far = dot_right(grad_gate[half:], up_pair).astype(BF)
    back_came = peer(back_far)
    grad_ffn_in = dot_right(grad_gate[:half], up_pair) + back_came.astype(F32)

    back_second, grad_ffn_gain, grad_ffn_bias = norm_back(second, ffn_gain, grad_ffn_in)
    grad_second = own_cotangent.astype(F32) + back_second
    back_cross, grad_co_gain, grad_co_bias = norm_back(cross_attn, crossout_gain, grad_second)
    grad_cross_attn = back_cross.astype(BF)
    grad_cross_mixed = dot_right(grad_cross_attn, cross_output_all).astype(BF)
    grad_cq, grad_mk, grad_mv = pl.pallas_call(
        cross_backward_kernel,
        out_shape=(
            shape_of((half, width), BF),
            shape_of((row_memory.shape[0], width), F32),
            shape_of((row_memory.shape[0], width), F32),
        ),
        compiler_params=kernel_params(),
        name="cross_backward",
    )(cross_queries, mem_keys, mem_values, valid, cross_stats, grad_cross_mixed)
    grad_cross_in = dot_right(grad_cq, cross_query_all)
    back_first, grad_cross_gain, grad_cross_bias = norm_back(first, cross_gain, grad_cross_in)
    grad_first = grad_second + back_first
    back_attn, grad_after_gain, grad_after_bias = norm_back(attn, after_gain, grad_first)
    grad_attn = back_attn.astype(BF)
    all_scale = jnp.concatenate([both_scale, peer(both_scale)])
    grad_mixed_own = (
        dot_right(grad_attn, output_all) * jnp.repeat(all_scale, HEAD_DIM)[None, :]
    ).astype(BF)
    grad_mixed = in_order(side, grad_mixed_own[:, :lanes], peer(grad_mixed_own[:, lanes:]))
    grad_qkv, grad_table, grad_heads = pl.pallas_call(
        self_backward_kernel,
        out_shape=(
            shape_of((length, 3 * lanes), BF),
            shape_of(table.shape, F32),
            shape_of((8, LANES), F32),
        ),
        scratch_shapes=[
            pltpu.VMEM((length, lanes), F32),
            pltpu.VMEM((length, lanes), F32),
            pltpu.VMEM(ext.shape, F32),
        ],
        compiler_params=kernel_params(),
        name="self_backward",
    )(qkv, grad_mixed, ext, seg_col, seg_row, stats, ids)
    far_in = dot_right(cut(grad_qkv, 1 - side, half), qkv_weight).astype(BF)
    grad_self_in = dot_right(cut(grad_qkv, side, half), qkv_weight) + peer(far_in).astype(F32)
    back_tokens, grad_self_gain, grad_self_bias = norm_back(stream, self_gain, grad_self_in)
    own_grad_tokens = grad_first + back_tokens

    def by_quarter(own):
        keep = cut(own, core, quarter)
        came = mate(cut(own, 1 - core, quarter))
        return jnp.stack([jnp.where(core == 0, keep, came), jnp.where(core == 0, came, keep)], 1)

    grad_tokens = by_quarter(own_grad_tokens)
    out_far = dot(middle[half:], down_pair).astype(BF)
    out_own = second + dot(middle[:half], down_pair) + peer(out_far).astype(F32)
    output = by_quarter(out_own.astype(BF))

    def own_columns(grads):
        cols = width // 2
        return (grads[:, :cols] + peer(grads[:, cols:].astype(BF)).astype(F32)).astype(BF)

    grad_kv = jnp.concatenate([own_columns(grad_mk), own_columns(grad_mv)], 1)
    part_normed = dot_right(grad_kv, kv_weight)
    half_normed = cut(part_normed, side, width // 2, 1) + peer(
        cut(part_normed, 1 - side, width // 2, 1).astype(BF)
    ).astype(F32)
    channels = width // 4
    keep_normed = cut(half_normed, core, channels, 1)
    came_normed = mate(cut(half_normed, 1 - core, channels, 1))
    both_normed = jnp.stack(
        [
            jnp.where(core == 0, keep_normed, came_normed),
            jnp.where(core == 0, came_normed, keep_normed),
        ],
        1,
    )
    grad_normed = lax.all_to_all(both_normed, "batch", split_axis=0, concat_axis=1, tiled=True)
    mean_slice = cut(mem_mean, place, channels)
    gain_slice = cut(batch_gain, place, channels)
    scale_slice = cut(mem_scale, place, channels)
    hat_slice = (cut(memory, place, channels, 2).astype(F32) - mean_slice) * scale_slice
    shift_term = jnp.sum(grad_normed, (0, 1))
    scale_term = jnp.sum(grad_normed * hat_slice, (0, 1))

    def own_near(grads, axis):
        size = grads.shape[axis] // 2
        keep = lax.slice_in_dim(grads, 0, size, axis=axis)
        give = lax.slice_in_dim(grads, size, 2 * size, axis=axis)
        return keep + mate(give.astype(BF)).astype(F32)

    def own_of_four(grads, axis):
        size = grads.shape[axis] // 4
        part = [lax.slice_in_dim(grads, i * size, (i + 1) * size, axis=axis) for i in range(4)]
        came = mate(jnp.concatenate([part[1], part[3]], axis).astype(BF)).astype(F32)
        near = part[0] + lax.slice_in_dim(came, 0, size, axis=axis)
        far = part[2] + lax.slice_in_dim(came, size, 2 * size, axis=axis)
        return near + peer(far.astype(BF)).astype(F32)

    grad_up = own_near(dot_left(ffn_in, grad_gate), 1)
    grad_down = own_near(dot_left(middle, row_cotangent), 0)
    sum_ffn = sum_rows(jnp.concatenate([grad_up, grad_down], 0), over_batch)
    sum_up, sum_down = sum_ffn[: grad_up.shape[0]], sum_ffn[grad_up.shape[0] :]
    sum_coutput = sum_rows(own_of_four(dot_left(cross_mixed, grad_cross_attn), 0), over_batch)
    grad_cquery = own_of_four(dot_left(cross_in, grad_cq), 1)
    grad_ckv = dot_left(normed, grad_kv)
    cols = width // 2
    grad_ckey = own_near(grad_ckv[:, :cols], 1)
    grad_cvalue = own_near(grad_ckv[:, cols:], 1)
    sum_cross = sum_rows(jnp.concatenate([grad_cquery, grad_ckey, grad_cvalue], 1), over_batch)
    sum_output = sum_rows(own_of_four(dot_left(own_scaled, grad_attn), 0), over_batch)
    grad_weights = dot_left(self_in, grad_qkv)
    sum_qkv = sum_rows(
        jnp.concatenate(
            [own_near(grad_weights[:, i * lanes : (i + 1) * lanes], 1) for i in range(3)], 1
        ),
        over_batch,
    )
    step = width // 4

    own_heads = heads // 2
    mine_small = pack_small(
        [
            grad_table[:own_heads],
            grad_heads[:own_heads, 0] / both_scale[:own_heads],
            grad_mid_gain[: hidden // 2],
            grad_mid_bias[: hidden // 2],
        ]
    )
    near_small = pack_small(
        [
            grad_table[own_heads:heads],
            grad_heads[own_heads:heads, 0] / both_scale[own_heads:],
            grad_mid_gain[hidden // 2 :],
            grad_mid_bias[hidden // 2 :],
        ]
    )
    small = mine_small + mate(near_small)
    mem_small = pack_small([shift_term, scale_term])
    shared = sum_small(
        pack_small(
            [
                grad_self_gain,
                grad_self_bias,
                grad_after_gain,
                grad_after_bias,
                grad_cross_gain,
                grad_cross_bias,
                grad_co_gain,
                grad_co_bias,
                grad_ffn_gain,
                grad_ffn_bias,
            ]
        ),
        [("mp", 1), ("mp", 2)],
    )
    joined = sum_small(jnp.concatenate([small, mem_small, shared], 0), over_batch)
    a, b = small.shape[0], small.shape[0] + mem_small.shape[0]
    sum_table, sum_scale, sum_mid_gain, sum_mid_bias = unpack_small(
        joined[:a],
        [(own_heads, table.shape[1]), (own_heads,), (hidden // 2,), (hidden // 2,)],
    )
    shift_total, scale_total = unpack_small(joined[a:b], [(channels,), (channels,)])
    norm_totals = unpack_small(joined[b:], [(width,)] * 10)
    grad_memory = (
        gain_slice
        * scale_slice
        * (grad_normed - shift_total / count - hat_slice * scale_total / count)
    )
    return (
        output,
        grad_tokens,
        grad_memory,
        norm_totals[0],
        norm_totals[1],
        sum_qkv[:, :step],
        sum_qkv[:, step : 2 * step],
        sum_qkv[:, 2 * step :],
        sum_table.T,
        sum_scale,
        sum_output,
        norm_totals[2],
        norm_totals[3],
        norm_totals[4],
        norm_totals[5],
        scale_total,
        shift_total,
        sum_cross[:, :step],
        sum_cross[:, step : 2 * step],
        sum_cross[:, 2 * step :],
        sum_coutput,
        norm_totals[6],
        norm_totals[7],
        norm_totals[8],
        norm_totals[9],
        sum_up,
        sum_mid_gain,
        sum_mid_bias,
        sum_down,
    )


def solution(mesh):
    in_specs = (
        P("mp", "batch", None),
        P("batch", None),
        P(),
        P("batch", None, None),
        P("batch", None),
        P("mp", "batch", None),
        P(),
        P(),
        P(None, "mp"),
        P(None, "mp"),
        P(None, "mp"),
        P(None, "mp"),
        P("mp"),
        P("mp", None),
        P(),
        P(),
        P(),
        P(),
        P(),
        P(),
        P(None, "mp"),
        P(None, "mp"),
        P(None, "mp"),
        P("mp", None),
        P(),
        P(),
        P(),
        P(),
        P(None, "mp"),
        P("mp"),
        P("mp"),
        P("mp", None),
    )
    out_specs = (
        P("mp", "batch", None),
        P("mp", "batch", None),
        P("batch", None, "mp"),
        P(),
        P(),
        P(None, "mp"),
        P(None, "mp"),
        P(None, "mp"),
        P(None, "mp"),
        P("mp"),
        P("mp", None),
        P(),
        P(),
        P(),
        P(),
        P("mp"),
        P("mp"),
        P(None, "mp"),
        P(None, "mp"),
        P(None, "mp"),
        P("mp", None),
        P(),
        P(),
        P(),
        P(),
        P(None, "mp"),
        P("mp"),
        P("mp"),
        P("mp", None),
    )
    return jax.shard_map(
        on_device, mesh=mesh, in_specs=in_specs, out_specs=out_specs, check_vma=False
    )
```

```python
import functools

import jax
import jax.numpy as jnp
from jax import lax
from jax.experimental import pallas as pl
from jax.experimental.pallas import tpu as pltpu
from jax.sharding import PartitionSpec as P

HEAD_DIM = 64
EPSILON = 1e-05
MASKED = -1e30
LANES = 128
BF = jnp.bfloat16
F32 = jnp.float32
SCALE = HEAD_DIM ** (-0.5)
VMEM_LIMIT = 18 * 1024 * 1024
LATE_LIMIT = 58 * 1024 * 1024


def contract(left, right, left_dim, right_dim, precision=None):
    return lax.dot_general(
        left,
        right,
        (((left_dim,), (right_dim,)), ((), ())),
        precision=precision,
        preferred_element_type=F32,
    )


def kernel_params(late=()):
    return pltpu.CompilerParams(vmem_limit_bytes=LATE_LIMIT if late else VMEM_LIMIT)


class Late:
    def __init__(self, source, slot, sem):
        self.slot, self.copy = slot, pltpu.make_async_copy(source, slot, sem)
        self.shape, self.dtype = slot.shape, slot.dtype
        self.copy.start()

    def ready(self):
        if self.copy is not None:
            self.copy.wait()
            self.copy = None

    def __getitem__(self, index):
        self.ready()
        return self.slot[index]


def ready(*refs):
    for ref in refs:
        if isinstance(ref, Late):
            ref.ready()


def with_late(kernel, inputs, late):
    def wrapped(*refs):
        body = list(refs[: -1 - len(late)])
        slots, sems = refs[-1 - len(late) : -1], refs[-1]
        for place, (index, slot) in enumerate(zip(late, slots)):
            body[index] = Late(refs[index], slot, sems.at[place])
        kernel(*body)
        ready(*body[:inputs])

    return wrapped


def choice_of(ids, buckets):
    places = lax.broadcasted_iota(jnp.int32, (buckets, ids.shape[1]), 0)
    return jnp.where(places == ids, 1.0, 0.0).astype(F32)


def bias_kernel(ids_ref, table_ref, ext_ref):
    heads, width = 2 * ext_ref.shape[0], ext_ref.shape[2]
    choose = choice_of(ids_ref[...], table_ref.shape[1])
    by_offset = contract(table_ref[...], choose, 1, 0, lax.Precision.HIGHEST)
    sub = lax.broadcasted_iota(jnp.int32, (8, width), 0)
    for head in range(heads):
        rolled = jnp.broadcast_to(by_offset[head : head + 1, :], (8, width))
        for bit in (1, 2, 4):
            rolled = jnp.where((sub & bit) > 0, pltpu.roll(rolled, bit, 1), rolled)
        for group in range(LANES // 8):
            start = (head % 2) * LANES + group * 8
            moved = rolled if group == 0 else pltpu.roll(rolled, group * 8, 1)
            ext_ref[head // 2, start : start + 8, :] = moved


def halves(block, low):
    zero = jnp.zeros_like(block)
    return jnp.concatenate([jnp.where(low, block, zero), jnp.where(low, zero, block)], 0)


def merge(block, low):
    rows = block.shape[0] // 2
    return jnp.where(low, block[:rows], block[rows:])


def pair_columns(pair, base=0):
    return pl.ds(pl.multiple_of(base + pair * LANES, LANES), LANES)


def penalty_of(rows, first_row, count, seg_col, seg_row):
    i = lax.broadcasted_iota(jnp.int32, (rows, count), 0) + first_row
    j = lax.broadcasted_iota(jnp.int32, (rows, count), 1)
    one = jnp.where((j <= i) & (seg_col == seg_row), 0.0, MASKED).astype(F32)
    return jnp.concatenate([one, one], 0)


def ext_block(ext_ref, pair, rows, shift, count):
    if rows == LANES:
        return ext_ref[pair, :, shift : shift + count]
    return jnp.concatenate(
        [
            ext_ref[pair, 0:rows, shift : shift + count],
            ext_ref[pair, LANES : LANES + rows, shift : shift + count],
        ],
        0,
    )


def self_forward_kernel(qkv_ref, ext_ref, seg_col_ref, seg_row_ref, scale_ref, out_ref, stats_ref):
    length, width = out_ref.shape
    pairs = width // LANES
    blocks = -(-length // LANES)
    lane = lax.broadcasted_iota(jnp.int32, (1, LANES), 1)
    low = lane < HEAD_DIM
    stats_ref[...] = jnp.zeros_like(stats_ref)
    ready(qkv_ref, ext_ref)
    for block in range(blocks):
        start = block * LANES
        rows = min(LANES, length - start)
        count = start + rows
        shift = (blocks - 1 - block) * LANES
        penalty = penalty_of(
            rows, start, count, seg_col_ref[start : start + rows, :], seg_row_ref[:, 0:count]
        )

        def one_pair(pair, carry):
            columns = pair_columns(pair)
            query = halves(qkv_ref[start : start + rows, columns].astype(F32) * SCALE, low).astype(BF)
            key = qkv_ref[0:count, pair_columns(pair, width)]
            value = qkv_ref[0:count, pair_columns(pair, 2 * width)]
            scores = contract(query, key, 1, 1) + (
                ext_block(ext_ref, pair, rows, shift, count) + penalty
            )
            peak = jnp.max(scores, -1, keepdims=True)
            shifted = jnp.exp(scores - peak)
            total = jnp.sum(shifted, -1, keepdims=True)
            weights = (shifted * (1.0 / total)).astype(BF)
            mixed = merge(contract(weights, value, 1, 0), low)
            out_ref[start : start + rows, columns] = (mixed * scale_ref[:, columns]).astype(BF)
            level = peak + jnp.log(total)
            stats_ref[start : start + rows, :] += jnp.where(
                lane == 2 * pair, level[:rows], 0.0
            ) + jnp.where(lane == 2 * pair + 1, level[rows:], 0.0)
            return carry

        lax.fori_loop(0, pairs, one_pair, 0)


def level_of(stats, lane, pair):
    return jnp.concatenate(
        [
            jnp.sum(jnp.where(lane == 2 * pair + side, stats, 0.0), -1, keepdims=True)
            for side in (0, 1)
        ],
        0,
    )


def self_backward_kernel(
    qkv_ref,
    upstream_ref,
    ext_ref,
    seg_col_ref,
    seg_row_ref,
    stats_ref,
    ids_ref,
    grad_ref,
    table_ref,
    head_ref,
    key_sum,
    value_sum,
    offset_sum,
):
    length, width = upstream_ref.shape
    pairs = width // LANES
    blocks = -(-length // LANES)
    lane = lax.broadcasted_iota(jnp.int32, (1, LANES), 1)
    low = lane < HEAD_DIM
    key_sum[...] = jnp.zeros_like(key_sum)
    value_sum[...] = jnp.zeros_like(value_sum)
    offset_sum[...] = jnp.zeros_like(offset_sum)
    ready(qkv_ref, upstream_ref, ext_ref, stats_ref)
    head_ref[...] = jnp.zeros_like(head_ref)
    for block in range(blocks):
        start = block * LANES
        rows = min(LANES, length - start)
        count = start + rows
        shift = (blocks - 1 - block) * LANES
        penalty = penalty_of(
            rows, start, count, seg_col_ref[start : start + rows, :], seg_row_ref[:, 0:count]
        )

        def one_pair(pair, carry):
            columns = pair_columns(pair)
            query = halves(qkv_ref[start : start + rows, columns].astype(F32) * SCALE, low).astype(BF)
            key = qkv_ref[0:count, pair_columns(pair, width)]
            value = qkv_ref[0:count, pair_columns(pair, 2 * width)]
            upstream = halves(upstream_ref[start : start + rows, columns].astype(F32), low).astype(BF)
            level = level_of(stats_ref[start : start + rows, :], lane, pair)
            scores = contract(query, key, 1, 1) + (
                ext_block(ext_ref, pair, rows, shift, count) + penalty
            )
            probs = jnp.exp(scores - level)
            grad_probs = contract(upstream, value, 1, 1)
            inner = jnp.sum(probs * grad_probs, -1, keepdims=True)
            grad_scores = (probs * (grad_probs - inner)).astype(BF)
            weights = probs.astype(BF)
            grad_query = merge(contract(grad_scores, key, 1, 0), low) * SCALE
            grad_ref[start : start + rows, columns] = grad_query.astype(BF)
            key_sum[0:count, columns] += contract(grad_scores, query, 0, 0)
            value_sum[0:count, columns] += contract(weights, upstream, 0, 0)
            wide = grad_scores.astype(F32)
            if rows == LANES:
                offset_sum[pair, :, shift : shift + count] += wide
            else:
                offset_sum[pair, 0:rows, shift : shift + count] += wide[:rows]
                offset_sum[pair, LANES : LANES + rows, shift : shift + count] += wide[rows:]
            for side in (0, 1):
                part = jnp.sum(inner[side * rows : (side + 1) * rows], 0, keepdims=True)
                head_ref[pl.ds(2 * pair + side, 1), :] += jnp.broadcast_to(part, (1, LANES))
            return carry

        lax.fori_loop(0, pairs, one_pair, 0)
    grad_ref[:, width : 2 * width] = key_sum[...].astype(BF)
    grad_ref[:, 2 * width : 3 * width] = value_sum[...].astype(BF)
    span = offset_sum.shape[2]
    sub = lax.broadcasted_iota(jnp.int32, (8, span), 0)
    head_places = lax.broadcasted_iota(jnp.int32, (table_ref.shape[0], span), 0)
    by_offset = jnp.zeros((table_ref.shape[0], span), F32)
    for head in range(2 * pairs):
        total = None
        for group in range(LANES // 8):
            first = (head % 2) * LANES + group * 8
            piece = offset_sum[head // 2, first : first + 8, :]
            moved = piece if group == 0 else pltpu.roll(piece, span - group * 8, 1)
            total = moved if total is None else total + moved
        for bit in (1, 2, 4):
            total = jnp.where((sub & bit) > 0, pltpu.roll(total, span - bit, 1), total)
        line = jnp.sum(total, 0, keepdims=True)
        by_offset = by_offset + jnp.where(head_places == head, line, 0.0)
    choose = choice_of(ids_ref[...], table_ref.shape[1])
    table_ref[...] = contract(by_offset, choose, 1, 1, lax.Precision.HIGHEST)


def norm_parts(values):
    center = values - jnp.mean(values, -1, keepdims=True)
    factor = lax.rsqrt(jnp.mean(center * center, -1, keepdims=True) + EPSILON)
    return center * factor, factor


def norm_back(values, gain, upstream):
    hat, factor = norm_parts(values)
    leaned = upstream * gain
    grad = factor * (
        leaned
        - jnp.mean(leaned, -1, keepdims=True)
        - hat * jnp.mean(leaned * hat, -1, keepdims=True)
    )
    return grad, jnp.sum(upstream * hat, 0), jnp.sum(upstream, 0)


def kv_blocks(key_ref, value_ref, near_ref):
    step = key_ref.shape[0]
    return jnp.concatenate(
        [key_ref[...], near_ref[3 * step : 4 * step, :], value_ref[...], near_ref[4 * step : 5 * step, :]],
        0,
    )


def four_of(own_ref, near_ref, far_ref, across_ref, index):
    step = own_ref.shape[0]
    rows = slice(index * step, (index + 1) * step)
    return jnp.concatenate([own_ref[...], near_ref[rows, :], far_ref[rows, :], across_ref[rows, :]], 0)


def pack_kernel(*refs):
    *blocks, first_ref, trio_ref, sems = refs
    targets = [first_ref] * 5 + [trio_ref] * 3
    copies = []
    for index, (block, target) in enumerate(zip(blocks, targets)):
        start = block.shape[0] * (index % 5)
        copies.append(
            pltpu.make_async_copy(
                block, target.at[start : start + block.shape[0], :], sems.at[index]
            )
        )
    for copy in copies:
        copy.start()
    for copy in copies:
        copy.wait()


def project_kernel(tokens_ref, gains_ref, q0, k0, v0, near_ref, self_in_ref, qkv_ref, weight_ref):
    step = q0.shape[0]
    for index, own in enumerate((q0, k0, v0)):
        weight_ref[2 * index * step : (2 * index + 1) * step, :] = own[...]
        weight_ref[(2 * index + 1) * step : (2 * index + 2) * step, :] = near_ref[
            index * step : (index + 1) * step, :
        ]
    hat, _ = norm_parts(tokens_ref[...].astype(F32))
    self_in = (hat * gains_ref[10:11, :] + gains_ref[11:12, :]).astype(BF)
    self_in_ref[...] = self_in
    qkv_ref[...] = contract(self_in, weight_ref[...], 1, 1).astype(BF)


def memory_kernel(gathered_ref, k0, v0, near_ref, gains_ref, normed_ref, kv_ref, stats_ref, *, count):
    batch, rows = gathered_ref.shape[0], gathered_ref.shape[1] - 16
    sums = None
    for index in range(batch):
        piece = gathered_ref[index, rows : rows + 16, :].astype(F32)
        sums = piece if sums is None else sums + piece
    total = jnp.sum(sums[0:3], 0, keepdims=True) / count
    square = jnp.sum(sums[3:6], 0, keepdims=True) / count
    factor = lax.rsqrt(square - total * total + EPSILON)
    stats_ref[0:1, :] = total
    stats_ref[1:2, :] = factor
    for index in range(batch):
        hat = (gathered_ref[index, 0:rows, :].astype(F32) - total) * factor
        normed_ref[index * rows : (index + 1) * rows, :] = (
            hat * gains_ref[8:9, :] + gains_ref[9:10, :]
        ).astype(BF)
    kv_ref[...] = contract(normed_ref[...], kv_blocks(k0, v0, near_ref), 1, 1).astype(BF)


def mid_forward_kernel(
    keep_ref,
    far_ref,
    tokens_ref,
    o0,
    q0,
    c0,
    near_ref,
    far_trio_ref,
    across_ref,
    kv_ref,
    far_kv_ref,
    valid_ref,
    gains_ref,
    attn_ref,
    first_ref,
    cross_in_ref,
    query_ref,
    mixed_ref,
    cross_attn_ref,
    second_ref,
    ffn_ref,
    stats_ref,
):
    def gain(index):
        return gains_ref[index : index + 1, :]

    half_lanes = keep_ref.shape[1]
    trio = (near_ref, far_trio_ref, across_ref)
    output_all = four_of(o0, *trio, 0)
    attn = contract(keep_ref[...], output_all[:half_lanes], 1, 0) + contract(
        far_ref[...], output_all[half_lanes:], 1, 0
    )
    attn_ref[...] = attn
    first = tokens_ref[...].astype(F32) + norm_parts(attn)[0] * gain(0) + gain(1)
    first_ref[...] = first
    cross_in = (norm_parts(first)[0] * gain(2) + gain(3)).astype(BF)
    cross_in_ref[...] = cross_in
    query_ref[...] = contract(cross_in, four_of(q0, *trio, 1), 1, 1).astype(BF)
    lane = lax.broadcasted_iota(jnp.int32, (1, LANES), 1)
    low = lane < HEAD_DIM
    penalty = jnp.where(valid_ref[...] > 0, 0.0, MASKED).astype(F32)
    stats_ref[...] = jnp.zeros_like(stats_ref)
    ready(kv_ref, far_kv_ref)

    def one_pair(pair, carry):
        for far, source in enumerate((kv_ref, far_kv_ref)):
            columns = pair_columns(pair, far * half_lanes)
            number = pair + far * (half_lanes // LANES)
            query = query_ref[:, columns].astype(F32) * SCALE
            key = source[:, pair_columns(pair)]
            value = source[:, pair_columns(pair, half_lanes)]
            mixed = None
            for side in (0, 1):
                mine = low if side == 0 else jnp.logical_not(low)
                scores = contract(jnp.where(mine, query, 0.0).astype(BF), key, 1, 1) + penalty
                peak = jnp.max(scores, -1, keepdims=True)
                shifted = jnp.exp(scores - peak)
                total = jnp.sum(shifted, -1, keepdims=True)
                weights = (shifted * (1.0 / total)).astype(BF)
                part = contract(weights, value, 1, 0)
                mixed = part if mixed is None else jnp.where(low, mixed, part)
                stats_ref[...] += jnp.where(lane == 2 * number + side, peak + jnp.log(total), 0.0)
            mixed_ref[:, columns] = mixed.astype(BF)
        return carry

    lax.fori_loop(0, half_lanes // LANES, one_pair, 0)
    cross_attn = contract(mixed_ref[...], four_of(c0, *trio, 2), 1, 0)
    cross_attn_ref[...] = cross_attn
    second = first_ref[...] + norm_parts(cross_attn)[0] * gain(4) + gain(5)
    second_ref[...] = second
    ffn_ref[...] = (norm_parts(second)[0] * gain(6) + gain(7)).astype(BF)


def mid_backward_kernel(
    back_ref,
    came_ref,
    upstream_ref,
    second_ref,
    cross_attn_ref,
    first_ref,
    attn_ref,
    query_ref,
    stats_ref,
    o0,
    q0,
    c0,
    near_ref,
    far_trio_ref,
    across_ref,
    kv_ref,
    far_kv_ref,
    valid_ref,
    gains_ref,
    scale_ref,
    grad_first_ref,
    grad_cattn_ref,
    grad_query_ref,
    grad_attn_ref,
    keep_ref,
    far_ref,
    grad_kv_ref,
    far_grad_kv_ref,
    norms_ref,
    mixed_ref,
):
    def gain(index):
        return gains_ref[index : index + 1, :]

    half_lanes = keep_ref.shape[1]
    trio = (near_ref, far_trio_ref, across_ref)
    ffn_grad = back_ref[...] + came_ref[...].astype(F32)
    grad, norms_ref[6, :], norms_ref[7, :] = norm_back(second_ref[...], gain(6), ffn_grad)
    grad_second = upstream_ref[...].astype(F32) + grad
    grad_first_ref[...] = grad_second
    grad, norms_ref[4, :], norms_ref[5, :] = norm_back(cross_attn_ref[...], gain(4), grad_second)
    grad_cattn = grad.astype(BF)
    grad_cattn_ref[...] = grad_cattn
    mixed_ref[...] = contract(grad_cattn, four_of(c0, *trio, 2), 1, 1).astype(BF)
    lane = lax.broadcasted_iota(jnp.int32, (1, LANES), 1)
    low = lane < HEAD_DIM
    penalty = jnp.where(valid_ref[...] > 0, 0.0, MASKED).astype(F32)
    ready(query_ref, stats_ref, kv_ref, far_kv_ref)

    def one_pair(pair, carry):
        for far, source in enumerate((kv_ref, far_kv_ref)):
            columns = pair_columns(pair, far * half_lanes)
            number = pair + far * (half_lanes // LANES)
            query = query_ref[:, columns].astype(F32) * SCALE
            upstream = mixed_ref[:, columns].astype(F32)
            key = source[:, pair_columns(pair)]
            value = source[:, pair_columns(pair, half_lanes)]
            grad_query = grad_key = grad_value = None
            for side in (0, 1):
                mine = low if side == 0 else jnp.logical_not(low)
                my_query = jnp.where(mine, query, 0.0).astype(BF)
                my_upstream = jnp.where(mine, upstream, 0.0).astype(BF)
                level = jnp.sum(
                    jnp.where(lane == 2 * number + side, stats_ref[...], 0.0), -1, keepdims=True
                )
                probs = jnp.exp(contract(my_query, key, 1, 1) + penalty - level)
                grad_probs = contract(my_upstream, value, 1, 1)
                inner = jnp.sum(probs * grad_probs, -1, keepdims=True)
                grad_scores = (probs * (grad_probs - inner)).astype(BF)
                part_query = contract(grad_scores, key, 1, 0)
                part_key = contract(grad_scores, my_query, 0, 0)
                part_value = contract(probs.astype(BF), my_upstream, 0, 0)
                if side == 0:
                    grad_query, grad_key, grad_value = part_query, part_key, part_value
                else:
                    grad_query = jnp.where(low, grad_query, part_query)
                    grad_key, grad_value = grad_key + part_key, grad_value + part_value
            grad_query_ref[:, columns] = (grad_query * SCALE).astype(BF)
            target = far_grad_kv_ref if far else grad_kv_ref
            target[:, pair_columns(pair)] = grad_key.astype(target.dtype)
            target[:, pair_columns(pair, half_lanes)] = grad_value.astype(target.dtype)
        return carry

    lax.fori_loop(0, half_lanes // LANES, one_pair, 0)
    grad_in = contract(grad_query_ref[...], four_of(q0, *trio, 1), 1, 0)
    grad, norms_ref[2, :], norms_ref[3, :] = norm_back(first_ref[...], gain(2), grad_in)
    grad_first = grad_first_ref[...] + grad
    grad_first_ref[...] = grad_first
    grad, norms_ref[0, :], norms_ref[1, :] = norm_back(attn_ref[...], gain(0), grad_first)
    grad_attn = grad.astype(BF)
    grad_attn_ref[...] = grad_attn
    grad_mixed = (contract(grad_attn, four_of(o0, *trio, 0), 1, 1) * scale_ref[...]).astype(BF)
    keep_ref[...] = grad_mixed[:, :half_lanes]
    far_ref[...] = grad_mixed[:, half_lanes:]


def put_blocks(keep_ref, give_ref, place, step, grads):
    block = grads.astype(BF)
    for index in range(block.shape[0] // (2 * step)):
        rows = slice((place + index) * step, (place + index + 1) * step)
        keep_ref[rows, :] = block[2 * index * step : (2 * index + 1) * step]
        give_ref[rows, :] = block[(2 * index + 1) * step : (2 * index + 2) * step]


def mid_weights_kernel(
    keep_scaled_ref,
    far_scaled_ref,
    grad_attn_ref,
    mixed_ref,
    grad_cattn_ref,
    grad_query_ref,
    cross_in_ref,
    keep_ref,
    give_ref,
):
    step = keep_ref.shape[0] // 6
    put = functools.partial(put_blocks, keep_ref, give_ref)
    put(0, step, contract(keep_scaled_ref[...], grad_attn_ref[...], 0, 0))
    put(1, step, contract(mixed_ref[:, 0 : 2 * step], grad_cattn_ref[...], 0, 0))
    put(2, step, contract(grad_query_ref[:, 0 : 2 * step], cross_in_ref[...], 0, 0))
    put(3, step, contract(far_scaled_ref[...], grad_attn_ref[...], 0, 0))
    put(4, step, contract(mixed_ref[:, 2 * step : 4 * step], grad_cattn_ref[...], 0, 0))
    put(5, step, contract(grad_query_ref[:, 2 * step : 4 * step], cross_in_ref[...], 0, 0))


def memory_weights_kernel(
    grad_kv_ref, came_kv_ref, normed_ref, k0, v0, near_ref, keep_ref, give_ref, normed_grad_ref
):
    step = k0.shape[0]
    grad_kv = (grad_kv_ref[...] + came_kv_ref[...].astype(F32)).astype(BF)
    put_blocks(keep_ref, give_ref, 0, step, contract(grad_kv, normed_ref[...], 0, 0))
    normed_grad_ref[...] = contract(grad_kv, kv_blocks(k0, v0, near_ref), 1, 0)


def self_weights_kernel(grad_qkv_ref, self_in_ref, keep_ref, give_ref):
    step = keep_ref.shape[0] // 3
    for index in range(3):
        lanes = slice(2 * index * step, 2 * (index + 1) * step)
        put_blocks(
            keep_ref, give_ref, index, step, contract(grad_qkv_ref[:, lanes], self_in_ref[...], 0, 0)
        )


def flip_over(axis, bit):
    def send(block):
        size = lax.axis_size(axis)
        return lax.ppermute(block, axis, [(i, i ^ bit) for i in range(size)])

    return send


def mate(block):
    return flip_over("mp", 1)(block)


def peer(block):
    return flip_over("mp", 2)(block)


def cut(block, index, size, axis=0):
    return lax.dynamic_slice_in_dim(block, index * size, size, axis)


def dot_right(left, right):
    return contract(left, right, 1, 1)


def dot_left(left, right):
    return contract(left, right, 0, 0)


def dot(left, right):
    return contract(left, right, 1, 0)


def batch_bits():
    size = lax.axis_size("batch")
    bits = []
    while (1 << len(bits)) < size:
        bits.append(1 << len(bits))
    return bits


def pack_small(parts):
    flat = jnp.concatenate([part.reshape(-1) for part in parts])
    size = -(-flat.shape[0] // (8 * LANES)) * 8 * LANES
    return jnp.pad(flat, (0, size - flat.shape[0])).reshape(-1, LANES)


def unpack_small(packed, shapes):
    flat = packed.reshape(-1)
    parts, start = [], 0
    for shape in shapes:
        size = 1
        for extent in shape:
            size *= extent
        parts.append(flat[start : start + size].reshape(shape))
        start += size
    return parts


def shape_of(shape, dtype):
    return jax.ShapeDtypeStruct(shape, dtype)


def pieces_of(values):
    high = lax.reduce_precision(values, 8, 7)
    middle = lax.reduce_precision(values - high, 8, 7)
    return [high.astype(BF), middle.astype(BF), (values - high - middle).astype(BF)]


def tie(*arrays):
    return lax.optimization_barrier(arrays)


def two_of(index, own, other):
    return jnp.where(index == 0, own, other), jnp.where(index == 0, other, own)


def in_order(index, own, other):
    return jnp.concatenate(two_of(index, own, other), 0)


class Summing:
    def __init__(self, blocks, bits):
        self.blocks = blocks
        self.bits = bits
        self.todo = [("halve", bit) for bit in bits] + [("double", bit) for bit in reversed(bits)]
        self.start = None
        self.size = blocks[0].shape[0]
        self.terms = []
        self.block = None
        self.came = None

    def part(self, start, size):
        total = lax.dynamic_slice_in_dim(self.base, start, size).astype(F32)
        for offset, came in self.terms:
            total = total + lax.dynamic_slice_in_dim(came, start - offset, size).astype(F32)
        return total.astype(BF)

    def prepare(self):
        kind, bit = self.todo.pop(0)
        index = (lax.axis_index("batch") // bit) % 2
        self.kind, self.index, self.bit = kind, index, bit
        if kind == "halve" and self.start is None:
            first, second = self.blocks
            self.base = jnp.where(index == 0, first, second)
            self.give = jnp.where(index == 0, second, first)
            self.start = jnp.int32(0)
        elif kind == "halve":
            self.size = self.size // 2
            self.give = self.part(self.start + (1 - index) * self.size, self.size)
            self.start = self.start + index * self.size
        else:
            if self.block is None:
                self.block = self.part(self.start, self.size)
            self.give = self.block

    def land(self):
        if self.kind == "halve":
            self.terms.append((self.start, self.came))
        elif self.todo:
            self.block = in_order(self.index, self.block, self.came)
        else:
            self.block = two_of(self.index, self.block, self.came)
        self.came = None

    def blocks_of(self, rows):
        whole = jnp.concatenate(self.block, 0)
        return [whole[i : i + rows].astype(F32) for i in range(0, whole.shape[0], rows)]


def advance(flows, *others):
    for flow in flows:
        if flow.came is not None:
            flow.land()
    going = [flow for flow in flows if flow.todo]
    for flow in going:
        flow.prepare()
    ready = tie(*[flow.give for flow in going], *others) if going or others else ()
    for flow, give in zip(going, ready):
        flow.give = give
        flow.came = flip_over("batch", flow.bit)(give)
    return ready[len(going) :]


def finish(flows):
    while any(flow.came is not None for flow in flows):
        advance(flows)


def cost_of(micros):
    return pl.CostEstimate(flops=0, bytes_accessed=int(micros * 3.0e6), transcendentals=0)


def on_device(
    tokens,
    segment_ids,
    bucket_ids,
    memory,
    memory_mask,
    cotangent,
    self_gain,
    self_bias,
    query_weight,
    key_weight,
    value_weight,
    rel_table,
    head_scale,
    output_weight,
    after_gain,
    after_bias,
    cross_gain,
    cross_bias,
    batch_gain,
    batch_bias,
    cross_query,
    cross_key,
    cross_value,
    cross_output,
    crossout_gain,
    crossout_bias,
    ffn_gain,
    ffn_bias,
    up_weight,
    middle_gain,
    middle_bias,
    down_weight,
):
    place = lax.axis_index("mp")
    core, side = place % 2, place // 2
    batch = lax.axis_size("batch")
    bits = batch_bits()
    quarter, _, width = tokens.shape
    length = 4 * quarter
    half = 2 * quarter
    heads = 2 * rel_table.shape[1]
    lanes = heads * HEAD_DIM
    step = lanes // 2
    units = up_weight.shape[1]
    all_hidden = 4 * units
    mem_rows = memory.shape[0]
    positions = mem_rows * batch

    def call(kernel, shapes, micros, late=(), scratch=(), name=None):
        def run(*args):
            taken = list(scratch)
            specs = [pl.BlockSpec(memory_space=pltpu.VMEM)] * len(args)
            wrapped = kernel
            if late:
                for index in late:
                    specs[index] = pl.BlockSpec(memory_space=pltpu.HBM)
                    taken.append(pltpu.VMEM(args[index].shape, args[index].dtype))
                taken.append(pltpu.SemaphoreType.DMA((len(late),)))
                wrapped = with_late(kernel, len(args), late)
            return pl.pallas_call(
                wrapped,
                out_shape=shapes,
                in_specs=specs,
                scratch_shapes=taken,
                compiler_params=kernel_params(late),
                cost_estimate=cost_of(micros),
                name=name,
            )(*args)

        return run

    def rows_of(array):
        keep = jnp.where(core == 0, array[:, 0], array[:, 1])
        give = jnp.where(core == 0, array[:, 1], array[:, 0])
        return keep, give

    keep_tokens, give_tokens = rows_of(tokens)
    far_keep, far_give = peer(keep_tokens), flip_over("mp", 3)(give_tokens)
    near_tokens = mate(give_tokens)

    query_t, key_t, value_t = query_weight.T, key_weight.T, value_weight.T
    own_trio = [output_weight, cross_query.T, cross_output]
    key_c, value_c = cross_key.T, cross_value.T
    all_blocks = [query_t, key_t, value_t, key_c, value_c, *own_trio]
    anywhere = pl.BlockSpec(memory_space=pl.ANY)
    own_first, trio = pl.pallas_call(
        pack_kernel,
        out_shape=tuple(shape_of((count * step, width), BF) for count in (5, 3)),
        in_specs=[anywhere] * len(all_blocks),
        out_specs=(anywhere,) * 2,
        scratch_shapes=[pltpu.SemaphoreType.DMA((len(all_blocks),))],
        compiler_params=pltpu.CompilerParams(vmem_limit_bytes=1024 * 1024),
        cost_estimate=cost_of(3),
        name="pack",
    )(*all_blocks)
    near_first = mate(own_first)
    far_keep, far_give, trio = tie(far_keep, far_give, trio)
    far_trio = peer(trio)
    near_small = unpack_small(
        mate(pack_small([rel_table.T, head_scale, middle_gain, middle_bias])),
        [(heads // 2, rel_table.shape[0]), (heads // 2,), (units,), (units,)],
    )
    both_scale = jnp.concatenate([head_scale, near_small[1]])
    gain_pair = jnp.concatenate([middle_gain, near_small[2]])
    bias_pair = jnp.concatenate([middle_bias, near_small[3]])
    gains = jnp.stack(
        [
            after_gain,
            after_bias,
            cross_gain,
            cross_bias,
            crossout_gain,
            crossout_bias,
            ffn_gain,
            ffn_bias,
            batch_gain,
            batch_bias,
            self_gain,
            self_bias,
        ]
    )

    blocks = -(-length // LANES)
    span = blocks * LANES
    split = length - 1 - (blocks - 1) * LANES
    ids = jnp.concatenate(
        [
            bucket_ids[split:length],
            jnp.full((span - length,), -1, bucket_ids.dtype),
            bucket_ids[:split],
        ]
    )[None, :]
    table = jnp.concatenate([rel_table.T, near_small[0]], 0)
    table = jnp.pad(table, ((0, -heads % 8), (0, 0)))
    ext = call(bias_kernel, shape_of((heads // 2, 2 * LANES, span), F32), 2, name="bias")(ids, table)

    mem_float = memory.astype(F32)
    sums = [jnp.sum(mem_float, (0, 1)), jnp.sum(mem_float * mem_float, (0, 1))]
    extra = jnp.stack([piece for total in sums for piece in pieces_of(total)])
    extra = jnp.broadcast_to(jnp.pad(extra, ((0, 10), (0, 0)))[None], (batch, 16, width))
    rows_here = memory.reshape(mem_rows, batch, 2, width)
    my_rows = jnp.where(core == 0, rows_here[:, :, 0], rows_here[:, :, 1])
    outgoing = jnp.concatenate([jnp.swapaxes(my_rows, 0, 1), extra], 1)
    gathered = lax.all_to_all(outgoing, "batch", split_axis=0, concat_axis=0, tiled=True)
    count = positions * memory.shape[1]
    normed, own_kv, mem_stats = call(
        functools.partial(memory_kernel, count=count),
        (
            shape_of((positions, width), BF),
            shape_of((positions, width), BF),
            shape_of((2, width), F32),
        ),
        2,
        name="memory",
    )(gathered, key_c, value_c, near_first, gains)
    far_kv = peer(own_kv)

    own_tokens = in_order(core, keep_tokens, near_tokens)
    row_tokens = in_order(side, own_tokens, in_order(core, far_keep, far_give))
    self_in, qkv, qkv_weight = call(
        project_kernel,
        (
            shape_of((length, width), BF),
            shape_of((length, 3 * lanes), BF),
            shape_of((3 * lanes, width), BF),
        ),
        5,
        name="project",
    )(row_tokens, gains, query_t, key_t, value_t, near_first)
    keep_cotangent, give_cotangent = rows_of(cotangent)
    segment = lax.dynamic_index_in_dim(segment_ids, core, 0, keepdims=False)
    seg_col, seg_row = segment[:, None], segment[None, :]
    scale_lanes = jnp.repeat(both_scale, HEAD_DIM)[None, :]
    qkv, own_kv, give_cotangent, up_give, down_give, trio = tie(
        qkv, own_kv, give_cotangent, up_weight, down_weight, trio
    )
    near_trio = mate(trio)
    near_cotangent = mate(give_cotangent)
    scaled, stats = call(
        self_forward_kernel,
        (shape_of((length, lanes), BF), shape_of((length, LANES), F32)),
        16,
        name="self_forward",
    )(qkv, ext, seg_col, seg_row, scale_lanes)
    scaled, far_kv, far_trio, near_cotangent = tie(scaled, far_kv, far_trio, near_cotangent)
    keep_scaled, far_scaled = cut(scaled, side, half), peer(cut(scaled, 1 - side, half))
    across_trio = mate(far_trio)
    own_cotangent = in_order(core, keep_cotangent, near_cotangent)
    up_pair = jnp.concatenate([up_weight, mate(up_give)], 1)
    down_pair = jnp.concatenate([down_weight, mate(down_give)], 0)
    far_scaled, own_cotangent, up_pair, down_pair, across_trio = tie(
        far_scaled, own_cotangent, up_pair, down_pair, across_trio
    )
    far_cotangent = peer(own_cotangent)
    trio_args = [*own_trio, near_trio, far_trio, across_trio]

    valid = lax.dynamic_index_in_dim(memory_mask, core, 0, keepdims=True)
    wide, narrow = shape_of((half, width), F32), shape_of((half, width), BF)
    attn, first, cross_in, cross_queries, cross_mixed, cross_attn, second, ffn_own, cross_stats = call(
        mid_forward_kernel,
        (wide, wide, narrow, narrow, narrow, wide, wide, narrow, shape_of((half, LANES), F32)),
        10,
        name="mid_forward",
    )(keep_scaled, far_scaled, own_tokens, *trio_args, own_kv, far_kv, valid, gains)

    ffn_own, far_cotangent = tie(ffn_own, far_cotangent)
    ffn_far = peer(ffn_own)

    def ffn_start(values, grad_middle):
        gate = dot(values, up_pair)
        active = gate * (0.5 * (1.0 + lax.erf(gate * (0.5**0.5))))
        leaned = grad_middle * gain_pair
        sums = jnp.stack(
            [
                jnp.sum(active, -1),
                jnp.sum(active * active, -1),
                jnp.sum(leaned, -1),
                jnp.sum(leaned * active, -1),
            ]
        )
        return gate, sums

    grad_middle_own = dot_right(own_cotangent, down_pair)
    grad_middle_far = dot_right(far_cotangent, down_pair)
    gate_own, sums_own = ffn_start(ffn_own, grad_middle_own)
    ffn_far, grad_middle_far, gate_own, sums_own = tie(ffn_far, grad_middle_far, gate_own, sums_own)
    gate_far, sums_far = ffn_start(ffn_far, grad_middle_far)
    scale_row = jnp.pad(both_scale, (0, half - heads))[None, :]
    came_sums = peer(jnp.concatenate([sums_far, sums_own, scale_row], 0))
    sums_own = (sums_own + came_sums[:4]) / all_hidden
    sums_far = (sums_far + came_sums[4:8]) / all_hidden
    all_scale = jnp.concatenate([both_scale, came_sums[8, :heads]])

    def ffn_end(gate, grad_middle, sums):
        chance = 0.5 * (1.0 + lax.erf(gate * (0.5**0.5)))
        active = gate * chance
        leaned = grad_middle * gain_pair
        act_mean = sums[0][:, None]
        act_scale = lax.rsqrt(sums[1][:, None] - act_mean * act_mean + EPSILON)
        act_hat = (active - act_mean) * act_scale
        middle = (act_hat * gain_pair + bias_pair).astype(BF)
        leaned_mean = sums[2][:, None]
        leaned_hat = act_scale * (sums[3][:, None] - act_mean * leaned_mean)
        grad_active = act_scale * (leaned - leaned_mean - act_hat * leaned_hat)
        density = jnp.exp(-0.5 * gate * gate) * ((2.0 * jnp.pi) ** -0.5)
        grad_gate = (grad_active * (chance + gate * density)).astype(BF)
        return middle, grad_gate, jnp.sum(grad_middle * act_hat, 0), jnp.sum(grad_middle, 0)

    middle_far, gate_grad_far, mid_gain_far, mid_bias_far = ffn_end(
        gate_far, grad_middle_far, sums_far
    )
    back_far = dot_right(gate_grad_far, up_pair).astype(BF)
    back_far, gate_own, grad_middle_own, sums_own = tie(
        back_far, gate_own, grad_middle_own, sums_own
    )
    back_came = peer(back_far)
    middle_own, gate_grad_own, mid_gain_own, mid_bias_own = ffn_end(
        gate_own, grad_middle_own, sums_own
    )
    grad_mid_gain = mid_gain_own + mid_gain_far
    grad_mid_bias = mid_bias_own + mid_bias_far

    def two(far, own):
        return dot_left(*far) + dot_left(*own)

    def units_of(array, index):
        return array[:, index * units : (index + 1) * units]

    def up_grad(index):
        return two(
            (ffn_far, units_of(gate_grad_far, index)), (ffn_own, units_of(gate_grad_own, index))
        )

    def down_grad(index):
        return two(
            (units_of(middle_far, index), far_cotangent), (units_of(middle_own, index), own_cotangent)
        )

    part_up = (up_grad(0) + mate(up_grad(1).astype(BF)).astype(F32)).astype(BF)
    part_down = (down_grad(0) + mate(down_grad(1).astype(BF)).astype(F32)).astype(BF)
    back_own = dot_right(gate_grad_own, up_pair)
    out_far = dot(middle_far, down_pair).astype(BF)
    part_ffn = jnp.concatenate([part_up, part_down], 0)
    back_came, back_own, part_ffn, out_far = tie(back_came, back_own, part_ffn, out_far)
    ffn_chunk = lax.psum_scatter(part_ffn, "batch", scatter_dimension=0, tiled=True)
    turned = bits[1:] + bits[:1]
    out_came = peer(out_far)

    (
        grad_first,
        grad_cattn,
        grad_cq,
        grad_attn,
        keep_mixed,
        give_mixed,
        grad_kv,
        give_kv,
        norms,
    ) = call(
        mid_backward_kernel,
        (
            wide,
            narrow,
            narrow,
            narrow,
            shape_of((half, lanes), BF),
            shape_of((half, lanes), BF),
            shape_of((positions, width), F32),
            shape_of((positions, width), BF),
            shape_of((8, width), F32),
        ),
        16,
        late=(3, 2, 4, 11, 12, 13, 14, 7, 8, 15, 16, 10, 5, 6, 9),
        scratch=[pltpu.VMEM((half, width), BF)],
        name="mid_backward",
    )(
        back_own,
        back_came,
        own_cotangent,
        second,
        cross_attn,
        first,
        attn,
        cross_queries,
        cross_stats,
        *trio_args,
        own_kv,
        far_kv,
        valid,
        gains,
        jnp.repeat(all_scale, HEAD_DIM)[None, :],
    )
    came_mixed = peer(give_mixed)
    keep_cross, give_cross = call(
        mid_weights_kernel,
        (shape_of((6 * step, width), BF), shape_of((6 * step, width), BF)),
        4,
        name="mid_weights",
    )(keep_scaled, far_scaled, grad_attn, cross_mixed, grad_cattn, grad_cq, cross_in)
    near_cross = mate(give_cross)
    far_cross = (keep_cross[3 * step :].astype(F32) + near_cross[3 * step :].astype(F32)).astype(BF)
    grad_mixed = in_order(side, keep_mixed, came_mixed)
    grad_mixed, far_cross, give_kv = tie(grad_mixed, far_cross, give_kv)
    came_cross = peer(far_cross)
    came_kv = peer(give_kv)
    grad_qkv, grad_table, grad_heads = call(
        self_backward_kernel,
        (
            shape_of((length, 3 * lanes), BF),
            shape_of(table.shape, F32),
            shape_of((8, LANES), F32),
        ),
        22,
        scratch=[
            pltpu.VMEM((length, lanes), F32),
            pltpu.VMEM((length, lanes), F32),
            pltpu.VMEM(ext.shape, F32),
        ],
        name="self_backward",
    )(qkv, grad_mixed, ext, seg_col, seg_row, stats, ids)
    grad_qkv, ffn_chunk, out_came, came_cross, came_kv = tie(
        grad_qkv, ffn_chunk, out_came, came_cross, came_kv
    )
    sum_ffn = lax.all_gather(ffn_chunk, "batch", axis=0, tiled=True)
    far_in = dot(cut(grad_qkv, 1 - side, half), qkv_weight).astype(BF)
    came_in = peer(far_in)
    grad_qkv, far_in = tie(grad_qkv, far_in)
    keep_last, give_last = call(
        self_weights_kernel,
        (shape_of((3 * step, width), BF), shape_of((3 * step, width), BF)),
        4,
        name="self_weights",
    )(grad_qkv, self_in)
    near_last = mate(give_last)
    keep_mem, give_mem, normed_grad = call(
        memory_weights_kernel,
        (
            shape_of((2 * step, width), BF),
            shape_of((2 * step, width), BF),
            shape_of((positions, width), F32),
        ),
        2,
        name="memory_weights",
    )(grad_kv, came_kv, normed, key_c, value_c, near_first)
    near_mem = mate(give_mem)

    def add_up(*terms):
        total = terms[0].astype(F32)
        for term in terms[1:]:
            total = total + term.astype(F32)
        return total.astype(BF)

    part_last = add_up(keep_last, near_last)
    some = 3 * step // 2
    last_sum = Summing((part_last[:some], part_last[some:]), turned)
    part_cross = jnp.concatenate(
        [add_up(keep_cross[: 3 * step], near_cross[: 3 * step], came_cross), add_up(keep_mem, near_mem)],
        0,
    )
    some = 5 * step // 2
    cross_sum = Summing((part_cross[:some], part_cross[some:]), bits)
    last_flows = [last_sum, cross_sum]
    grad_qkv, out_came, normed_grad = advance(last_flows, grad_qkv, out_came, normed_grad)
    out_own = (second + dot(middle_own, down_pair) + out_came.astype(F32)).astype(BF)

    def by_quarter(own):
        keep = cut(own, core, quarter)
        came = mate(cut(own, 1 - core, quarter))
        return jnp.stack([jnp.where(core == 0, keep, came), jnp.where(core == 0, came, keep)], 1)

    output = by_quarter(out_own)
    half_cols = width // 2
    give_normed = cut(normed_grad, 1 - side, half_cols, 1).astype(BF)
    back_in = dot(cut(grad_qkv, side, half), qkv_weight)
    back_in, came_in, give_normed, output = advance(
        last_flows, back_in, came_in, give_normed, output
    )
    came_half = peer(give_normed)
    grad_self_in = back_in + came_in.astype(F32)
    back_tokens, grad_self_gain, grad_self_bias = norm_back(
        own_tokens.astype(F32), self_gain, grad_self_in
    )
    own_grad_tokens = grad_first + back_tokens
    half_normed = cut(normed_grad, side, half_cols, 1) + came_half.astype(F32)
    channels = width // 4
    keep_normed = cut(half_normed, core, channels, 1)
    give_part = cut(half_normed, 1 - core, channels, 1).astype(BF)

    own_heads = heads // 2

    def small_of(index):
        mine = slice(index * own_heads, (index + 1) * own_heads)
        some = slice(index * units, (index + 1) * units)
        return pack_small(
            [
                grad_table[mine],
                grad_heads[mine, 0] / both_scale[mine],
                grad_mid_gain[some],
                grad_mid_bias[some],
            ]
        )

    shared = pack_small([norms, grad_self_gain, grad_self_bias])
    keep_small = small_of(0)
    here = shared.shape[0]
    give_small = jnp.concatenate([shared, small_of(1)], 0)
    own_grad_tokens, give_part, give_small = advance(
        last_flows, own_grad_tokens, give_part, give_small
    )
    came_small = mate(give_small)
    came_normed = mate(give_part).astype(F32)
    grad_tokens = by_quarter(own_grad_tokens)
    both_normed = jnp.stack(
        [
            jnp.where(core == 0, keep_normed, came_normed),
            jnp.where(core == 0, came_normed, keep_normed),
        ],
        1,
    ).astype(BF)
    shared = shared + came_small[:here]
    shared, both_normed, grad_tokens = advance(last_flows, shared, both_normed, grad_tokens)
    came_shared = peer(shared)
    grad_normed = lax.all_to_all(
        both_normed, "batch", split_axis=0, concat_axis=1, tiled=True
    ).astype(F32)
    mean_slice = cut(mem_stats[0], place, channels)
    gain_slice = cut(batch_gain, place, channels)
    scale_slice = cut(mem_stats[1], place, channels)
    hat_slice = (cut(memory, place, channels, 2).astype(F32) - mean_slice) * scale_slice
    shift_term = jnp.sum(grad_normed, (0, 1))
    scale_term = jnp.sum(grad_normed * hat_slice, (0, 1))
    mem_small = pack_small([shift_term, scale_term])
    total = jnp.concatenate([shared + came_shared, keep_small + came_small[here:], mem_small], 0)
    for bit in bits:
        (total,) = advance(last_flows, total)
        total = total + flip_over("batch", bit)(total)
    finish(last_flows)
    sum_up, sum_down = sum_ffn[:width].astype(F32), sum_ffn[width:].astype(F32)
    sum_output, sum_coutput, sum_cquery, sum_ckey, sum_cvalue = cross_sum.blocks_of(step)
    sum_query, sum_key, sum_value = last_sum.blocks_of(step)
    there = here + keep_small.shape[0]
    norm_totals = unpack_small(total[:here], [(width,)] * 10)
    sum_table, sum_scale, sum_mid_gain, sum_mid_bias = unpack_small(
        total[here:there], [(own_heads, table.shape[1]), (own_heads,), (units,), (units,)]
    )
    shift_total, scale_total = unpack_small(total[there:], [(channels,), (channels,)])
    grad_memory = (
        gain_slice
        * scale_slice
        * (grad_normed - shift_total / count - hat_slice * scale_total / count)
    )
    return (
        output,
        grad_tokens,
        grad_memory,
        norm_totals[8],
        norm_totals[9],
        sum_query.T,
        sum_key.T,
        sum_value.T,
        sum_table.T,
        sum_scale,
        sum_output,
        norm_totals[0],
        norm_totals[1],
        norm_totals[2],
        norm_totals[3],
        scale_total,
        shift_total,
        sum_cquery.T,
        sum_ckey.T,
        sum_cvalue.T,
        sum_coutput,
        norm_totals[4],
        norm_totals[5],
        norm_totals[6],
        norm_totals[7],
        sum_up,
        sum_mid_gain,
        sum_mid_bias,
        sum_down,
    )


def solution(mesh):
    in_specs = (
        P("mp", "batch", None),
        P("batch", None),
        P(),
        P("batch", None, None),
        P("batch", None),
        P("mp", "batch", None),
        P(),
        P(),
        P(None, "mp"),
        P(None, "mp"),
        P(None, "mp"),
        P(None, "mp"),
        P("mp"),
        P("mp", None),
        P(),
        P(),
        P(),
        P(),
        P(),
        P(),
        P(None, "mp"),
        P(None, "mp"),
        P(None, "mp"),
        P("mp", None),
        P(),
        P(),
        P(),
        P(),
        P(None, "mp"),
        P("mp"),
        P("mp"),
        P("mp", None),
    )
    out_specs = (
        P("mp", "batch", None),
        P("mp", "batch", None),
        P("batch", None, "mp"),
        P(),
        P(),
        P(None, "mp"),
        P(None, "mp"),
        P(None, "mp"),
        P(None, "mp"),
        P("mp"),
        P("mp", None),
        P(),
        P(),
        P(),
        P(),
        P("mp"),
        P("mp"),
        P(None, "mp"),
        P(None, "mp"),
        P(None, "mp"),
        P("mp", None),
        P(),
        P(),
        P(),
        P(),
        P(None, "mp"),
        P("mp"),
        P("mp"),
        P("mp", None),
    )
    return jax.shard_map(
        on_device, mesh=mesh, in_specs=in_specs, out_specs=out_specs, check_vma=False
    )
```

```python
import functools

import jax
import jax.numpy as jnp
from jax import lax
from jax.experimental import pallas as pl
from jax.experimental.pallas import tpu as pltpu
from jax.sharding import PartitionSpec as P

HEAD_DIM = 64
EPSILON = 1e-05
MASKED = -1e30
LANES = 128
BF = jnp.bfloat16
F32 = jnp.float32
SCALE = HEAD_DIM ** (-0.5)
VMEM_LIMIT = 18 * 1024 * 1024
LATE_LIMIT = 58 * 1024 * 1024


def contract(left, right, left_dim, right_dim, precision=None):
    return lax.dot_general(
        left,
        right,
        (((left_dim,), (right_dim,)), ((), ())),
        precision=precision,
        preferred_element_type=F32,
    )


def kernel_params(late=()):
    return pltpu.CompilerParams(vmem_limit_bytes=LATE_LIMIT if late else VMEM_LIMIT)


class Late:
    def __init__(self, source, slot, sem):
        self.slot, self.copy = slot, pltpu.make_async_copy(source, slot, sem)
        self.shape, self.dtype = slot.shape, slot.dtype
        self.copy.start()

    def ready(self):
        if self.copy is not None:
            self.copy.wait()
            self.copy = None

    def __getitem__(self, index):
        self.ready()
        return self.slot[index]


def ready(*refs):
    for ref in refs:
        if isinstance(ref, Late):
            ref.ready()


def with_late(kernel, inputs, late):
    def wrapped(*refs):
        body = list(refs[: -1 - len(late)])
        slots, sems = refs[-1 - len(late) : -1], refs[-1]
        for place, (index, slot) in enumerate(zip(late, slots)):
            body[index] = Late(refs[index], slot, sems.at[place])
        kernel(*body)
        ready(*body[:inputs])

    return wrapped


def choice_of(ids, buckets):
    places = lax.broadcasted_iota(jnp.int32, (buckets, ids.shape[1]), 0)
    return jnp.where(places == ids, 1.0, 0.0).astype(F32)


def bias_kernel(ids_ref, table_ref, ext_ref):
    heads, width = 2 * ext_ref.shape[0], ext_ref.shape[2]
    choose = choice_of(ids_ref[...], table_ref.shape[1])
    by_offset = contract(table_ref[...], choose, 1, 0, lax.Precision.HIGHEST)
    sub = lax.broadcasted_iota(jnp.int32, (8, width), 0)
    for head in range(heads):
        rolled = jnp.broadcast_to(by_offset[head : head + 1, :], (8, width))
        for bit in (1, 2, 4):
            rolled = jnp.where((sub & bit) > 0, pltpu.roll(rolled, bit, 1), rolled)
        for group in range(LANES // 8):
            start = (head % 2) * LANES + group * 8
            moved = rolled if group == 0 else pltpu.roll(rolled, group * 8, 1)
            ext_ref[head // 2, start : start + 8, :] = moved


def halves(block, low):
    zero = jnp.zeros_like(block)
    return jnp.concatenate([jnp.where(low, block, zero), jnp.where(low, zero, block)], 0)


def merge(block, low):
    rows = block.shape[0] // 2
    return jnp.where(low, block[:rows], block[rows:])


def pair_columns(pair, base=0):
    return pl.ds(pl.multiple_of(base + pair * LANES, LANES), LANES)


def penalty_of(rows, first_row, count, seg_col, seg_row):
    i = lax.broadcasted_iota(jnp.int32, (rows, count), 0) + first_row
    j = lax.broadcasted_iota(jnp.int32, (rows, count), 1)
    one = jnp.where((j <= i) & (seg_col == seg_row), 0.0, MASKED).astype(F32)
    return jnp.concatenate([one, one], 0)


def ext_block(ext_ref, pair, rows, shift, count):
    if rows == LANES:
        return ext_ref[pair, :, shift : shift + count]
    return jnp.concatenate(
        [
            ext_ref[pair, 0:rows, shift : shift + count],
            ext_ref[pair, LANES : LANES + rows, shift : shift + count],
        ],
        0,
    )


def self_forward_kernel(qkv_ref, ext_ref, seg_col_ref, seg_row_ref, scale_ref, out_ref, stats_ref):
    length, width = out_ref.shape
    pairs = width // LANES
    blocks = -(-length // LANES)
    lane = lax.broadcasted_iota(jnp.int32, (1, LANES), 1)
    low = lane < HEAD_DIM
    stats_ref[...] = jnp.zeros_like(stats_ref)
    ready(qkv_ref, ext_ref)
    for block in range(blocks):
        start = block * LANES
        rows = min(LANES, length - start)
        count = start + rows
        shift = (blocks - 1 - block) * LANES
        penalty = penalty_of(
            rows, start, count, seg_col_ref[start : start + rows, :], seg_row_ref[:, 0:count]
        )

        def one_pair(pair, carry):
            columns = pair_columns(pair)
            query = halves(qkv_ref[start : start + rows, columns].astype(F32) * SCALE, low).astype(BF)
            key = qkv_ref[0:count, pair_columns(pair, width)]
            value = qkv_ref[0:count, pair_columns(pair, 2 * width)]
            scores = contract(query, key, 1, 1) + (
                ext_block(ext_ref, pair, rows, shift, count) + penalty
            )
            peak = jnp.max(scores, -1, keepdims=True)
            shifted = jnp.exp(scores - peak)
            total = jnp.sum(shifted, -1, keepdims=True)
            weights = (shifted * (1.0 / total)).astype(BF)
            mixed = merge(contract(weights, value, 1, 0), low)
            out_ref[start : start + rows, columns] = (mixed * scale_ref[:, columns]).astype(BF)
            level = peak + jnp.log(total)
            stats_ref[start : start + rows, :] += jnp.where(
                lane == 2 * pair, level[:rows], 0.0
            ) + jnp.where(lane == 2 * pair + 1, level[rows:], 0.0)
            return carry

        lax.fori_loop(0, pairs, one_pair, 0)


def level_of(stats, lane, pair):
    return jnp.concatenate(
        [
            jnp.sum(jnp.where(lane == 2 * pair + side, stats, 0.0), -1, keepdims=True)
            for side in (0, 1)
        ],
        0,
    )


def self_backward_kernel(
    qkv_ref,
    upstream_ref,
    ext_ref,
    seg_col_ref,
    seg_row_ref,
    stats_ref,
    ids_ref,
    grad_ref,
    table_ref,
    head_ref,
    key_sum,
    value_sum,
    offset_sum,
):
    length, width = upstream_ref.shape
    pairs = width // LANES
    blocks = -(-length // LANES)
    lane = lax.broadcasted_iota(jnp.int32, (1, LANES), 1)
    low = lane < HEAD_DIM
    key_sum[...] = jnp.zeros_like(key_sum)
    value_sum[...] = jnp.zeros_like(value_sum)
    offset_sum[...] = jnp.zeros_like(offset_sum)
    ready(qkv_ref, upstream_ref, ext_ref, stats_ref)
    head_ref[...] = jnp.zeros_like(head_ref)
    for block in range(blocks):
        start = block * LANES
        rows = min(LANES, length - start)
        count = start + rows
        shift = (blocks - 1 - block) * LANES
        penalty = penalty_of(
            rows, start, count, seg_col_ref[start : start + rows, :], seg_row_ref[:, 0:count]
        )

        def one_pair(pair, carry):
            columns = pair_columns(pair)
            query = halves(qkv_ref[start : start + rows, columns].astype(F32) * SCALE, low).astype(BF)
            key = qkv_ref[0:count, pair_columns(pair, width)]
            value = qkv_ref[0:count, pair_columns(pair, 2 * width)]
            upstream = halves(upstream_ref[start : start + rows, columns].astype(F32), low).astype(BF)
            level = level_of(stats_ref[start : start + rows, :], lane, pair)
            scores = contract(query, key, 1, 1) + (
                ext_block(ext_ref, pair, rows, shift, count) + penalty
            )
            probs = jnp.exp(scores - level)
            grad_probs = contract(upstream, value, 1, 1)
            inner = jnp.sum(probs * grad_probs, -1, keepdims=True)
            grad_scores = (probs * (grad_probs - inner)).astype(BF)
            weights = probs.astype(BF)
            grad_query = merge(contract(grad_scores, key, 1, 0), low) * SCALE
            grad_ref[start : start + rows, columns] = grad_query.astype(BF)
            key_sum[0:count, columns] += contract(grad_scores, query, 0, 0)
            value_sum[0:count, columns] += contract(weights, upstream, 0, 0)
            wide = grad_scores.astype(F32)
            if rows == LANES:
                offset_sum[pair, :, shift : shift + count] += wide
            else:
                offset_sum[pair, 0:rows, shift : shift + count] += wide[:rows]
                offset_sum[pair, LANES : LANES + rows, shift : shift + count] += wide[rows:]
            for side in (0, 1):
                part = jnp.sum(inner[side * rows : (side + 1) * rows], 0, keepdims=True)
                head_ref[pl.ds(2 * pair + side, 1), :] += jnp.broadcast_to(part, (1, LANES))
            return carry

        lax.fori_loop(0, pairs, one_pair, 0)
    grad_ref[:, width : 2 * width] = key_sum[...].astype(BF)
    grad_ref[:, 2 * width : 3 * width] = value_sum[...].astype(BF)
    span = offset_sum.shape[2]
    sub = lax.broadcasted_iota(jnp.int32, (8, span), 0)
    head_places = lax.broadcasted_iota(jnp.int32, (table_ref.shape[0], span), 0)
    by_offset = jnp.zeros((table_ref.shape[0], span), F32)
    for head in range(2 * pairs):
        total = None
        for group in range(LANES // 8):
            first = (head % 2) * LANES + group * 8
            piece = offset_sum[head // 2, first : first + 8, :]
            moved = piece if group == 0 else pltpu.roll(piece, span - group * 8, 1)
            total = moved if total is None else total + moved
        for bit in (1, 2, 4):
            total = jnp.where((sub & bit) > 0, pltpu.roll(total, span - bit, 1), total)
        line = jnp.sum(total, 0, keepdims=True)
        by_offset = by_offset + jnp.where(head_places == head, line, 0.0)
    choose = choice_of(ids_ref[...], table_ref.shape[1])
    table_ref[...] = contract(by_offset, choose, 1, 1, lax.Precision.HIGHEST)


def norm_parts(values):
    center = values - jnp.mean(values, -1, keepdims=True)
    factor = lax.rsqrt(jnp.mean(center * center, -1, keepdims=True) + EPSILON)
    return center * factor, factor


def norm_back(values, gain, upstream):
    hat, factor = norm_parts(values)
    leaned = upstream * gain
    grad = factor * (
        leaned
        - jnp.mean(leaned, -1, keepdims=True)
        - hat * jnp.mean(leaned * hat, -1, keepdims=True)
    )
    return grad, jnp.sum(upstream * hat, 0), jnp.sum(upstream, 0)


def kv_blocks(key_ref, value_ref, near_ref):
    step = key_ref.shape[0]
    return jnp.concatenate(
        [key_ref[...], near_ref[3 * step : 4 * step, :], value_ref[...], near_ref[4 * step : 5 * step, :]],
        0,
    )


def four_of(own_ref, near_ref, far_ref, across_ref, index):
    step = own_ref.shape[0]
    rows = slice(index * step, (index + 1) * step)
    return jnp.concatenate([own_ref[...], near_ref[rows, :], far_ref[rows, :], across_ref[rows, :]], 0)


def pack_kernel(*refs):
    *blocks, first_ref, trio_ref, sems = refs
    targets = [first_ref] * 5 + [trio_ref] * 3
    copies = []
    for index, (block, target) in enumerate(zip(blocks, targets)):
        start = block.shape[0] * (index % 5)
        copies.append(
            pltpu.make_async_copy(
                block, target.at[start : start + block.shape[0], :], sems.at[index]
            )
        )
    for copy in copies:
        copy.start()
    for copy in copies:
        copy.wait()


def project_kernel(tokens_ref, gains_ref, q0, k0, v0, near_ref, self_in_ref, qkv_ref, weight_ref):
    step = q0.shape[0]
    for index, own in enumerate((q0, k0, v0)):
        weight_ref[2 * index * step : (2 * index + 1) * step, :] = own[...]
        weight_ref[(2 * index + 1) * step : (2 * index + 2) * step, :] = near_ref[
            index * step : (index + 1) * step, :
        ]
    hat, _ = norm_parts(tokens_ref[...].astype(F32))
    self_in = (hat * gains_ref[10:11, :] + gains_ref[11:12, :]).astype(BF)
    self_in_ref[...] = self_in
    qkv_ref[...] = contract(self_in, weight_ref[...], 1, 1).astype(BF)


def memory_kernel(gathered_ref, k0, v0, near_ref, gains_ref, normed_ref, kv_ref, stats_ref, *, count):
    batch, rows = gathered_ref.shape[0], gathered_ref.shape[1] - 16
    sums = None
    for index in range(batch):
        piece = gathered_ref[index, rows : rows + 16, :].astype(F32)
        sums = piece if sums is None else sums + piece
    total = jnp.sum(sums[0:3], 0, keepdims=True) / count
    square = jnp.sum(sums[3:6], 0, keepdims=True) / count
    factor = lax.rsqrt(square - total * total + EPSILON)
    stats_ref[0:1, :] = total
    stats_ref[1:2, :] = factor
    for index in range(batch):
        hat = (gathered_ref[index, 0:rows, :].astype(F32) - total) * factor
        normed_ref[index * rows : (index + 1) * rows, :] = (
            hat * gains_ref[8:9, :] + gains_ref[9:10, :]
        ).astype(BF)
    kv_ref[...] = contract(normed_ref[...], kv_blocks(k0, v0, near_ref), 1, 1).astype(BF)


def mid_forward_kernel(
    keep_ref,
    far_ref,
    tokens_ref,
    o0,
    q0,
    c0,
    near_ref,
    far_trio_ref,
    across_ref,
    kv_ref,
    far_kv_ref,
    valid_ref,
    gains_ref,
    attn_ref,
    first_ref,
    cross_in_ref,
    query_ref,
    mixed_ref,
    cross_attn_ref,
    second_ref,
    ffn_ref,
    stats_ref,
):
    def gain(index):
        return gains_ref[index : index + 1, :]

    half_lanes = keep_ref.shape[1]
    trio = (near_ref, far_trio_ref, across_ref)
    output_all = four_of(o0, *trio, 0)
    attn = contract(keep_ref[...], output_all[:half_lanes], 1, 0) + contract(
        far_ref[...], output_all[half_lanes:], 1, 0
    )
    attn_ref[...] = attn
    first = tokens_ref[...].astype(F32) + norm_parts(attn)[0] * gain(0) + gain(1)
    first_ref[...] = first
    cross_in = (norm_parts(first)[0] * gain(2) + gain(3)).astype(BF)
    cross_in_ref[...] = cross_in
    query_ref[...] = contract(cross_in, four_of(q0, *trio, 1), 1, 1).astype(BF)
    lane = lax.broadcasted_iota(jnp.int32, (1, LANES), 1)
    low = lane < HEAD_DIM
    penalty = jnp.where(valid_ref[...] > 0, 0.0, MASKED).astype(F32)
    stats_ref[...] = jnp.zeros_like(stats_ref)
    ready(kv_ref, far_kv_ref)

    def one_pair(pair, carry):
        for far, source in enumerate((kv_ref, far_kv_ref)):
            columns = pair_columns(pair, far * half_lanes)
            number = pair + far * (half_lanes // LANES)
            query = query_ref[:, columns].astype(F32) * SCALE
            key = source[:, pair_columns(pair)]
            value = source[:, pair_columns(pair, half_lanes)]
            mixed = None
            for side in (0, 1):
                mine = low if side == 0 else jnp.logical_not(low)
                scores = contract(jnp.where(mine, query, 0.0).astype(BF), key, 1, 1) + penalty
                peak = jnp.max(scores, -1, keepdims=True)
                shifted = jnp.exp(scores - peak)
                total = jnp.sum(shifted, -1, keepdims=True)
                weights = (shifted * (1.0 / total)).astype(BF)
                part = contract(weights, value, 1, 0)
                mixed = part if mixed is None else jnp.where(low, mixed, part)
                stats_ref[...] += jnp.where(lane == 2 * number + side, peak + jnp.log(total), 0.0)
            mixed_ref[:, columns] = mixed.astype(BF)
        return carry

    lax.fori_loop(0, half_lanes // LANES, one_pair, 0)
    cross_attn = contract(mixed_ref[...], four_of(c0, *trio, 2), 1, 0)
    cross_attn_ref[...] = cross_attn
    second = first_ref[...] + norm_parts(cross_attn)[0] * gain(4) + gain(5)
    second_ref[...] = second
    ffn_ref[...] = (norm_parts(second)[0] * gain(6) + gain(7)).astype(BF)


def put_blocks(keep_ref, give_ref, place, step, grads):
    block = grads.astype(BF)
    for index in range(block.shape[0] // (2 * step)):
        rows = slice((place + index) * step, (place + index + 1) * step)
        keep_ref[rows, :] = block[2 * index * step : (2 * index + 1) * step]
        give_ref[rows, :] = block[(2 * index + 1) * step : (2 * index + 2) * step]


def mid_backward_kernel(
    back_ref,
    came_ref,
    upstream_ref,
    second_ref,
    cross_attn_ref,
    first_ref,
    attn_ref,
    query_ref,
    stats_ref,
    o0,
    q0,
    c0,
    near_ref,
    far_trio_ref,
    across_ref,
    kv_ref,
    far_kv_ref,
    valid_ref,
    gains_ref,
    scale_ref,
    keep_scaled_ref,
    far_scaled_ref,
    cross_mixed_ref,
    cross_in_ref,
    grad_first_ref,
    keep_ref,
    far_ref,
    grad_kv_ref,
    far_grad_kv_ref,
    norms_ref,
    keep_weights_ref,
    give_weights_ref,
    mixed_ref,
    grad_query_ref,
):
    def gain(index):
        return gains_ref[index : index + 1, :]

    half_lanes = keep_ref.shape[1]
    trio = (near_ref, far_trio_ref, across_ref)
    ffn_grad = back_ref[...] + came_ref[...].astype(F32)
    grad, norms_ref[6, :], norms_ref[7, :] = norm_back(second_ref[...], gain(6), ffn_grad)
    grad_second = upstream_ref[...].astype(F32) + grad
    grad_first_ref[...] = grad_second
    grad, norms_ref[4, :], norms_ref[5, :] = norm_back(cross_attn_ref[...], gain(4), grad_second)
    grad_cattn = grad.astype(BF)
    mixed_ref[...] = contract(grad_cattn, four_of(c0, *trio, 2), 1, 1).astype(BF)
    lane = lax.broadcasted_iota(jnp.int32, (1, LANES), 1)
    low = lane < HEAD_DIM
    penalty = jnp.where(valid_ref[...] > 0, 0.0, MASKED).astype(F32)
    ready(query_ref, stats_ref, kv_ref, far_kv_ref)

    def one_pair(pair, carry):
        for far, source in enumerate((kv_ref, far_kv_ref)):
            columns = pair_columns(pair, far * half_lanes)
            number = pair + far * (half_lanes // LANES)
            query = query_ref[:, columns].astype(F32) * SCALE
            upstream = mixed_ref[:, columns].astype(F32)
            key = source[:, pair_columns(pair)]
            value = source[:, pair_columns(pair, half_lanes)]
            grad_query = grad_key = grad_value = None
            for side in (0, 1):
                mine = low if side == 0 else jnp.logical_not(low)
                my_query = jnp.where(mine, query, 0.0).astype(BF)
                my_upstream = jnp.where(mine, upstream, 0.0).astype(BF)
                level = jnp.sum(
                    jnp.where(lane == 2 * number + side, stats_ref[...], 0.0), -1, keepdims=True
                )
                probs = jnp.exp(contract(my_query, key, 1, 1) + penalty - level)
                grad_probs = contract(my_upstream, value, 1, 1)
                inner = jnp.sum(probs * grad_probs, -1, keepdims=True)
                grad_scores = (probs * (grad_probs - inner)).astype(BF)
                part_query = contract(grad_scores, key, 1, 0)
                part_key = contract(grad_scores, my_query, 0, 0)
                part_value = contract(probs.astype(BF), my_upstream, 0, 0)
                if side == 0:
                    grad_query, grad_key, grad_value = part_query, part_key, part_value
                else:
                    grad_query = jnp.where(low, grad_query, part_query)
                    grad_key, grad_value = grad_key + part_key, grad_value + part_value
            grad_query_ref[:, columns] = (grad_query * SCALE).astype(BF)
            target = far_grad_kv_ref if far else grad_kv_ref
            target[:, pair_columns(pair)] = grad_key.astype(target.dtype)
            target[:, pair_columns(pair, half_lanes)] = grad_value.astype(target.dtype)
        return carry

    lax.fori_loop(0, half_lanes // LANES, one_pair, 0)
    grad_in = contract(grad_query_ref[...], four_of(q0, *trio, 1), 1, 0)
    grad, norms_ref[2, :], norms_ref[3, :] = norm_back(first_ref[...], gain(2), grad_in)
    grad_first = grad_first_ref[...] + grad
    grad_first_ref[...] = grad_first
    grad, norms_ref[0, :], norms_ref[1, :] = norm_back(attn_ref[...], gain(0), grad_first)
    grad_attn = grad.astype(BF)
    grad_mixed = (contract(grad_attn, four_of(o0, *trio, 0), 1, 1) * scale_ref[...]).astype(BF)
    keep_ref[...] = grad_mixed[:, :half_lanes]
    far_ref[...] = grad_mixed[:, half_lanes:]
    step = half_lanes // 2
    put = functools.partial(put_blocks, keep_weights_ref, give_weights_ref)
    low_lanes, high_lanes = slice(0, half_lanes), slice(half_lanes, 2 * half_lanes)
    put(0, step, contract(keep_scaled_ref[...], grad_attn, 0, 0))
    put(1, step, contract(cross_mixed_ref[:, low_lanes], grad_cattn, 0, 0))
    put(2, step, contract(grad_query_ref[:, low_lanes], cross_in_ref[...], 0, 0))
    put(3, step, contract(far_scaled_ref[...], grad_attn, 0, 0))
    put(4, step, contract(cross_mixed_ref[:, high_lanes], grad_cattn, 0, 0))
    put(5, step, contract(grad_query_ref[:, high_lanes], cross_in_ref[...], 0, 0))


def ffn_weights_kernel(
    ffn_own_ref,
    ffn_far_ref,
    gate_own_ref,
    gate_far_ref,
    middle_own_ref,
    middle_far_ref,
    upstream_own_ref,
    upstream_far_ref,
    up_ref,
    down_ref,
    keep_ref,
    give_ref,
    back_ref,
    out_own_ref,
    out_far_ref,
):
    units = keep_ref.shape[0] // 2
    for target, lanes in ((give_ref, slice(units, 2 * units)), (keep_ref, slice(0, units))):
        target[0:units, :] = (
            contract(ffn_own_ref[...], gate_own_ref[:, lanes], 0, 0)
            + contract(ffn_far_ref[...], gate_far_ref[:, lanes], 0, 0)
        ).astype(BF)
        target[units : 2 * units, :] = (
            contract(middle_own_ref[:, lanes], upstream_own_ref[...], 0, 0)
            + contract(middle_far_ref[:, lanes], upstream_far_ref[...], 0, 0)
        ).astype(BF)
    back_ref[...] = contract(gate_own_ref[...], up_ref[...], 1, 1)
    out_far_ref[...] = contract(middle_far_ref[...], down_ref[...], 1, 0).astype(BF)
    out_own_ref[...] = contract(middle_own_ref[...], down_ref[...], 1, 0)


def memory_weights_kernel(
    grad_kv_ref, came_kv_ref, normed_ref, k0, v0, near_ref, keep_ref, give_ref, normed_grad_ref
):
    step = k0.shape[0]
    grad_kv = (grad_kv_ref[...] + came_kv_ref[...].astype(F32)).astype(BF)
    put_blocks(keep_ref, give_ref, 0, step, contract(grad_kv, normed_ref[...], 0, 0))
    normed_grad_ref[...] = contract(grad_kv, kv_blocks(k0, v0, near_ref), 1, 0)


def self_weights_kernel(grad_qkv_ref, self_in_ref, keep_ref, give_ref):
    step = keep_ref.shape[0] // 3
    for index in range(3):
        lanes = slice(2 * index * step, 2 * (index + 1) * step)
        put_blocks(
            keep_ref, give_ref, index, step, contract(grad_qkv_ref[:, lanes], self_in_ref[...], 0, 0)
        )


def flip_over(axis, bit):
    def send(block):
        size = lax.axis_size(axis)
        return lax.ppermute(block, axis, [(i, i ^ bit) for i in range(size)])

    return send


def mate(block):
    return flip_over("mp", 1)(block)


def peer(block):
    return flip_over("mp", 2)(block)


def cut(block, index, size, axis=0):
    return lax.dynamic_slice_in_dim(block, index * size, size, axis)


def dot_right(left, right):
    return contract(left, right, 1, 1)


def dot_left(left, right):
    return contract(left, right, 0, 0)


def dot(left, right):
    return contract(left, right, 1, 0)


def batch_bits():
    size = lax.axis_size("batch")
    bits = []
    while (1 << len(bits)) < size:
        bits.append(1 << len(bits))
    return bits


def pack_small(parts):
    flat = jnp.concatenate([part.reshape(-1) for part in parts])
    size = -(-flat.shape[0] // (8 * LANES)) * 8 * LANES
    return jnp.pad(flat, (0, size - flat.shape[0])).reshape(-1, LANES)


def unpack_small(packed, shapes):
    flat = packed.reshape(-1)
    parts, start = [], 0
    for shape in shapes:
        size = 1
        for extent in shape:
            size *= extent
        parts.append(flat[start : start + size].reshape(shape))
        start += size
    return parts


def shape_of(shape, dtype):
    return jax.ShapeDtypeStruct(shape, dtype)


def pieces_of(values):
    high = lax.reduce_precision(values, 8, 7)
    middle = lax.reduce_precision(values - high, 8, 7)
    return [high.astype(BF), middle.astype(BF), (values - high - middle).astype(BF)]


def tie(*arrays):
    return lax.optimization_barrier(arrays)


def two_of(index, own, other):
    return jnp.where(index == 0, own, other), jnp.where(index == 0, other, own)


def in_order(index, own, other):
    return jnp.concatenate(two_of(index, own, other), 0)


class Summing:
    def __init__(self, blocks, bits):
        self.blocks = blocks
        self.bits = bits
        self.todo = [("halve", bit) for bit in bits] + [("double", bit) for bit in reversed(bits)]
        self.start = None
        self.size = blocks[0].shape[0]
        self.terms = []
        self.block = None
        self.came = None

    def part(self, start, size):
        total = lax.dynamic_slice_in_dim(self.base, start, size).astype(F32)
        for offset, came in self.terms:
            total = total + lax.dynamic_slice_in_dim(came, start - offset, size).astype(F32)
        return total.astype(BF)

    def prepare(self):
        kind, bit = self.todo.pop(0)
        index = (lax.axis_index("batch") // bit) % 2
        self.kind, self.index, self.bit = kind, index, bit
        if kind == "halve" and self.start is None:
            first, second = self.blocks
            self.base = jnp.where(index == 0, first, second)
            self.give = jnp.where(index == 0, second, first)
            self.start = jnp.int32(0)
        elif kind == "halve":
            self.size = self.size // 2
            self.give = self.part(self.start + (1 - index) * self.size, self.size)
            self.start = self.start + index * self.size
        else:
            if self.block is None:
                self.block = self.part(self.start, self.size)
            self.give = self.block

    def land(self):
        if self.kind == "halve":
            self.terms.append((self.start, self.came))
        elif self.todo:
            self.block = in_order(self.index, self.block, self.came)
        else:
            self.block = two_of(self.index, self.block, self.came)
        self.came = None

    def blocks_of(self, rows):
        whole = jnp.concatenate(self.block, 0)
        return [whole[i : i + rows].astype(F32) for i in range(0, whole.shape[0], rows)]


def advance(flows, *others):
    for flow in flows:
        if flow.came is not None:
            flow.land()
    going = [flow for flow in flows if flow.todo]
    for flow in going:
        flow.prepare()
    ready = tie(*[flow.give for flow in going], *others) if going or others else ()
    for flow, give in zip(going, ready):
        flow.give = give
        flow.came = flip_over("batch", flow.bit)(give)
    return ready[len(going) :]


def finish(flows):
    while any(flow.came is not None for flow in flows):
        advance(flows)


def cost_of(micros):
    return pl.CostEstimate(flops=0, bytes_accessed=int(micros * 3.0e6), transcendentals=0)


def on_device(
    tokens,
    segment_ids,
    bucket_ids,
    memory,
    memory_mask,
    cotangent,
    self_gain,
    self_bias,
    query_weight,
    key_weight,
    value_weight,
    rel_table,
    head_scale,
    output_weight,
    after_gain,
    after_bias,
    cross_gain,
    cross_bias,
    batch_gain,
    batch_bias,
    cross_query,
    cross_key,
    cross_value,
    cross_output,
    crossout_gain,
    crossout_bias,
    ffn_gain,
    ffn_bias,
    up_weight,
    middle_gain,
    middle_bias,
    down_weight,
):
    place = lax.axis_index("mp")
    core, side = place % 2, place // 2
    batch = lax.axis_size("batch")
    bits = batch_bits()
    quarter, _, width = tokens.shape
    length = 4 * quarter
    half = 2 * quarter
    heads = 2 * rel_table.shape[1]
    lanes = heads * HEAD_DIM
    step = lanes // 2
    units = up_weight.shape[1]
    all_hidden = 4 * units
    mem_rows = memory.shape[0]
    positions = mem_rows * batch

    def call(kernel, shapes, micros, late=(), scratch=(), name=None):
        def run(*args):
            taken = list(scratch)
            specs = [pl.BlockSpec(memory_space=pltpu.VMEM)] * len(args)
            wrapped = kernel
            if late:
                for index in late:
                    specs[index] = pl.BlockSpec(memory_space=pltpu.HBM)
                    taken.append(pltpu.VMEM(args[index].shape, args[index].dtype))
                taken.append(pltpu.SemaphoreType.DMA((len(late),)))
                wrapped = with_late(kernel, len(args), late)
            return pl.pallas_call(
                wrapped,
                out_shape=shapes,
                in_specs=specs,
                scratch_shapes=taken,
                compiler_params=kernel_params(late),
                cost_estimate=cost_of(micros),
                name=name,
            )(*args)

        return run

    def rows_of(array):
        return tuple(
            lax.dynamic_index_in_dim(array, index, 1, keepdims=False) for index in (core, 1 - core)
        )

    keep_tokens, give_tokens = rows_of(tokens)
    keep_tokens, give_tokens, memory = tie(keep_tokens, give_tokens, memory)
    far_keep, far_give = peer(keep_tokens), flip_over("mp", 3)(give_tokens)
    near_tokens = mate(give_tokens)

    query_t, key_t, value_t = query_weight.T, key_weight.T, value_weight.T
    own_trio = [output_weight, cross_query.T, cross_output]
    key_c, value_c = cross_key.T, cross_value.T
    all_blocks = [query_t, key_t, value_t, key_c, value_c, *own_trio]
    anywhere = pl.BlockSpec(memory_space=pl.ANY)
    own_first, trio = pl.pallas_call(
        pack_kernel,
        out_shape=tuple(shape_of((count * step, width), BF) for count in (5, 3)),
        in_specs=[anywhere] * len(all_blocks),
        out_specs=(anywhere,) * 2,
        scratch_shapes=[pltpu.SemaphoreType.DMA((len(all_blocks),))],
        compiler_params=pltpu.CompilerParams(vmem_limit_bytes=1024 * 1024),
        cost_estimate=cost_of(3),
        name="pack",
    )(*all_blocks)
    near_first = mate(own_first)
    far_keep, far_give, trio = tie(far_keep, far_give, trio)
    far_trio = peer(trio)
    near_small = unpack_small(
        mate(pack_small([rel_table.T, head_scale, middle_gain, middle_bias])),
        [(heads // 2, rel_table.shape[0]), (heads // 2,), (units,), (units,)],
    )
    both_scale = jnp.concatenate([head_scale, near_small[1]])
    gain_pair = jnp.concatenate([middle_gain, near_small[2]])
    bias_pair = jnp.concatenate([middle_bias, near_small[3]])
    gains = jnp.stack(
        [
            after_gain,
            after_bias,
            cross_gain,
            cross_bias,
            crossout_gain,
            crossout_bias,
            ffn_gain,
            ffn_bias,
            batch_gain,
            batch_bias,
            self_gain,
            self_bias,
        ]
    )

    blocks = -(-length // LANES)
    span = blocks * LANES
    split = length - 1 - (blocks - 1) * LANES
    ids = jnp.concatenate(
        [
            bucket_ids[split:length],
            jnp.full((span - length,), -1, bucket_ids.dtype),
            bucket_ids[:split],
        ]
    )[None, :]
    table = jnp.concatenate([rel_table.T, near_small[0]], 0)
    table = jnp.pad(table, ((0, -heads % 8), (0, 0)))
    ext = call(bias_kernel, shape_of((heads // 2, 2 * LANES, span), F32), 2, name="bias")(ids, table)

    mem_float = memory.astype(F32)
    sums = [jnp.sum(mem_float, (0, 1)), jnp.sum(mem_float * mem_float, (0, 1))]
    extra = jnp.stack([piece for total in sums for piece in pieces_of(total)])
    extra = jnp.broadcast_to(jnp.pad(extra, ((0, 10), (0, 0)))[None], (batch, 16, width))
    rows_here = memory.reshape(mem_rows, batch, 2, width)
    my_rows = jnp.where(core == 0, rows_here[:, :, 0], rows_here[:, :, 1])
    outgoing = jnp.concatenate([jnp.swapaxes(my_rows, 0, 1), extra], 1)
    gathered = lax.all_to_all(outgoing, "batch", split_axis=0, concat_axis=0, tiled=True)
    count = positions * memory.shape[1]
    normed, own_kv, mem_stats = call(
        functools.partial(memory_kernel, count=count),
        (
            shape_of((positions, width), BF),
            shape_of((positions, width), BF),
            shape_of((2, width), F32),
        ),
        2,
        name="memory",
    )(gathered, key_c, value_c, near_first, gains)
    far_kv = peer(own_kv)

    own_tokens = in_order(core, keep_tokens, near_tokens)
    row_tokens = in_order(side, own_tokens, in_order(core, far_keep, far_give))
    self_in, qkv, qkv_weight = call(
        project_kernel,
        (
            shape_of((length, width), BF),
            shape_of((length, 3 * lanes), BF),
            shape_of((3 * lanes, width), BF),
        ),
        5,
        name="project",
    )(row_tokens, gains, query_t, key_t, value_t, near_first)
    keep_cotangent, give_cotangent = rows_of(cotangent)
    segment = lax.dynamic_index_in_dim(segment_ids, core, 0, keepdims=False)
    seg_col, seg_row = segment[:, None], segment[None, :]
    scale_lanes = jnp.repeat(both_scale, HEAD_DIM)[None, :]
    qkv, own_kv, give_cotangent, up_give, down_give, trio = tie(
        qkv, own_kv, give_cotangent, up_weight, down_weight, trio
    )
    near_trio = mate(trio)
    near_cotangent = mate(give_cotangent)
    scaled, stats = call(
        self_forward_kernel,
        (shape_of((length, lanes), BF), shape_of((length, LANES), F32)),
        16,
        name="self_forward",
    )(qkv, ext, seg_col, seg_row, scale_lanes)
    scaled, far_kv, far_trio, near_cotangent = tie(scaled, far_kv, far_trio, near_cotangent)
    keep_scaled, far_scaled = cut(scaled, side, half), peer(cut(scaled, 1 - side, half))
    across_trio = mate(far_trio)
    own_cotangent = in_order(core, keep_cotangent, near_cotangent)
    up_pair = jnp.concatenate([up_weight, mate(up_give)], 1)
    down_pair = jnp.concatenate([down_weight, mate(down_give)], 0)
    far_scaled, own_cotangent, up_pair, down_pair, across_trio = tie(
        far_scaled, own_cotangent, up_pair, down_pair, across_trio
    )
    far_cotangent = peer(own_cotangent)
    trio_args = [*own_trio, near_trio, far_trio, across_trio]

    valid = lax.dynamic_index_in_dim(memory_mask, core, 0, keepdims=True)
    wide, narrow = shape_of((half, width), F32), shape_of((half, width), BF)
    attn, first, cross_in, cross_queries, cross_mixed, cross_attn, second, ffn_own, cross_stats = call(
        mid_forward_kernel,
        (wide, wide, narrow, narrow, narrow, wide, wide, narrow, shape_of((half, LANES), F32)),
        10,
        name="mid_forward",
    )(keep_scaled, far_scaled, own_tokens, *trio_args, own_kv, far_kv, valid, gains)

    ffn_own, far_cotangent = tie(ffn_own, far_cotangent)
    ffn_far = peer(ffn_own)

    def ffn_start(values, grad_middle):
        gate = dot(values, up_pair)
        active = gate * (0.5 * (1.0 + lax.erf(gate * (0.5**0.5))))
        leaned = grad_middle * gain_pair
        sums = jnp.stack(
            [
                jnp.sum(active, -1),
                jnp.sum(active * active, -1),
                jnp.sum(leaned, -1),
                jnp.sum(leaned * active, -1),
            ]
        )
        return gate, sums

    grad_middle_own = dot_right(own_cotangent, down_pair)
    grad_middle_far = dot_right(far_cotangent, down_pair)
    gate_own, sums_own = ffn_start(ffn_own, grad_middle_own)
    ffn_far, grad_middle_far, gate_own, sums_own = tie(ffn_far, grad_middle_far, gate_own, sums_own)
    gate_far, sums_far = ffn_start(ffn_far, grad_middle_far)
    scale_row = jnp.pad(both_scale, (0, half - heads))[None, :]
    came_sums = peer(jnp.concatenate([sums_far, sums_own, scale_row], 0))
    sums_own = (sums_own + came_sums[:4]) / all_hidden
    sums_far = (sums_far + came_sums[4:8]) / all_hidden
    all_scale = jnp.concatenate([both_scale, came_sums[8, :heads]])

    def ffn_end(gate, grad_middle, sums):
        chance = 0.5 * (1.0 + lax.erf(gate * (0.5**0.5)))
        active = gate * chance
        leaned = grad_middle * gain_pair
        act_mean = sums[0][:, None]
        act_scale = lax.rsqrt(sums[1][:, None] - act_mean * act_mean + EPSILON)
        act_hat = (active - act_mean) * act_scale
        middle = (act_hat * gain_pair + bias_pair).astype(BF)
        leaned_mean = sums[2][:, None]
        leaned_hat = act_scale * (sums[3][:, None] - act_mean * leaned_mean)
        grad_active = act_scale * (leaned - leaned_mean - act_hat * leaned_hat)
        density = jnp.exp(-0.5 * gate * gate) * ((2.0 * jnp.pi) ** -0.5)
        grad_gate = (grad_active * (chance + gate * density)).astype(BF)
        return middle, grad_gate, jnp.sum(grad_middle * act_hat, 0), jnp.sum(grad_middle, 0)

    middle_far, gate_grad_far, mid_gain_far, mid_bias_far = ffn_end(
        gate_far, grad_middle_far, sums_far
    )
    back_far = dot_right(gate_grad_far, up_pair).astype(BF)
    back_far, gate_own, grad_middle_own, sums_own = tie(
        back_far, gate_own, grad_middle_own, sums_own
    )
    back_came = peer(back_far)
    middle_own, gate_grad_own, mid_gain_own, mid_bias_own = ffn_end(
        gate_own, grad_middle_own, sums_own
    )
    grad_mid_gain = mid_gain_own + mid_gain_far
    grad_mid_bias = mid_bias_own + mid_bias_far

    wide, narrow = shape_of((half, width), F32), shape_of((half, width), BF)
    both_grads = shape_of((width + units, width), BF)
    keep_ffn, give_ffn, back_own, out_part, out_far = call(
        ffn_weights_kernel,
        (both_grads, both_grads, wide, wide, narrow),
        0,
        name="ffn_weights",
    )(
        ffn_own,
        ffn_far,
        gate_grad_own,
        gate_grad_far,
        middle_own,
        middle_far,
        own_cotangent,
        far_cotangent,
        up_pair,
        down_pair,
    )
    back_came, back_own, give_ffn, out_far = tie(back_came, back_own, give_ffn, out_far)
    part_ffn = (keep_ffn.astype(F32) + mate(give_ffn).astype(F32)).astype(BF)
    back_came, part_ffn = tie(back_came, part_ffn)
    ffn_chunk = lax.psum_scatter(part_ffn, "batch", scatter_dimension=0, tiled=True)
    turned = bits[1:] + bits[:1]

    six = shape_of((6 * step, width), BF)
    (
        grad_first,
        keep_mixed,
        give_mixed,
        grad_kv,
        give_kv,
        norms,
        keep_cross,
        give_cross,
    ) = call(
        mid_backward_kernel,
        (
            wide,
            shape_of((half, lanes), BF),
            shape_of((half, lanes), BF),
            shape_of((positions, width), F32),
            shape_of((positions, width), BF),
            shape_of((8, width), F32),
            six,
            six,
        ),
        16,
        late=(3, 2, 4, 11, 12, 13, 14, 7, 8, 15, 16, 10, 5, 6, 9, 20, 21, 22, 23),
        scratch=[pltpu.VMEM((half, width), BF), pltpu.VMEM((half, width), BF)],
        name="mid_backward",
    )(
        back_own,
        back_came,
        own_cotangent,
        second,
        cross_attn,
        first,
        attn,
        cross_queries,
        cross_stats,
        *trio_args,
        own_kv,
        far_kv,
        valid,
        gains,
        jnp.repeat(all_scale, HEAD_DIM)[None, :],
        keep_scaled,
        far_scaled,
        cross_mixed,
        cross_in,
    )
    came_mixed = peer(give_mixed)
    near_cross = mate(give_cross)
    near_cross, give_kv = tie(near_cross, give_kv)
    came_kv = peer(give_kv)
    far_cross = (keep_cross[3 * step :].astype(F32) + near_cross[3 * step :].astype(F32)).astype(BF)
    grad_mixed = in_order(side, keep_mixed, came_mixed)
    grad_mixed, far_cross = tie(grad_mixed, far_cross)
    came_cross = peer(far_cross)
    grad_qkv, grad_table, grad_heads = call(
        self_backward_kernel,
        (
            shape_of((length, 3 * lanes), BF),
            shape_of(table.shape, F32),
            shape_of((8, LANES), F32),
        ),
        22,
        scratch=[
            pltpu.VMEM((length, lanes), F32),
            pltpu.VMEM((length, lanes), F32),
            pltpu.VMEM(ext.shape, F32),
        ],
        name="self_backward",
    )(qkv, grad_mixed, ext, seg_col, seg_row, stats, ids)
    grad_qkv, came_kv = tie(grad_qkv, came_kv)
    far_in = dot(cut(grad_qkv, 1 - side, half), qkv_weight).astype(BF)
    came_in = peer(far_in)
    grad_qkv, far_in = tie(grad_qkv, far_in)
    keep_last, give_last = call(
        self_weights_kernel,
        (shape_of((3 * step, width), BF), shape_of((3 * step, width), BF)),
        4,
        name="self_weights",
    )(grad_qkv, self_in)
    near_last = mate(give_last)
    keep_mem, give_mem, normed_grad = call(
        memory_weights_kernel,
        (
            shape_of((2 * step, width), BF),
            shape_of((2 * step, width), BF),
            shape_of((positions, width), F32),
        ),
        2,
        late=(0, 1, 2, 3, 4, 5),
        name="memory_weights",
    )(grad_kv, came_kv, normed, key_c, value_c, near_first)
    near_mem = mate(give_mem)

    def add_up(*terms):
        total = terms[0].astype(F32)
        for term in terms[1:]:
            total = total + term.astype(F32)
        return total.astype(BF)

    part_last = add_up(keep_last, near_last)
    some = 3 * step // 2
    last_sum = Summing((part_last[:some], part_last[some:]), turned)
    part_cross = jnp.concatenate(
        [add_up(keep_cross[: 3 * step], near_cross[: 3 * step], came_cross), add_up(keep_mem, near_mem)],
        0,
    )
    some = 5 * step // 2
    cross_sum = Summing((part_cross[:some], part_cross[some:]), bits)
    last_flows = [last_sum, cross_sum]
    half_cols = width // 2
    give_normed = cut(normed_grad, 1 - side, half_cols, 1).astype(BF)
    grad_qkv, give_normed, ffn_chunk = advance(last_flows, grad_qkv, give_normed, ffn_chunk)
    came_half = peer(give_normed)
    sum_ffn = lax.all_gather(ffn_chunk, "batch", axis=0, tiled=True)
    def by_quarter(own):
        keep = cut(own, core, quarter)
        came = mate(cut(own, 1 - core, quarter))
        return jnp.stack([jnp.where(core == 0, keep, came), jnp.where(core == 0, came, keep)], 1)

    channels = width // 4
    half_normed = cut(normed_grad, side, half_cols, 1) + came_half.astype(F32)
    keep_normed = cut(half_normed, core, channels, 1)
    give_part = cut(half_normed, 1 - core, channels, 1).astype(BF)
    back_in = dot(cut(grad_qkv, side, half), qkv_weight)
    back_in, came_in, give_part, out_far = advance(last_flows, back_in, came_in, give_part, out_far)
    came_normed = mate(give_part).astype(F32)
    out_came = peer(out_far)
    grad_self_in = back_in + came_in.astype(F32)
    back_tokens, grad_self_gain, grad_self_bias = norm_back(
        own_tokens.astype(F32), self_gain, grad_self_in
    )
    own_grad_tokens = grad_first + back_tokens
    both_normed = jnp.stack(
        [
            jnp.where(core == 0, keep_normed, came_normed),
            jnp.where(core == 0, came_normed, keep_normed),
        ],
        1,
    ).astype(BF)

    own_heads = heads // 2

    def small_of(index):
        mine = slice(index * own_heads, (index + 1) * own_heads)
        some = slice(index * units, (index + 1) * units)
        return pack_small(
            [
                grad_table[mine],
                grad_heads[mine, 0] / both_scale[mine],
                grad_mid_gain[some],
                grad_mid_bias[some],
            ]
        )

    shared = pack_small([norms, grad_self_gain, grad_self_bias])
    keep_small = small_of(0)
    here = shared.shape[0]
    give_small = jnp.concatenate([shared, small_of(1)], 0)
    own_grad_tokens, both_normed, give_small, out_came = advance(
        last_flows, own_grad_tokens, both_normed, give_small, out_came
    )
    came_small = mate(give_small)
    grad_normed = lax.all_to_all(
        both_normed, "batch", split_axis=0, concat_axis=1, tiled=True
    ).astype(F32)
    grad_tokens = by_quarter(own_grad_tokens)
    out_own = (second + out_part + out_came.astype(F32)).astype(BF)
    output = by_quarter(out_own)
    shared = shared + came_small[:here]
    shared, grad_normed, grad_tokens, output = advance(
        last_flows, shared, grad_normed, grad_tokens, output
    )
    came_shared = peer(shared)
    mean_slice = cut(mem_stats[0], place, channels)
    gain_slice = cut(batch_gain, place, channels)
    scale_slice = cut(mem_stats[1], place, channels)
    hat_slice = (cut(memory, place, channels, 2).astype(F32) - mean_slice) * scale_slice
    shift_term = jnp.sum(grad_normed, (0, 1))
    scale_term = jnp.sum(grad_normed * hat_slice, (0, 1))
    mem_small = pack_small([shift_term, scale_term])
    total = jnp.concatenate([shared + came_shared, keep_small + came_small[here:], mem_small], 0)
    sum_up, sum_down = sum_ffn[:width].astype(F32), sum_ffn[width:].astype(F32)
    for place, bit in enumerate(bits):
        if place == 1:
            total, sum_up, sum_down = advance(last_flows, total, sum_up, sum_down)
        else:
            (total,) = advance(last_flows, total)
        total = total + flip_over("batch", bit)(total)
    finish(last_flows)
    sum_output, sum_coutput, sum_cquery, sum_ckey, sum_cvalue = cross_sum.blocks_of(step)
    sum_query, sum_key, sum_value = last_sum.blocks_of(step)
    there = here + keep_small.shape[0]
    norm_totals = unpack_small(total[:here], [(width,)] * 10)
    sum_table, sum_scale, sum_mid_gain, sum_mid_bias = unpack_small(
        total[here:there], [(own_heads, table.shape[1]), (own_heads,), (units,), (units,)]
    )
    shift_total, scale_total = unpack_small(total[there:], [(channels,), (channels,)])
    grad_memory = (
        gain_slice
        * scale_slice
        * (grad_normed - shift_total / count - hat_slice * scale_total / count)
    )
    return (
        output,
        grad_tokens,
        grad_memory,
        norm_totals[8],
        norm_totals[9],
        sum_query.T,
        sum_key.T,
        sum_value.T,
        sum_table.T,
        sum_scale,
        sum_output,
        norm_totals[0],
        norm_totals[1],
        norm_totals[2],
        norm_totals[3],
        scale_total,
        shift_total,
        sum_cquery.T,
        sum_ckey.T,
        sum_cvalue.T,
        sum_coutput,
        norm_totals[4],
        norm_totals[5],
        norm_totals[6],
        norm_totals[7],
        sum_up,
        sum_mid_gain,
        sum_mid_bias,
        sum_down,
    )


def solution(mesh):
    in_specs = (
        P("mp", "batch", None),
        P("batch", None),
        P(),
        P("batch", None, None),
        P("batch", None),
        P("mp", "batch", None),
        P(),
        P(),
        P(None, "mp"),
        P(None, "mp"),
        P(None, "mp"),
        P(None, "mp"),
        P("mp"),
        P("mp", None),
        P(),
        P(),
        P(),
        P(),
        P(),
        P(),
        P(None, "mp"),
        P(None, "mp"),
        P(None, "mp"),
        P("mp", None),
        P(),
        P(),
        P(),
        P(),
        P(None, "mp"),
        P("mp"),
        P("mp"),
        P("mp", None),
    )
    out_specs = (
        P("mp", "batch", None),
        P("mp", "batch", None),
        P("batch", None, "mp"),
        P(),
        P(),
        P(None, "mp"),
        P(None, "mp"),
        P(None, "mp"),
        P(None, "mp"),
        P("mp"),
        P("mp", None),
        P(),
        P(),
        P(),
        P(),
        P("mp"),
        P("mp"),
        P(None, "mp"),
        P(None, "mp"),
        P(None, "mp"),
        P("mp", None),
        P(),
        P(),
        P(),
        P(),
        P(None, "mp"),
        P("mp"),
        P("mp"),
        P("mp", None),
    )
    return jax.shard_map(
        on_device, mesh=mesh, in_specs=in_specs, out_specs=out_specs, check_vma=False
    )
```

```python
import functools

import jax
import jax.numpy as jnp
from jax import lax
from jax.experimental import pallas as pl
from jax.experimental.pallas import tpu as pltpu
from jax.sharding import PartitionSpec as P

HEAD_DIM = 64
EPSILON = 1e-05
MASKED = -1e30
LANES = 128
BF = jnp.bfloat16
F32 = jnp.float32
SCALE = HEAD_DIM ** (-0.5)
VMEM_LIMIT = 18 * 1024 * 1024
LATE_LIMIT = 58 * 1024 * 1024


def contract(left, right, left_dim, right_dim, precision=None):
    return lax.dot_general(
        left,
        right,
        (((left_dim,), (right_dim,)), ((), ())),
        precision=precision,
        preferred_element_type=F32,
    )


def kernel_params(late=()):
    return pltpu.CompilerParams(vmem_limit_bytes=LATE_LIMIT if late else VMEM_LIMIT)


class Late:
    def __init__(self, source, slot, sem):
        self.slot, self.copy = slot, pltpu.make_async_copy(source, slot, sem)
        self.shape, self.dtype = slot.shape, slot.dtype
        self.copy.start()

    def ready(self):
        if self.copy is not None:
            self.copy.wait()
            self.copy = None

    def __getitem__(self, index):
        self.ready()
        return self.slot[index]


def ready(*refs):
    for ref in refs:
        if isinstance(ref, Late):
            ref.ready()


def with_late(kernel, inputs, late):
    def wrapped(*refs):
        body = list(refs[: -1 - len(late)])
        slots, sems = refs[-1 - len(late) : -1], refs[-1]
        for place, (index, slot) in enumerate(zip(late, slots)):
            body[index] = Late(refs[index], slot, sems.at[place])
        kernel(*body)
        ready(*body[:inputs])

    return wrapped


def choice_of(ids, buckets):
    places = lax.broadcasted_iota(jnp.int32, (buckets, ids.shape[1]), 0)
    return jnp.where(places == ids, 1.0, 0.0).astype(F32)


def bias_kernel(ids_ref, table_ref, ext_ref):
    heads, width = 2 * ext_ref.shape[0], ext_ref.shape[2]
    choose = choice_of(ids_ref[...], table_ref.shape[1])
    by_offset = contract(table_ref[...], choose, 1, 0, lax.Precision.HIGHEST)
    sub = lax.broadcasted_iota(jnp.int32, (8, width), 0)
    for head in range(heads):
        rolled = jnp.broadcast_to(by_offset[head : head + 1, :], (8, width))
        for bit in (1, 2, 4):
            rolled = jnp.where((sub & bit) > 0, pltpu.roll(rolled, bit, 1), rolled)
        for group in range(LANES // 8):
            start = (head % 2) * LANES + group * 8
            moved = rolled if group == 0 else pltpu.roll(rolled, group * 8, 1)
            ext_ref[head // 2, start : start + 8, :] = moved


def halves(block, low):
    zero = jnp.zeros_like(block)
    return jnp.concatenate([jnp.where(low, block, zero), jnp.where(low, zero, block)], 0)


def merge(block, low):
    rows = block.shape[0] // 2
    return jnp.where(low, block[:rows], block[rows:])


def pair_columns(pair, base=0):
    return pl.ds(pl.multiple_of(base + pair * LANES, LANES), LANES)


def penalty_of(rows, first_row, count, seg_col, seg_row):
    i = lax.broadcasted_iota(jnp.int32, (rows, count), 0) + first_row
    j = lax.broadcasted_iota(jnp.int32, (rows, count), 1)
    one = jnp.where((j <= i) & (seg_col == seg_row), 0.0, MASKED).astype(F32)
    return jnp.concatenate([one, one], 0)


def ext_block(ext_ref, pair, rows, shift, count):
    if rows == LANES:
        return ext_ref[pair, :, shift : shift + count]
    return jnp.concatenate(
        [
            ext_ref[pair, 0:rows, shift : shift + count],
            ext_ref[pair, LANES : LANES + rows, shift : shift + count],
        ],
        0,
    )


def self_forward_kernel(qkv_ref, ext_ref, seg_col_ref, seg_row_ref, scale_ref, out_ref, stats_ref):
    length, width = out_ref.shape
    pairs = width // LANES
    blocks = -(-length // LANES)
    lane = lax.broadcasted_iota(jnp.int32, (1, LANES), 1)
    low = lane < HEAD_DIM
    stats_ref[...] = jnp.zeros_like(stats_ref)
    ready(qkv_ref, ext_ref)
    for block in range(blocks):
        start = block * LANES
        rows = min(LANES, length - start)
        count = start + rows
        shift = (blocks - 1 - block) * LANES
        penalty = penalty_of(
            rows, start, count, seg_col_ref[start : start + rows, :], seg_row_ref[:, 0:count]
        )

        def one_pair(pair, carry):
            columns = pair_columns(pair)
            query = halves(qkv_ref[start : start + rows, columns].astype(F32) * SCALE, low).astype(BF)
            key = qkv_ref[0:count, pair_columns(pair, width)]
            value = qkv_ref[0:count, pair_columns(pair, 2 * width)]
            scores = contract(query, key, 1, 1) + (
                ext_block(ext_ref, pair, rows, shift, count) + penalty
            )
            peak = jnp.max(scores, -1, keepdims=True)
            shifted = jnp.exp(scores - peak)
            total = jnp.sum(shifted, -1, keepdims=True)
            weights = (shifted * (1.0 / total)).astype(BF)
            mixed = merge(contract(weights, value, 1, 0), low)
            out_ref[start : start + rows, columns] = (mixed * scale_ref[:, columns]).astype(BF)
            level = peak + jnp.log(total)
            stats_ref[start : start + rows, :] += jnp.where(
                lane == 2 * pair, level[:rows], 0.0
            ) + jnp.where(lane == 2 * pair + 1, level[rows:], 0.0)
            return carry

        lax.fori_loop(0, pairs, one_pair, 0)


def level_of(stats, lane, pair):
    return jnp.concatenate(
        [
            jnp.sum(jnp.where(lane == 2 * pair + side, stats, 0.0), -1, keepdims=True)
            for side in (0, 1)
        ],
        0,
    )


def self_backward_kernel(
    qkv_ref,
    upstream_ref,
    ext_ref,
    seg_col_ref,
    seg_row_ref,
    stats_ref,
    ids_ref,
    grad_ref,
    table_ref,
    head_ref,
    key_sum,
    value_sum,
    offset_sum,
):
    length, width = upstream_ref.shape
    pairs = width // LANES
    blocks = -(-length // LANES)
    lane = lax.broadcasted_iota(jnp.int32, (1, LANES), 1)
    low = lane < HEAD_DIM
    key_sum[...] = jnp.zeros_like(key_sum)
    value_sum[...] = jnp.zeros_like(value_sum)
    offset_sum[...] = jnp.zeros_like(offset_sum)
    ready(qkv_ref, upstream_ref, ext_ref, stats_ref)
    head_ref[...] = jnp.zeros_like(head_ref)
    for block in range(blocks):
        start = block * LANES
        rows = min(LANES, length - start)
        count = start + rows
        shift = (blocks - 1 - block) * LANES
        penalty = penalty_of(
            rows, start, count, seg_col_ref[start : start + rows, :], seg_row_ref[:, 0:count]
        )

        def one_pair(pair, carry):
            columns = pair_columns(pair)
            query = halves(qkv_ref[start : start + rows, columns].astype(F32) * SCALE, low).astype(BF)
            key = qkv_ref[0:count, pair_columns(pair, width)]
            value = qkv_ref[0:count, pair_columns(pair, 2 * width)]
            upstream = halves(upstream_ref[start : start + rows, columns].astype(F32), low).astype(BF)
            level = level_of(stats_ref[start : start + rows, :], lane, pair)
            scores = contract(query, key, 1, 1) + (
                ext_block(ext_ref, pair, rows, shift, count) + penalty
            )
            probs = jnp.exp(scores - level)
            grad_probs = contract(upstream, value, 1, 1)
            inner = jnp.sum(probs * grad_probs, -1, keepdims=True)
            grad_scores = (probs * (grad_probs - inner)).astype(BF)
            weights = probs.astype(BF)
            grad_query = merge(contract(grad_scores, key, 1, 0), low) * SCALE
            grad_ref[start : start + rows, columns] = grad_query.astype(BF)
            key_sum[0:count, columns] += contract(grad_scores, query, 0, 0)
            value_sum[0:count, columns] += contract(weights, upstream, 0, 0)
            wide = grad_scores.astype(F32)
            if rows == LANES:
                offset_sum[pair, :, shift : shift + count] += wide
            else:
                offset_sum[pair, 0:rows, shift : shift + count] += wide[:rows]
                offset_sum[pair, LANES : LANES + rows, shift : shift + count] += wide[rows:]
            for side in (0, 1):
                part = jnp.sum(inner[side * rows : (side + 1) * rows], 0, keepdims=True)
                head_ref[pl.ds(2 * pair + side, 1), :] += jnp.broadcast_to(part, (1, LANES))
            return carry

        lax.fori_loop(0, pairs, one_pair, 0)
    grad_ref[:, width : 2 * width] = key_sum[...].astype(BF)
    grad_ref[:, 2 * width : 3 * width] = value_sum[...].astype(BF)
    span = offset_sum.shape[2]
    sub = lax.broadcasted_iota(jnp.int32, (8, span), 0)
    head_places = lax.broadcasted_iota(jnp.int32, (table_ref.shape[0], span), 0)
    by_offset = jnp.zeros((table_ref.shape[0], span), F32)
    for head in range(2 * pairs):
        total = None
        for group in range(LANES // 8):
            first = (head % 2) * LANES + group * 8
            piece = offset_sum[head // 2, first : first + 8, :]
            moved = piece if group == 0 else pltpu.roll(piece, span - group * 8, 1)
            total = moved if total is None else total + moved
        for bit in (1, 2, 4):
            total = jnp.where((sub & bit) > 0, pltpu.roll(total, span - bit, 1), total)
        line = jnp.sum(total, 0, keepdims=True)
        by_offset = by_offset + jnp.where(head_places == head, line, 0.0)
    choose = choice_of(ids_ref[...], table_ref.shape[1])
    table_ref[...] = contract(by_offset, choose, 1, 1, lax.Precision.HIGHEST)


def norm_parts(values):
    center = values - jnp.mean(values, -1, keepdims=True)
    factor = lax.rsqrt(jnp.mean(center * center, -1, keepdims=True) + EPSILON)
    return center * factor, factor


def norm_back(values, gain, upstream):
    hat, factor = norm_parts(values)
    leaned = upstream * gain
    grad = factor * (
        leaned
        - jnp.mean(leaned, -1, keepdims=True)
        - hat * jnp.mean(leaned * hat, -1, keepdims=True)
    )
    return grad, jnp.sum(upstream * hat, 0), jnp.sum(upstream, 0)


def kv_blocks(key_ref, value_ref, near_ref):
    step = key_ref.shape[0]
    return jnp.concatenate(
        [key_ref[...], near_ref[3 * step : 4 * step, :], value_ref[...], near_ref[4 * step : 5 * step, :]],
        0,
    )


def four_of(own_ref, near_ref, far_ref, across_ref, index):
    step = own_ref.shape[0]
    rows = slice(index * step, (index + 1) * step)
    return jnp.concatenate([own_ref[...], near_ref[rows, :], far_ref[rows, :], across_ref[rows, :]], 0)


def pack_kernel(*refs):
    *blocks, first_ref, trio_ref, sems = refs
    targets = [first_ref] * 5 + [trio_ref] * 3
    copies = []
    for index, (block, target) in enumerate(zip(blocks, targets)):
        start = block.shape[0] * (index % 5)
        copies.append(
            pltpu.make_async_copy(
                block, target.at[start : start + block.shape[0], :], sems.at[index]
            )
        )
    for copy in copies:
        copy.start()
    for copy in copies:
        copy.wait()


def widen_kernel(block_ref, up_ref, down_ref):
    rows = up_ref.shape[0]
    up_ref[...] = block_ref[:rows, :].astype(F32)
    down_ref[...] = block_ref[rows:, :].astype(F32)


def project_kernel(tokens_ref, gains_ref, q0, k0, v0, near_ref, self_in_ref, qkv_ref, weight_ref):
    step = q0.shape[0]
    for index, own in enumerate((q0, k0, v0)):
        weight_ref[2 * index * step : (2 * index + 1) * step, :] = own[...]
        weight_ref[(2 * index + 1) * step : (2 * index + 2) * step, :] = near_ref[
            index * step : (index + 1) * step, :
        ]
    hat, _ = norm_parts(tokens_ref[...].astype(F32))
    self_in = (hat * gains_ref[10:11, :] + gains_ref[11:12, :]).astype(BF)
    self_in_ref[...] = self_in
    qkv_ref[...] = contract(self_in, weight_ref[...], 1, 1).astype(BF)


def memory_kernel(gathered_ref, k0, v0, near_ref, gains_ref, normed_ref, kv_ref, stats_ref, *, count):
    batch, rows = gathered_ref.shape[0], gathered_ref.shape[1] - 16
    sums = None
    for index in range(batch):
        piece = gathered_ref[index, rows : rows + 16, :].astype(F32)
        sums = piece if sums is None else sums + piece
    total = jnp.sum(sums[0:3], 0, keepdims=True) / count
    square = jnp.sum(sums[3:6], 0, keepdims=True) / count
    factor = lax.rsqrt(square - total * total + EPSILON)
    stats_ref[0:1, :] = total
    stats_ref[1:2, :] = factor
    for index in range(batch):
        hat = (gathered_ref[index, 0:rows, :].astype(F32) - total) * factor
        normed_ref[index * rows : (index + 1) * rows, :] = (
            hat * gains_ref[8:9, :] + gains_ref[9:10, :]
        ).astype(BF)
    kv_ref[...] = contract(normed_ref[...], kv_blocks(k0, v0, near_ref), 1, 1).astype(BF)


def mid_forward_kernel(
    keep_ref,
    far_ref,
    tokens_ref,
    o0,
    q0,
    c0,
    near_ref,
    far_trio_ref,
    across_ref,
    kv_ref,
    far_kv_ref,
    valid_ref,
    gains_ref,
    attn_ref,
    first_ref,
    cross_in_ref,
    query_ref,
    mixed_ref,
    cross_attn_ref,
    second_ref,
    ffn_ref,
    stats_ref,
):
    def gain(index):
        return gains_ref[index : index + 1, :]

    half_lanes = keep_ref.shape[1]
    trio = (near_ref, far_trio_ref, across_ref)
    output_all = four_of(o0, *trio, 0)
    attn = contract(keep_ref[...], output_all[:half_lanes], 1, 0) + contract(
        far_ref[...], output_all[half_lanes:], 1, 0
    )
    attn_ref[...] = attn
    first = tokens_ref[...].astype(F32) + norm_parts(attn)[0] * gain(0) + gain(1)
    first_ref[...] = first
    cross_in = (norm_parts(first)[0] * gain(2) + gain(3)).astype(BF)
    cross_in_ref[...] = cross_in
    query_ref[...] = contract(cross_in, four_of(q0, *trio, 1), 1, 1).astype(BF)
    lane = lax.broadcasted_iota(jnp.int32, (1, LANES), 1)
    low = lane < HEAD_DIM
    penalty = jnp.where(valid_ref[...] > 0, 0.0, MASKED).astype(F32)
    stats_ref[...] = jnp.zeros_like(stats_ref)
    ready(kv_ref, far_kv_ref)

    def one_pair(pair, carry):
        for far, source in enumerate((kv_ref, far_kv_ref)):
            columns = pair_columns(pair, far * half_lanes)
            number = pair + far * (half_lanes // LANES)
            query = query_ref[:, columns].astype(F32) * SCALE
            key = source[:, pair_columns(pair)]
            value = source[:, pair_columns(pair, half_lanes)]
            mixed = None
            for side in (0, 1):
                mine = low if side == 0 else jnp.logical_not(low)
                scores = contract(jnp.where(mine, query, 0.0).astype(BF), key, 1, 1) + penalty
                peak = jnp.max(scores, -1, keepdims=True)
                shifted = jnp.exp(scores - peak)
                total = jnp.sum(shifted, -1, keepdims=True)
                weights = (shifted * (1.0 / total)).astype(BF)
                part = contract(weights, value, 1, 0)
                mixed = part if mixed is None else jnp.where(low, mixed, part)
                stats_ref[...] += jnp.where(lane == 2 * number + side, peak + jnp.log(total), 0.0)
            mixed_ref[:, columns] = mixed.astype(BF)
        return carry

    lax.fori_loop(0, half_lanes // LANES, one_pair, 0)
    cross_attn = contract(mixed_ref[...], four_of(c0, *trio, 2), 1, 0)
    cross_attn_ref[...] = cross_attn
    second = first_ref[...] + norm_parts(cross_attn)[0] * gain(4) + gain(5)
    second_ref[...] = second
    ffn_ref[...] = (norm_parts(second)[0] * gain(6) + gain(7)).astype(BF)


def put_blocks(keep_ref, give_ref, place, step, grads):
    block = grads.astype(BF)
    for index in range(block.shape[0] // (2 * step)):
        rows = slice((place + index) * step, (place + index + 1) * step)
        keep_ref[rows, :] = block[2 * index * step : (2 * index + 1) * step]
        give_ref[rows, :] = block[(2 * index + 1) * step : (2 * index + 2) * step]


def mid_backward_kernel(
    back_ref,
    came_ref,
    upstream_ref,
    second_ref,
    cross_attn_ref,
    first_ref,
    attn_ref,
    query_ref,
    stats_ref,
    o0,
    q0,
    c0,
    near_ref,
    far_trio_ref,
    across_ref,
    kv_ref,
    far_kv_ref,
    valid_ref,
    gains_ref,
    scale_ref,
    keep_scaled_ref,
    far_scaled_ref,
    cross_mixed_ref,
    cross_in_ref,
    grad_first_ref,
    keep_ref,
    far_ref,
    grad_kv_ref,
    far_grad_kv_ref,
    norms_ref,
    keep_weights_ref,
    give_weights_ref,
    mixed_ref,
    grad_query_ref,
):
    def gain(index):
        return gains_ref[index : index + 1, :]

    half_lanes = keep_ref.shape[1]
    trio = (near_ref, far_trio_ref, across_ref)
    ffn_grad = back_ref[...] + came_ref[...].astype(F32)
    grad, norms_ref[6, :], norms_ref[7, :] = norm_back(second_ref[...], gain(6), ffn_grad)
    grad_second = upstream_ref[...].astype(F32) + grad
    grad_first_ref[...] = grad_second
    grad, norms_ref[4, :], norms_ref[5, :] = norm_back(cross_attn_ref[...], gain(4), grad_second)
    grad_cattn = grad.astype(BF)
    mixed_ref[...] = contract(grad_cattn, four_of(c0, *trio, 2), 1, 1).astype(BF)
    lane = lax.broadcasted_iota(jnp.int32, (1, LANES), 1)
    low = lane < HEAD_DIM
    penalty = jnp.where(valid_ref[...] > 0, 0.0, MASKED).astype(F32)
    ready(query_ref, stats_ref, kv_ref, far_kv_ref)

    def one_pair(pair, carry):
        for far, source in enumerate((kv_ref, far_kv_ref)):
            columns = pair_columns(pair, far * half_lanes)
            number = pair + far * (half_lanes // LANES)
            query = query_ref[:, columns].astype(F32) * SCALE
            upstream = mixed_ref[:, columns].astype(F32)
            key = source[:, pair_columns(pair)]
            value = source[:, pair_columns(pair, half_lanes)]
            grad_query = grad_key = grad_value = None
            for side in (0, 1):
                mine = low if side == 0 else jnp.logical_not(low)
                my_query = jnp.where(mine, query, 0.0).astype(BF)
                my_upstream = jnp.where(mine, upstream, 0.0).astype(BF)
                level = jnp.sum(
                    jnp.where(lane == 2 * number + side, stats_ref[...], 0.0), -1, keepdims=True
                )
                probs = jnp.exp(contract(my_query, key, 1, 1) + penalty - level)
                grad_probs = contract(my_upstream, value, 1, 1)
                inner = jnp.sum(probs * grad_probs, -1, keepdims=True)
                grad_scores = (probs * (grad_probs - inner)).astype(BF)
                part_query = contract(grad_scores, key, 1, 0)
                part_key = contract(grad_scores, my_query, 0, 0)
                part_value = contract(probs.astype(BF), my_upstream, 0, 0)
                if side == 0:
                    grad_query, grad_key, grad_value = part_query, part_key, part_value
                else:
                    grad_query = jnp.where(low, grad_query, part_query)
                    grad_key, grad_value = grad_key + part_key, grad_value + part_value
            grad_query_ref[:, columns] = (grad_query * SCALE).astype(BF)
            target = far_grad_kv_ref if far else grad_kv_ref
            target[:, pair_columns(pair)] = grad_key.astype(target.dtype)
            target[:, pair_columns(pair, half_lanes)] = grad_value.astype(target.dtype)
        return carry

    lax.fori_loop(0, half_lanes // LANES, one_pair, 0)
    grad_in = contract(grad_query_ref[...], four_of(q0, *trio, 1), 1, 0)
    grad, norms_ref[2, :], norms_ref[3, :] = norm_back(first_ref[...], gain(2), grad_in)
    grad_first = grad_first_ref[...] + grad
    grad_first_ref[...] = grad_first
    grad, norms_ref[0, :], norms_ref[1, :] = norm_back(attn_ref[...], gain(0), grad_first)
    grad_attn = grad.astype(BF)
    grad_mixed = (contract(grad_attn, four_of(o0, *trio, 0), 1, 1) * scale_ref[...]).astype(BF)
    keep_ref[...] = grad_mixed[:, :half_lanes]
    far_ref[...] = grad_mixed[:, half_lanes:]
    step = half_lanes // 2
    put = functools.partial(put_blocks, keep_weights_ref, give_weights_ref)
    low_lanes, high_lanes = slice(0, half_lanes), slice(half_lanes, 2 * half_lanes)
    put(0, step, contract(keep_scaled_ref[...], grad_attn, 0, 0))
    put(1, step, contract(cross_mixed_ref[:, low_lanes], grad_cattn, 0, 0))
    put(2, step, contract(grad_query_ref[:, low_lanes], cross_in_ref[...], 0, 0))
    put(3, step, contract(far_scaled_ref[...], grad_attn, 0, 0))
    put(4, step, contract(cross_mixed_ref[:, high_lanes], grad_cattn, 0, 0))
    put(5, step, contract(grad_query_ref[:, high_lanes], cross_in_ref[...], 0, 0))


def ffn_weights_kernel(
    ffn_own_ref,
    ffn_far_ref,
    gate_own_ref,
    gate_far_ref,
    middle_own_ref,
    middle_far_ref,
    upstream_own_ref,
    upstream_far_ref,
    up_ref,
    down_ref,
    keep_ref,
    give_ref,
    back_ref,
    out_own_ref,
    out_far_ref,
):
    units = keep_ref.shape[0] // 2
    for target, lanes in ((give_ref, slice(units, 2 * units)), (keep_ref, slice(0, units))):
        target[0:units, :] = (
            contract(ffn_own_ref[...], gate_own_ref[:, lanes], 0, 0)
            + contract(ffn_far_ref[...], gate_far_ref[:, lanes], 0, 0)
        ).astype(BF)
        target[units : 2 * units, :] = (
            contract(middle_own_ref[:, lanes], upstream_own_ref[...], 0, 0)
            + contract(middle_far_ref[:, lanes], upstream_far_ref[...], 0, 0)
        ).astype(BF)
    back_ref[...] = contract(gate_own_ref[...], up_ref[...], 1, 1)
    out_far_ref[...] = contract(middle_far_ref[...], down_ref[...], 1, 0).astype(BF)
    out_own_ref[...] = contract(middle_own_ref[...], down_ref[...], 1, 0)


def memory_weights_kernel(
    grad_kv_ref, came_kv_ref, normed_ref, k0, v0, near_ref, keep_ref, give_ref, normed_grad_ref
):
    step = k0.shape[0]
    grad_kv = (grad_kv_ref[...] + came_kv_ref[...].astype(F32)).astype(BF)
    put_blocks(keep_ref, give_ref, 0, step, contract(grad_kv, normed_ref[...], 0, 0))
    normed_grad_ref[...] = contract(grad_kv, kv_blocks(k0, v0, near_ref), 1, 0)


def self_weights_kernel(grad_qkv_ref, self_in_ref, keep_ref, give_ref):
    step = keep_ref.shape[0] // 3
    for index in range(3):
        lanes = slice(2 * index * step, 2 * (index + 1) * step)
        put_blocks(
            keep_ref, give_ref, index, step, contract(grad_qkv_ref[:, lanes], self_in_ref[...], 0, 0)
        )


def flip_over(axis, bit):
    def send(block):
        size = lax.axis_size(axis)
        return lax.ppermute(block, axis, [(i, i ^ bit) for i in range(size)])

    return send


def mate(block):
    return flip_over("mp", 1)(block)


def peer(block):
    return flip_over("mp", 2)(block)


def cut(block, index, size, axis=0):
    return lax.dynamic_slice_in_dim(block, index * size, size, axis)


def dot_right(left, right):
    return contract(left, right, 1, 1)


def dot_left(left, right):
    return contract(left, right, 0, 0)


def dot(left, right):
    return contract(left, right, 1, 0)


def batch_bits():
    size = lax.axis_size("batch")
    bits = []
    while (1 << len(bits)) < size:
        bits.append(1 << len(bits))
    return bits


def mixed_bits(bits, order):
    return [bits[i] for i in order if i < len(bits)] + bits[len(order) :]


def pack_small(parts):
    flat = jnp.concatenate([part.reshape(-1) for part in parts])
    size = -(-flat.shape[0] // (8 * LANES)) * 8 * LANES
    return jnp.pad(flat, (0, size - flat.shape[0])).reshape(-1, LANES)


def unpack_small(packed, shapes):
    flat = packed.reshape(-1)
    parts, start = [], 0
    for shape in shapes:
        size = 1
        for extent in shape:
            size *= extent
        parts.append(flat[start : start + size].reshape(shape))
        start += size
    return parts


def shape_of(shape, dtype):
    return jax.ShapeDtypeStruct(shape, dtype)


def pieces_of(values):
    high = lax.reduce_precision(values, 8, 7)
    middle = lax.reduce_precision(values - high, 8, 7)
    return [high.astype(BF), middle.astype(BF), (values - high - middle).astype(BF)]


def tie(*arrays):
    return lax.optimization_barrier(arrays)


def two_of(index, own, other):
    return jnp.where(index == 0, own, other), jnp.where(index == 0, other, own)


def in_order(index, own, other):
    return jnp.concatenate(two_of(index, own, other), 0)


class Summing:
    def __init__(self, blocks, bits):
        self.blocks = blocks
        self.bits = bits
        self.todo = [("halve", bit) for bit in bits] + [("double", bit) for bit in reversed(bits)]
        self.start = None
        self.size = blocks[0].shape[0]
        self.terms = []
        self.block = None
        self.came = None

    def part(self, start, size):
        total = lax.dynamic_slice_in_dim(self.base, start, size).astype(F32)
        for offset, came in self.terms:
            total = total + lax.dynamic_slice_in_dim(came, start - offset, size).astype(F32)
        return total.astype(BF)

    def prepare(self):
        kind, bit = self.todo.pop(0)
        index = (lax.axis_index("batch") // bit) % 2
        self.kind, self.index, self.bit = kind, index, bit
        if kind == "halve" and self.start is None:
            first, second = self.blocks
            self.base = jnp.where(index == 0, first, second)
            self.give = jnp.where(index == 0, second, first)
            self.start = jnp.int32(0)
        elif kind == "halve":
            self.size = self.size // 2
            self.give = self.part(self.start + (1 - index) * self.size, self.size)
            self.start = self.start + index * self.size
        else:
            if self.block is None:
                self.block = self.part(self.start, self.size)
            self.give = self.block

    def land(self):
        if self.kind == "halve":
            self.terms.append((self.start, self.came))
        elif self.todo:
            self.block = in_order(self.index, self.block, self.came)
        else:
            self.block = two_of(self.index, self.block, self.came)
        self.came = None

    def blocks_of(self, rows):
        whole = jnp.concatenate(self.block, 0)
        return [whole[i : i + rows].astype(F32) for i in range(0, whole.shape[0], rows)]


def advance(flows, *others):
    for flow in flows:
        if flow.came is not None:
            flow.land()
    going = [flow for flow in flows if flow.todo]
    for flow in going:
        flow.prepare()
    ready = tie(*[flow.give for flow in going], *others) if going or others else ()
    for flow, give in zip(going, ready):
        flow.give = give
        flow.came = flip_over("batch", flow.bit)(give)
    return ready[len(going) :]


def finish(flows):
    while any(flow.came is not None for flow in flows):
        advance(flows)


def cost_of(micros):
    return pl.CostEstimate(flops=0, bytes_accessed=int(micros * 3.0e6), transcendentals=0)


def on_device(
    tokens,
    segment_ids,
    bucket_ids,
    memory,
    memory_mask,
    cotangent,
    self_gain,
    self_bias,
    query_weight,
    key_weight,
    value_weight,
    rel_table,
    head_scale,
    output_weight,
    after_gain,
    after_bias,
    cross_gain,
    cross_bias,
    batch_gain,
    batch_bias,
    cross_query,
    cross_key,
    cross_value,
    cross_output,
    crossout_gain,
    crossout_bias,
    ffn_gain,
    ffn_bias,
    up_weight,
    middle_gain,
    middle_bias,
    down_weight,
):
    place = lax.axis_index("mp")
    core, side = place % 2, place // 2
    batch = lax.axis_size("batch")
    bits = batch_bits()
    quarter, _, width = tokens.shape
    length = 4 * quarter
    half = 2 * quarter
    heads = 2 * rel_table.shape[1]
    lanes = heads * HEAD_DIM
    step = lanes // 2
    units = up_weight.shape[1]
    all_hidden = 4 * units
    mem_rows = memory.shape[0]
    positions = mem_rows * batch

    def call(kernel, shapes, micros, late=(), scratch=(), name=None):
        def run(*args):
            taken = list(scratch)
            specs = [pl.BlockSpec(memory_space=pltpu.VMEM)] * len(args)
            wrapped = kernel
            if late:
                for index in late:
                    specs[index] = pl.BlockSpec(memory_space=pltpu.HBM)
                    taken.append(pltpu.VMEM(args[index].shape, args[index].dtype))
                taken.append(pltpu.SemaphoreType.DMA((len(late),)))
                wrapped = with_late(kernel, len(args), late)
            return pl.pallas_call(
                wrapped,
                out_shape=shapes,
                in_specs=specs,
                scratch_shapes=taken,
                compiler_params=kernel_params(late),
                cost_estimate=cost_of(micros),
                name=name,
            )(*args)

        return run

    def rows_of(array):
        return tuple(
            lax.dynamic_index_in_dim(array, index, 1, keepdims=False) for index in (core, 1 - core)
        )

    keep_tokens, give_tokens = rows_of(tokens)
    keep_tokens, give_tokens, memory = tie(keep_tokens, give_tokens, memory)
    far_keep, far_give = peer(keep_tokens), flip_over("mp", 3)(give_tokens)
    near_tokens = mate(give_tokens)

    query_t, key_t, value_t = query_weight.T, key_weight.T, value_weight.T
    own_trio = [output_weight, cross_query.T, cross_output]
    key_c, value_c = cross_key.T, cross_value.T
    all_blocks = [query_t, key_t, value_t, key_c, value_c, *own_trio]
    anywhere = pl.BlockSpec(memory_space=pl.ANY)
    own_first, trio = pl.pallas_call(
        pack_kernel,
        out_shape=tuple(shape_of((count * step, width), BF) for count in (5, 3)),
        in_specs=[anywhere] * len(all_blocks),
        out_specs=(anywhere,) * 2,
        scratch_shapes=[pltpu.SemaphoreType.DMA((len(all_blocks),))],
        compiler_params=pltpu.CompilerParams(vmem_limit_bytes=1024 * 1024),
        cost_estimate=cost_of(3),
        name="pack",
    )(*all_blocks)
    near_first = mate(own_first)
    far_keep, far_give, trio = tie(far_keep, far_give, trio)
    far_trio = peer(trio)
    near_small = unpack_small(
        mate(pack_small([rel_table.T, head_scale, middle_gain, middle_bias])),
        [(heads // 2, rel_table.shape[0]), (heads // 2,), (units,), (units,)],
    )
    both_scale = jnp.concatenate([head_scale, near_small[1]])
    gain_pair = jnp.concatenate([middle_gain, near_small[2]])
    bias_pair = jnp.concatenate([middle_bias, near_small[3]])
    gains = jnp.stack(
        [
            after_gain,
            after_bias,
            cross_gain,
            cross_bias,
            crossout_gain,
            crossout_bias,
            ffn_gain,
            ffn_bias,
            batch_gain,
            batch_bias,
            self_gain,
            self_bias,
        ]
    )

    blocks = -(-length // LANES)
    span = blocks * LANES
    split = length - 1 - (blocks - 1) * LANES
    ids = jnp.concatenate(
        [
            bucket_ids[split:length],
            jnp.full((span - length,), -1, bucket_ids.dtype),
            bucket_ids[:split],
        ]
    )[None, :]
    table = jnp.concatenate([rel_table.T, near_small[0]], 0)
    table = jnp.pad(table, ((0, -heads % 8), (0, 0)))
    ext = call(bias_kernel, shape_of((heads // 2, 2 * LANES, span), F32), 2, name="bias")(ids, table)

    mem_float = memory.astype(F32)
    sums = [jnp.sum(mem_float, (0, 1)), jnp.sum(mem_float * mem_float, (0, 1))]
    extra = jnp.stack([piece for total in sums for piece in pieces_of(total)])
    extra = jnp.broadcast_to(jnp.pad(extra, ((0, 10), (0, 0)))[None], (batch, 16, width))
    rows_here = memory.reshape(mem_rows, batch, 2, width)
    my_rows = jnp.where(core == 0, rows_here[:, :, 0], rows_here[:, :, 1])
    outgoing = jnp.concatenate([jnp.swapaxes(my_rows, 0, 1), extra], 1)
    gathered = lax.all_to_all(outgoing, "batch", split_axis=0, concat_axis=0, tiled=True)
    count = positions * memory.shape[1]
    own_tokens = in_order(core, keep_tokens, near_tokens)
    row_tokens = in_order(side, own_tokens, in_order(core, far_keep, far_give))
    self_in, qkv, qkv_weight = call(
        project_kernel,
        (
            shape_of((length, width), BF),
            shape_of((length, 3 * lanes), BF),
            shape_of((3 * lanes, width), BF),
        ),
        5,
        name="project",
    )(row_tokens, gains, query_t, key_t, value_t, near_first)
    keep_cotangent, give_cotangent = rows_of(cotangent)
    segment = lax.dynamic_index_in_dim(segment_ids, core, 0, keepdims=False)
    seg_col, seg_row = segment[:, None], segment[None, :]
    scale_lanes = jnp.repeat(both_scale, HEAD_DIM)[None, :]
    qkv, gathered = tie(qkv, gathered)
    normed, own_kv, mem_stats = call(
        functools.partial(memory_kernel, count=count),
        (
            shape_of((positions, width), BF),
            shape_of((positions, width), BF),
            shape_of((2, width), F32),
        ),
        0,
        name="memory",
    )(gathered, key_c, value_c, near_first, gains)
    far_kv = peer(own_kv)
    qkv, own_kv, give_cotangent, up_give, down_give, trio = tie(
        qkv, own_kv, give_cotangent, up_weight, down_weight, trio
    )
    near_trio = mate(trio)
    near_cotangent = mate(give_cotangent)
    scaled, stats = call(
        self_forward_kernel,
        (shape_of((length, lanes), BF), shape_of((length, LANES), F32)),
        16,
        name="self_forward",
    )(qkv, ext, seg_col, seg_row, scale_lanes)
    scaled, far_kv, far_trio, near_cotangent = tie(scaled, far_kv, far_trio, near_cotangent)
    keep_scaled, far_scaled = cut(scaled, side, half), peer(cut(scaled, 1 - side, half))
    across_trio = mate(far_trio)
    own_cotangent = in_order(core, keep_cotangent, near_cotangent)
    up_pair = jnp.concatenate([up_weight, mate(up_give)], 1)
    down_pair = jnp.concatenate([down_weight, mate(down_give)], 0)
    far_scaled, own_cotangent, up_pair, down_pair, across_trio = tie(
        far_scaled, own_cotangent, up_pair, down_pair, across_trio
    )
    far_cotangent = peer(own_cotangent)
    trio_args = [*own_trio, near_trio, far_trio, across_trio]

    valid = lax.dynamic_index_in_dim(memory_mask, core, 0, keepdims=True)
    wide, narrow = shape_of((half, width), F32), shape_of((half, width), BF)
    attn, first, cross_in, cross_queries, cross_mixed, cross_attn, second, ffn_own, cross_stats = call(
        mid_forward_kernel,
        (wide, wide, narrow, narrow, narrow, wide, wide, narrow, shape_of((half, LANES), F32)),
        10,
        name="mid_forward",
    )(keep_scaled, far_scaled, own_tokens, *trio_args, own_kv, far_kv, valid, gains)

    ffn_own, far_cotangent = tie(ffn_own, far_cotangent)
    ffn_far = peer(ffn_own)

    def ffn_start(values, grad_middle):
        gate = dot(values, up_pair)
        active = gate * (0.5 * (1.0 + lax.erf(gate * (0.5**0.5))))
        leaned = grad_middle * gain_pair
        sums = jnp.stack(
            [
                jnp.sum(active, -1),
                jnp.sum(active * active, -1),
                jnp.sum(leaned, -1),
                jnp.sum(leaned * active, -1),
            ]
        )
        return gate, sums

    grad_middle_own = dot_right(own_cotangent, down_pair)
    grad_middle_far = dot_right(far_cotangent, down_pair)
    gate_own, sums_own = ffn_start(ffn_own, grad_middle_own)
    ffn_far, grad_middle_far, gate_own, sums_own = tie(ffn_far, grad_middle_far, gate_own, sums_own)
    gate_far, sums_far = ffn_start(ffn_far, grad_middle_far)
    scale_row = jnp.pad(both_scale, (0, half - heads))[None, :]
    came_sums = peer(jnp.concatenate([sums_far, sums_own, scale_row], 0))
    sums_own = (sums_own + came_sums[:4]) / all_hidden
    sums_far = (sums_far + came_sums[4:8]) / all_hidden
    all_scale = jnp.concatenate([both_scale, came_sums[8, :heads]])

    def ffn_end(gate, grad_middle, sums):
        chance = 0.5 * (1.0 + lax.erf(gate * (0.5**0.5)))
        active = gate * chance
        leaned = grad_middle * gain_pair
        act_mean = sums[0][:, None]
        act_scale = lax.rsqrt(sums[1][:, None] - act_mean * act_mean + EPSILON)
        act_hat = (active - act_mean) * act_scale
        middle = (act_hat * gain_pair + bias_pair).astype(BF)
        leaned_mean = sums[2][:, None]
        leaned_hat = act_scale * (sums[3][:, None] - act_mean * leaned_mean)
        grad_active = act_scale * (leaned - leaned_mean - act_hat * leaned_hat)
        density = jnp.exp(-0.5 * gate * gate) * ((2.0 * jnp.pi) ** -0.5)
        grad_gate = (grad_active * (chance + gate * density)).astype(BF)
        return middle, grad_gate, jnp.sum(grad_middle * act_hat, 0), jnp.sum(grad_middle, 0)

    middle_far, gate_grad_far, mid_gain_far, mid_bias_far = ffn_end(
        gate_far, grad_middle_far, sums_far
    )
    back_far = dot_right(gate_grad_far, up_pair).astype(BF)
    back_far, gate_own, grad_middle_own, sums_own = tie(
        back_far, gate_own, grad_middle_own, sums_own
    )
    back_came = peer(back_far)
    middle_own, gate_grad_own, mid_gain_own, mid_bias_own = ffn_end(
        gate_own, grad_middle_own, sums_own
    )
    grad_mid_gain = mid_gain_own + mid_gain_far
    grad_mid_bias = mid_bias_own + mid_bias_far

    wide, narrow = shape_of((half, width), F32), shape_of((half, width), BF)
    both_grads = shape_of((width + units, width), BF)
    keep_ffn, give_ffn, back_own, out_part, out_far = call(
        ffn_weights_kernel,
        (both_grads, both_grads, wide, wide, narrow),
        0,
        name="ffn_weights",
    )(
        ffn_own,
        ffn_far,
        gate_grad_own,
        gate_grad_far,
        middle_own,
        middle_far,
        own_cotangent,
        far_cotangent,
        up_pair,
        down_pair,
    )
    back_came, back_own, give_ffn, out_far = tie(back_came, back_own, give_ffn, out_far)
    part_ffn = (keep_ffn.astype(F32) + mate(give_ffn).astype(F32)).astype(BF)
    back_came, part_ffn = tie(back_came, part_ffn)
    ffn_chunk = lax.psum_scatter(part_ffn, "batch", scatter_dimension=0, tiled=True)

    six = shape_of((6 * step, width), BF)
    (
        grad_first,
        keep_mixed,
        give_mixed,
        grad_kv,
        give_kv,
        norms,
        keep_cross,
        give_cross,
    ) = call(
        mid_backward_kernel,
        (
            wide,
            shape_of((half, lanes), BF),
            shape_of((half, lanes), BF),
            shape_of((positions, width), F32),
            shape_of((positions, width), BF),
            shape_of((8, width), F32),
            six,
            six,
        ),
        16,
        late=(3, 2, 4, 11, 12, 13, 14, 7, 8, 15, 16, 10, 5, 6, 9, 20, 21, 22, 23),
        scratch=[pltpu.VMEM((half, width), BF), pltpu.VMEM((half, width), BF)],
        name="mid_backward",
    )(
        back_own,
        back_came,
        own_cotangent,
        second,
        cross_attn,
        first,
        attn,
        cross_queries,
        cross_stats,
        *trio_args,
        own_kv,
        far_kv,
        valid,
        gains,
        jnp.repeat(all_scale, HEAD_DIM)[None, :],
        keep_scaled,
        far_scaled,
        cross_mixed,
        cross_in,
    )
    came_mixed = peer(give_mixed)
    near_cross = mate(give_cross)
    near_cross, give_kv = tie(near_cross, give_kv)
    came_kv = peer(give_kv)
    far_cross = (keep_cross[3 * step :].astype(F32) + near_cross[3 * step :].astype(F32)).astype(BF)
    grad_mixed = in_order(side, keep_mixed, came_mixed)
    grad_mixed, far_cross = tie(grad_mixed, far_cross)
    came_cross = peer(far_cross)
    grad_qkv, grad_table, grad_heads = call(
        self_backward_kernel,
        (
            shape_of((length, 3 * lanes), BF),
            shape_of(table.shape, F32),
            shape_of((8, LANES), F32),
        ),
        22,
        scratch=[
            pltpu.VMEM((length, lanes), F32),
            pltpu.VMEM((length, lanes), F32),
            pltpu.VMEM(ext.shape, F32),
        ],
        name="self_backward",
    )(qkv, grad_mixed, ext, seg_col, seg_row, stats, ids)
    grad_qkv, came_kv = tie(grad_qkv, came_kv)
    far_in = dot(cut(grad_qkv, 1 - side, half), qkv_weight).astype(BF)
    came_in = peer(far_in)
    grad_qkv, far_in = tie(grad_qkv, far_in)
    keep_last, give_last = call(
        self_weights_kernel,
        (shape_of((3 * step, width), BF), shape_of((3 * step, width), BF)),
        4,
        name="self_weights",
    )(grad_qkv, self_in)
    near_last = mate(give_last)
    keep_mem, give_mem, normed_grad = call(
        memory_weights_kernel,
        (
            shape_of((2 * step, width), BF),
            shape_of((2 * step, width), BF),
            shape_of((positions, width), F32),
        ),
        2,
        late=(0, 1, 2, 3, 4, 5),
        name="memory_weights",
    )(grad_kv, came_kv, normed, key_c, value_c, near_first)
    near_mem = mate(give_mem)

    def add_up(*terms):
        total = terms[0].astype(F32)
        for term in terms[1:]:
            total = total + term.astype(F32)
        return total.astype(BF)

    part_last = add_up(keep_last, near_last)
    some = 3 * step // 2
    last_sum = Summing((part_last[:some], part_last[some:]), mixed_bits(bits, (1, 0, 2)))
    part_cross = jnp.concatenate(
        [add_up(keep_cross[: 3 * step], near_cross[: 3 * step], came_cross), add_up(keep_mem, near_mem)],
        0,
    )
    some = 5 * step // 2
    cross_sum = Summing((part_cross[:some], part_cross[some:]), bits)
    last_flows = [last_sum, cross_sum]
    half_cols = width // 2
    give_normed = cut(normed_grad, 1 - side, half_cols, 1).astype(BF)
    grad_qkv, give_normed, ffn_chunk = advance(last_flows, grad_qkv, give_normed, ffn_chunk)
    came_half = peer(give_normed)
    sum_ffn = lax.all_gather(ffn_chunk, "batch", axis=0, tiled=True)
    def by_quarter(own):
        keep = cut(own, core, quarter)
        came = mate(cut(own, 1 - core, quarter))
        return jnp.stack([jnp.where(core == 0, keep, came), jnp.where(core == 0, came, keep)], 1)

    channels = width // 4
    half_normed = cut(normed_grad, side, half_cols, 1) + came_half.astype(F32)
    keep_normed = cut(half_normed, core, channels, 1)
    give_part = cut(half_normed, 1 - core, channels, 1).astype(BF)
    back_in = dot(cut(grad_qkv, side, half), qkv_weight)
    back_in, came_in, give_part, out_far = advance(last_flows, back_in, came_in, give_part, out_far)
    came_normed = mate(give_part).astype(F32)
    out_came = peer(out_far)
    grad_self_in = back_in + came_in.astype(F32)
    back_tokens, grad_self_gain, grad_self_bias = norm_back(
        own_tokens.astype(F32), self_gain, grad_self_in
    )
    own_grad_tokens = grad_first + back_tokens
    both_normed = jnp.stack(
        [
            jnp.where(core == 0, keep_normed, came_normed),
            jnp.where(core == 0, came_normed, keep_normed),
        ],
        1,
    ).astype(BF)

    own_heads = heads // 2

    def small_of(index):
        mine = slice(index * own_heads, (index + 1) * own_heads)
        some = slice(index * units, (index + 1) * units)
        return pack_small(
            [
                grad_table[mine],
                grad_heads[mine, 0] / both_scale[mine],
                grad_mid_gain[some],
                grad_mid_bias[some],
            ]
        )

    shared = pack_small([norms, grad_self_gain, grad_self_bias])
    keep_small = small_of(0)
    here = shared.shape[0]
    give_small = jnp.concatenate([shared, small_of(1)], 0)
    own_grad_tokens, both_normed, give_small, out_came = advance(
        last_flows, own_grad_tokens, both_normed, give_small, out_came
    )
    came_small = mate(give_small)
    grad_normed = lax.all_to_all(
        both_normed, "batch", split_axis=0, concat_axis=1, tiled=True
    ).astype(F32)
    grad_tokens = by_quarter(own_grad_tokens)
    out_own = (second + out_part + out_came.astype(F32)).astype(BF)
    output = by_quarter(out_own)
    shared = shared + came_small[:here]
    shared = shared + peer(shared)
    shared, grad_normed, grad_tokens, output = advance(
        last_flows, shared, grad_normed, grad_tokens, output
    )
    mean_slice = cut(mem_stats[0], place, channels)
    gain_slice = cut(batch_gain, place, channels)
    scale_slice = cut(mem_stats[1], place, channels)
    hat_slice = (cut(memory, place, channels, 2).astype(F32) - mean_slice) * scale_slice
    shift_term = jnp.sum(grad_normed, (0, 1))
    scale_term = jnp.sum(grad_normed * hat_slice, (0, 1))
    mem_small = pack_small([shift_term, scale_term])
    total = jnp.concatenate([shared, keep_small + came_small[here:], mem_small], 0)
    sum_up, sum_down = call(
        widen_kernel,
        (shape_of((width, width), F32), shape_of((units, width), F32)),
        0,
        name="widen",
    )(sum_ffn)
    for place, bit in enumerate(bits):
        total = total + flip_over("batch", bit)(total)
        if place == 0:
            total, sum_up, sum_down = advance(last_flows, total, sum_up, sum_down)
        else:
            (total,) = advance(last_flows, total)
    finish(last_flows)
    sum_output, sum_coutput, sum_cquery, sum_ckey, sum_cvalue = cross_sum.blocks_of(step)
    sum_query, sum_key, sum_value = last_sum.blocks_of(step)
    there = here + keep_small.shape[0]
    norm_totals = unpack_small(total[:here], [(width,)] * 10)
    sum_table, sum_scale, sum_mid_gain, sum_mid_bias = unpack_small(
        total[here:there], [(own_heads, table.shape[1]), (own_heads,), (units,), (units,)]
    )
    shift_total, scale_total = unpack_small(total[there:], [(channels,), (channels,)])
    grad_memory = (
        gain_slice
        * scale_slice
        * (grad_normed - shift_total / count - hat_slice * scale_total / count)
    )
    return (
        output,
        grad_tokens,
        grad_memory,
        norm_totals[8],
        norm_totals[9],
        sum_query.T,
        sum_key.T,
        sum_value.T,
        sum_table.T,
        sum_scale,
        sum_output,
        norm_totals[0],
        norm_totals[1],
        norm_totals[2],
        norm_totals[3],
        scale_total,
        shift_total,
        sum_cquery.T,
        sum_ckey.T,
        sum_cvalue.T,
        sum_coutput,
        norm_totals[4],
        norm_totals[5],
        norm_totals[6],
        norm_totals[7],
        sum_up,
        sum_mid_gain,
        sum_mid_bias,
        sum_down,
    )


def solution(mesh):
    in_specs = (
        P("mp", "batch", None),
        P("batch", None),
        P(),
        P("batch", None, None),
        P("batch", None),
        P("mp", "batch", None),
        P(),
        P(),
        P(None, "mp"),
        P(None, "mp"),
        P(None, "mp"),
        P(None, "mp"),
        P("mp"),
        P("mp", None),
        P(),
        P(),
        P(),
        P(),
        P(),
        P(),
        P(None, "mp"),
        P(None, "mp"),
        P(None, "mp"),
        P("mp", None),
        P(),
        P(),
        P(),
        P(),
        P(None, "mp"),
        P("mp"),
        P("mp"),
        P("mp", None),
    )
    out_specs = (
        P("mp", "batch", None),
        P("mp", "batch", None),
        P("batch", None, "mp"),
        P(),
        P(),
        P(None, "mp"),
        P(None, "mp"),
        P(None, "mp"),
        P(None, "mp"),
        P("mp"),
        P("mp", None),
        P(),
        P(),
        P(),
        P(),
        P("mp"),
        P("mp"),
        P(None, "mp"),
        P(None, "mp"),
        P(None, "mp"),
        P("mp", None),
        P(),
        P(),
        P(),
        P(),
        P(None, "mp"),
        P("mp"),
        P("mp"),
        P("mp", None),
    )
    return jax.shard_map(
        on_device, mesh=mesh, in_specs=in_specs, out_specs=out_specs, check_vma=False
    )
```

```python
import functools

import jax
import jax.numpy as jnp
from jax import lax
from jax.experimental import pallas as pl
from jax.experimental.pallas import tpu as pltpu
from jax.sharding import PartitionSpec as P

HEAD_DIM = 64
EPSILON = 1e-05
MASKED = -1e30
LANES = 128
BF = jnp.bfloat16
F32 = jnp.float32
SCALE = HEAD_DIM ** (-0.5)
VMEM_LIMIT = 18 * 1024 * 1024
LATE_LIMIT = 58 * 1024 * 1024


def contract(left, right, left_dim, right_dim, precision=None):
    return lax.dot_general(
        left,
        right,
        (((left_dim,), (right_dim,)), ((), ())),
        precision=precision,
        preferred_element_type=F32,
    )


def kernel_params(late=()):
    return pltpu.CompilerParams(vmem_limit_bytes=LATE_LIMIT if late else VMEM_LIMIT)


class Late:
    def __init__(self, source, slot, sem):
        self.slot, self.copy = slot, pltpu.make_async_copy(source, slot, sem)
        self.shape, self.dtype = slot.shape, slot.dtype
        self.copy.start()

    def ready(self):
        if self.copy is not None:
            self.copy.wait()
            self.copy = None

    def __getitem__(self, index):
        self.ready()
        return self.slot[index]


def ready(*refs):
    for ref in refs:
        if isinstance(ref, Late):
            ref.ready()


def with_late(kernel, inputs, late):
    def wrapped(*refs):
        body = list(refs[: -1 - len(late)])
        slots, sems = refs[-1 - len(late) : -1], refs[-1]
        for place, (index, slot) in enumerate(zip(late, slots)):
            body[index] = Late(refs[index], slot, sems.at[place])
        kernel(*body)
        ready(*body[:inputs])

    return wrapped


def choice_of(ids, buckets):
    places = lax.broadcasted_iota(jnp.int32, (buckets, ids.shape[1]), 0)
    return jnp.where(places == ids, 1.0, 0.0).astype(F32)


def bias_kernel(ids_ref, table_ref, ext_ref):
    heads, width = 2 * ext_ref.shape[0], ext_ref.shape[2]
    choose = choice_of(ids_ref[...], table_ref.shape[1])
    by_offset = contract(table_ref[...], choose, 1, 0, lax.Precision.HIGHEST)
    sub = lax.broadcasted_iota(jnp.int32, (8, width), 0)
    for head in range(heads):
        rolled = jnp.broadcast_to(by_offset[head : head + 1, :], (8, width))
        for bit in (1, 2, 4):
            rolled = jnp.where((sub & bit) > 0, pltpu.roll(rolled, bit, 1), rolled)
        for group in range(LANES // 8):
            start = (head % 2) * LANES + group * 8
            moved = rolled if group == 0 else pltpu.roll(rolled, group * 8, 1)
            ext_ref[head // 2, start : start + 8, :] = moved


def halves(block, low):
    zero = jnp.zeros_like(block)
    return jnp.concatenate([jnp.where(low, block, zero), jnp.where(low, zero, block)], 0)


def merge(block, low):
    rows = block.shape[0] // 2
    return jnp.where(low, block[:rows], block[rows:])


def pair_columns(pair, base=0):
    return pl.ds(pl.multiple_of(base + pair * LANES, LANES), LANES)


def penalty_of(rows, first_row, count, seg_col, seg_row):
    i = lax.broadcasted_iota(jnp.int32, (rows, count), 0) + first_row
    j = lax.broadcasted_iota(jnp.int32, (rows, count), 1)
    one = jnp.where((j <= i) & (seg_col == seg_row), 0.0, MASKED).astype(F32)
    return jnp.concatenate([one, one], 0)


def ext_block(ext_ref, pair, rows, shift, count):
    if rows == LANES:
        return ext_ref[pair, :, shift : shift + count]
    return jnp.concatenate(
        [
            ext_ref[pair, 0:rows, shift : shift + count],
            ext_ref[pair, LANES : LANES + rows, shift : shift + count],
        ],
        0,
    )


def self_forward_kernel(qkv_ref, ext_ref, seg_col_ref, seg_row_ref, scale_ref, out_ref, stats_ref):
    length, width = out_ref.shape
    pairs = width // LANES
    blocks = -(-length // LANES)
    lane = lax.broadcasted_iota(jnp.int32, (1, LANES), 1)
    low = lane < HEAD_DIM
    stats_ref[...] = jnp.zeros_like(stats_ref)
    ready(qkv_ref, ext_ref)
    for block in range(blocks):
        start = block * LANES
        rows = min(LANES, length - start)
        count = start + rows
        shift = (blocks - 1 - block) * LANES
        penalty = penalty_of(
            rows, start, count, seg_col_ref[start : start + rows, :], seg_row_ref[:, 0:count]
        )

        def one_pair(pair, carry):
            columns = pair_columns(pair)
            query = halves(qkv_ref[start : start + rows, columns].astype(F32) * SCALE, low).astype(BF)
            key = qkv_ref[0:count, pair_columns(pair, width)]
            value = qkv_ref[0:count, pair_columns(pair, 2 * width)]
            scores = contract(query, key, 1, 1) + (
                ext_block(ext_ref, pair, rows, shift, count) + penalty
            )
            peak = jnp.max(scores, -1, keepdims=True)
            shifted = jnp.exp(scores - peak)
            total = jnp.sum(shifted, -1, keepdims=True)
            weights = (shifted * (1.0 / total)).astype(BF)
            mixed = merge(contract(weights, value, 1, 0), low)
            out_ref[start : start + rows, columns] = (mixed * scale_ref[:, columns]).astype(BF)
            level = peak + jnp.log(total)
            stats_ref[start : start + rows, :] += jnp.where(
                lane == 2 * pair, level[:rows], 0.0
            ) + jnp.where(lane == 2 * pair + 1, level[rows:], 0.0)
            return carry

        lax.fori_loop(0, pairs, one_pair, 0)


def level_of(stats, lane, pair):
    return jnp.concatenate(
        [
            jnp.sum(jnp.where(lane == 2 * pair + side, stats, 0.0), -1, keepdims=True)
            for side in (0, 1)
        ],
        0,
    )


def self_backward_kernel(
    qkv_ref,
    upstream_ref,
    ext_ref,
    seg_col_ref,
    seg_row_ref,
    stats_ref,
    ids_ref,
    grad_ref,
    table_ref,
    head_ref,
    key_sum,
    value_sum,
    offset_sum,
):
    length, width = upstream_ref.shape
    pairs = width // LANES
    blocks = -(-length // LANES)
    lane = lax.broadcasted_iota(jnp.int32, (1, LANES), 1)
    low = lane < HEAD_DIM
    key_sum[...] = jnp.zeros_like(key_sum)
    value_sum[...] = jnp.zeros_like(value_sum)
    offset_sum[...] = jnp.zeros_like(offset_sum)
    ready(qkv_ref, upstream_ref, ext_ref, stats_ref)
    head_ref[...] = jnp.zeros_like(head_ref)
    for block in range(blocks):
        start = block * LANES
        rows = min(LANES, length - start)
        count = start + rows
        shift = (blocks - 1 - block) * LANES
        penalty = penalty_of(
            rows, start, count, seg_col_ref[start : start + rows, :], seg_row_ref[:, 0:count]
        )

        def one_pair(pair, carry):
            columns = pair_columns(pair)
            query = halves(qkv_ref[start : start + rows, columns].astype(F32) * SCALE, low).astype(BF)
            key = qkv_ref[0:count, pair_columns(pair, width)]
            value = qkv_ref[0:count, pair_columns(pair, 2 * width)]
            upstream = halves(upstream_ref[start : start + rows, columns].astype(F32), low).astype(BF)
            level = level_of(stats_ref[start : start + rows, :], lane, pair)
            scores = contract(query, key, 1, 1) + (
                ext_block(ext_ref, pair, rows, shift, count) + penalty
            )
            probs = jnp.exp(scores - level)
            grad_probs = contract(upstream, value, 1, 1)
            inner = jnp.sum(probs * grad_probs, -1, keepdims=True)
            grad_scores = (probs * (grad_probs - inner)).astype(BF)
            weights = probs.astype(BF)
            grad_query = merge(contract(grad_scores, key, 1, 0), low) * SCALE
            grad_ref[start : start + rows, columns] = grad_query.astype(BF)
            key_sum[0:count, columns] += contract(grad_scores, query, 0, 0)
            value_sum[0:count, columns] += contract(weights, upstream, 0, 0)
            wide = grad_scores.astype(F32)
            if rows == LANES:
                offset_sum[pair, :, shift : shift + count] += wide
            else:
                offset_sum[pair, 0:rows, shift : shift + count] += wide[:rows]
                offset_sum[pair, LANES : LANES + rows, shift : shift + count] += wide[rows:]
            for side in (0, 1):
                part = jnp.sum(inner[side * rows : (side + 1) * rows], 0, keepdims=True)
                head_ref[pl.ds(2 * pair + side, 1), :] += jnp.broadcast_to(part, (1, LANES))
            return carry

        lax.fori_loop(0, pairs, one_pair, 0)
    grad_ref[:, width : 2 * width] = key_sum[...].astype(BF)
    grad_ref[:, 2 * width : 3 * width] = value_sum[...].astype(BF)
    span = offset_sum.shape[2]
    sub = lax.broadcasted_iota(jnp.int32, (8, span), 0)
    head_places = lax.broadcasted_iota(jnp.int32, (table_ref.shape[0], span), 0)
    by_offset = jnp.zeros((table_ref.shape[0], span), F32)
    for head in range(2 * pairs):
        total = None
        for group in range(LANES // 8):
            first = (head % 2) * LANES + group * 8
            piece = offset_sum[head // 2, first : first + 8, :]
            moved = piece if group == 0 else pltpu.roll(piece, span - group * 8, 1)
            total = moved if total is None else total + moved
        for bit in (1, 2, 4):
            total = jnp.where((sub & bit) > 0, pltpu.roll(total, span - bit, 1), total)
        line = jnp.sum(total, 0, keepdims=True)
        by_offset = by_offset + jnp.where(head_places == head, line, 0.0)
    choose = choice_of(ids_ref[...], table_ref.shape[1])
    table_ref[...] = contract(by_offset, choose, 1, 1, lax.Precision.HIGHEST)


def norm_parts(values):
    center = values - jnp.mean(values, -1, keepdims=True)
    factor = lax.rsqrt(jnp.mean(center * center, -1, keepdims=True) + EPSILON)
    return center * factor, factor


def norm_back(values, gain, upstream):
    hat, factor = norm_parts(values)
    leaned = upstream * gain
    grad = factor * (
        leaned
        - jnp.mean(leaned, -1, keepdims=True)
        - hat * jnp.mean(leaned * hat, -1, keepdims=True)
    )
    return grad, jnp.sum(upstream * hat, 0), jnp.sum(upstream, 0)


def kv_blocks(key_ref, value_ref, near_ref):
    step = key_ref.shape[0]
    return jnp.concatenate(
        [key_ref[...], near_ref[3 * step : 4 * step, :], value_ref[...], near_ref[4 * step : 5 * step, :]],
        0,
    )


def four_of(own_ref, near_ref, far_ref, across_ref, index):
    step = own_ref.shape[0]
    rows = slice(index * step, (index + 1) * step)
    return jnp.concatenate([own_ref[...], near_ref[rows, :], far_ref[rows, :], across_ref[rows, :]], 0)


def pack_kernel(*refs):
    *blocks, first_ref, trio_ref, sems = refs
    targets = [first_ref] * 5 + [trio_ref] * 3
    copies = []
    for index, (block, target) in enumerate(zip(blocks, targets)):
        start = block.shape[0] * (index % 5)
        copies.append(
            pltpu.make_async_copy(
                block, target.at[start : start + block.shape[0], :], sems.at[index]
            )
        )
    for copy in copies:
        copy.start()
    for copy in copies:
        copy.wait()


def widen_kernel(block_ref, up_ref, down_ref):
    rows = up_ref.shape[0]
    up_ref[...] = block_ref[:rows, :].astype(F32)
    down_ref[...] = block_ref[rows:, :].astype(F32)


def project_kernel(tokens_ref, gains_ref, q0, k0, v0, near_ref, self_in_ref, qkv_ref, weight_ref):
    step = q0.shape[0]
    for index, own in enumerate((q0, k0, v0)):
        weight_ref[2 * index * step : (2 * index + 1) * step, :] = own[...]
        weight_ref[(2 * index + 1) * step : (2 * index + 2) * step, :] = near_ref[
            index * step : (index + 1) * step, :
        ]
    hat, _ = norm_parts(tokens_ref[...].astype(F32))
    self_in = (hat * gains_ref[10:11, :] + gains_ref[11:12, :]).astype(BF)
    self_in_ref[...] = self_in
    qkv_ref[...] = contract(self_in, weight_ref[...], 1, 1).astype(BF)


def memory_kernel(gathered_ref, k0, v0, near_ref, gains_ref, normed_ref, kv_ref, stats_ref, *, count):
    batch, rows = gathered_ref.shape[0], gathered_ref.shape[1] - 16
    sums = None
    for index in range(batch):
        piece = gathered_ref[index, rows : rows + 16, :].astype(F32)
        sums = piece if sums is None else sums + piece
    total = jnp.sum(sums[0:3], 0, keepdims=True) / count
    square = jnp.sum(sums[3:6], 0, keepdims=True) / count
    factor = lax.rsqrt(square - total * total + EPSILON)
    stats_ref[0:1, :] = total
    stats_ref[1:2, :] = factor
    for index in range(batch):
        hat = (gathered_ref[index, 0:rows, :].astype(F32) - total) * factor
        normed_ref[index * rows : (index + 1) * rows, :] = (
            hat * gains_ref[8:9, :] + gains_ref[9:10, :]
        ).astype(BF)
    kv_ref[...] = contract(normed_ref[...], kv_blocks(k0, v0, near_ref), 1, 1).astype(BF)


def mid_forward_kernel(
    keep_ref,
    far_ref,
    tokens_ref,
    o0,
    q0,
    c0,
    near_ref,
    far_trio_ref,
    across_ref,
    kv_ref,
    far_kv_ref,
    valid_ref,
    gains_ref,
    attn_ref,
    first_ref,
    cross_in_ref,
    query_ref,
    mixed_ref,
    cross_attn_ref,
    second_ref,
    ffn_ref,
    stats_ref,
):
    def gain(index):
        return gains_ref[index : index + 1, :]

    half_lanes = keep_ref.shape[1]
    trio = (near_ref, far_trio_ref, across_ref)
    output_all = four_of(o0, *trio, 0)
    attn = contract(keep_ref[...], output_all[:half_lanes], 1, 0) + contract(
        far_ref[...], output_all[half_lanes:], 1, 0
    )
    attn_ref[...] = attn
    first = tokens_ref[...].astype(F32) + norm_parts(attn)[0] * gain(0) + gain(1)
    first_ref[...] = first
    cross_in = (norm_parts(first)[0] * gain(2) + gain(3)).astype(BF)
    cross_in_ref[...] = cross_in
    query_ref[...] = contract(cross_in, four_of(q0, *trio, 1), 1, 1).astype(BF)
    lane = lax.broadcasted_iota(jnp.int32, (1, LANES), 1)
    low = lane < HEAD_DIM
    penalty = jnp.where(valid_ref[...] > 0, 0.0, MASKED).astype(F32)
    stats_ref[...] = jnp.zeros_like(stats_ref)
    ready(kv_ref, far_kv_ref)

    def one_pair(pair, carry):
        for far, source in enumerate((kv_ref, far_kv_ref)):
            columns = pair_columns(pair, far * half_lanes)
            number = pair + far * (half_lanes // LANES)
            query = query_ref[:, columns].astype(F32) * SCALE
            key = source[:, pair_columns(pair)]
            value = source[:, pair_columns(pair, half_lanes)]
            mixed = None
            for side in (0, 1):
                mine = low if side == 0 else jnp.logical_not(low)
                scores = contract(jnp.where(mine, query, 0.0).astype(BF), key, 1, 1) + penalty
                peak = jnp.max(scores, -1, keepdims=True)
                shifted = jnp.exp(scores - peak)
                total = jnp.sum(shifted, -1, keepdims=True)
                weights = (shifted * (1.0 / total)).astype(BF)
                part = contract(weights, value, 1, 0)
                mixed = part if mixed is None else jnp.where(low, mixed, part)
                stats_ref[...] += jnp.where(lane == 2 * number + side, peak + jnp.log(total), 0.0)
            mixed_ref[:, columns] = mixed.astype(BF)
        return carry

    lax.fori_loop(0, half_lanes // LANES, one_pair, 0)
    cross_attn = contract(mixed_ref[...], four_of(c0, *trio, 2), 1, 0)
    cross_attn_ref[...] = cross_attn
    second = first_ref[...] + norm_parts(cross_attn)[0] * gain(4) + gain(5)
    second_ref[...] = second
    ffn_ref[...] = (norm_parts(second)[0] * gain(6) + gain(7)).astype(BF)


def put_blocks(keep_ref, give_ref, place, step, grads):
    block = grads.astype(BF)
    for index in range(block.shape[0] // (2 * step)):
        rows = slice((place + index) * step, (place + index + 1) * step)
        keep_ref[rows, :] = block[2 * index * step : (2 * index + 1) * step]
        give_ref[rows, :] = block[(2 * index + 1) * step : (2 * index + 2) * step]


def mid_backward_kernel(
    back_ref,
    came_ref,
    upstream_ref,
    second_ref,
    cross_attn_ref,
    first_ref,
    attn_ref,
    query_ref,
    stats_ref,
    o0,
    q0,
    c0,
    near_ref,
    far_trio_ref,
    across_ref,
    kv_ref,
    far_kv_ref,
    valid_ref,
    gains_ref,
    scale_ref,
    keep_scaled_ref,
    far_scaled_ref,
    cross_mixed_ref,
    cross_in_ref,
    grad_first_ref,
    keep_ref,
    far_ref,
    grad_kv_ref,
    far_grad_kv_ref,
    norms_ref,
    keep_weights_ref,
    give_weights_ref,
    mixed_ref,
    grad_query_ref,
):
    def gain(index):
        return gains_ref[index : index + 1, :]

    half_lanes = keep_ref.shape[1]
    trio = (near_ref, far_trio_ref, across_ref)
    ffn_grad = back_ref[...] + came_ref[...].astype(F32)
    grad, norms_ref[6, :], norms_ref[7, :] = norm_back(second_ref[...], gain(6), ffn_grad)
    grad_second = upstream_ref[...].astype(F32) + grad
    grad_first_ref[...] = grad_second
    grad, norms_ref[4, :], norms_ref[5, :] = norm_back(cross_attn_ref[...], gain(4), grad_second)
    grad_cattn = grad.astype(BF)
    mixed_ref[...] = contract(grad_cattn, four_of(c0, *trio, 2), 1, 1).astype(BF)
    lane = lax.broadcasted_iota(jnp.int32, (1, LANES), 1)
    low = lane < HEAD_DIM
    penalty = jnp.where(valid_ref[...] > 0, 0.0, MASKED).astype(F32)
    ready(query_ref, stats_ref, kv_ref, far_kv_ref)

    def one_pair(pair, carry):
        for far, source in enumerate((kv_ref, far_kv_ref)):
            columns = pair_columns(pair, far * half_lanes)
            number = pair + far * (half_lanes // LANES)
            query = query_ref[:, columns].astype(F32) * SCALE
            upstream = mixed_ref[:, columns].astype(F32)
            key = source[:, pair_columns(pair)]
            value = source[:, pair_columns(pair, half_lanes)]
            grad_query = grad_key = grad_value = None
            for side in (0, 1):
                mine = low if side == 0 else jnp.logical_not(low)
                my_query = jnp.where(mine, query, 0.0).astype(BF)
                my_upstream = jnp.where(mine, upstream, 0.0).astype(BF)
                level = jnp.sum(
                    jnp.where(lane == 2 * number + side, stats_ref[...], 0.0), -1, keepdims=True
                )
                probs = jnp.exp(contract(my_query, key, 1, 1) + penalty - level)
                grad_probs = contract(my_upstream, value, 1, 1)
                inner = jnp.sum(probs * grad_probs, -1, keepdims=True)
                grad_scores = (probs * (grad_probs - inner)).astype(BF)
                part_query = contract(grad_scores, key, 1, 0)
                part_key = contract(grad_scores, my_query, 0, 0)
                part_value = contract(probs.astype(BF), my_upstream, 0, 0)
                if side == 0:
                    grad_query, grad_key, grad_value = part_query, part_key, part_value
                else:
                    grad_query = jnp.where(low, grad_query, part_query)
                    grad_key, grad_value = grad_key + part_key, grad_value + part_value
            grad_query_ref[:, columns] = (grad_query * SCALE).astype(BF)
            target = far_grad_kv_ref if far else grad_kv_ref
            target[:, pair_columns(pair)] = grad_key.astype(target.dtype)
            target[:, pair_columns(pair, half_lanes)] = grad_value.astype(target.dtype)
        return carry

    lax.fori_loop(0, half_lanes // LANES, one_pair, 0)
    grad_in = contract(grad_query_ref[...], four_of(q0, *trio, 1), 1, 0)
    grad, norms_ref[2, :], norms_ref[3, :] = norm_back(first_ref[...], gain(2), grad_in)
    grad_first = grad_first_ref[...] + grad
    grad_first_ref[...] = grad_first
    grad, norms_ref[0, :], norms_ref[1, :] = norm_back(attn_ref[...], gain(0), grad_first)
    grad_attn = grad.astype(BF)
    grad_mixed = (contract(grad_attn, four_of(o0, *trio, 0), 1, 1) * scale_ref[...]).astype(BF)
    keep_ref[...] = grad_mixed[:, :half_lanes]
    far_ref[...] = grad_mixed[:, half_lanes:]
    step = half_lanes // 2
    put = functools.partial(put_blocks, keep_weights_ref, give_weights_ref)
    low_lanes, high_lanes = slice(0, half_lanes), slice(half_lanes, 2 * half_lanes)
    put(0, step, contract(keep_scaled_ref[...], grad_attn, 0, 0))
    put(1, step, contract(cross_mixed_ref[:, low_lanes], grad_cattn, 0, 0))
    put(2, step, contract(grad_query_ref[:, low_lanes], cross_in_ref[...], 0, 0))
    put(3, step, contract(far_scaled_ref[...], grad_attn, 0, 0))
    put(4, step, contract(cross_mixed_ref[:, high_lanes], grad_cattn, 0, 0))
    put(5, step, contract(grad_query_ref[:, high_lanes], cross_in_ref[...], 0, 0))


def ffn_weights_kernel(
    ffn_own_ref,
    ffn_far_ref,
    gate_own_ref,
    gate_far_ref,
    middle_own_ref,
    middle_far_ref,
    upstream_own_ref,
    upstream_far_ref,
    up_ref,
    down_ref,
    keep_ref,
    give_ref,
    back_ref,
    out_own_ref,
    out_far_ref,
):
    units = keep_ref.shape[0] // 2
    for target, lanes in ((give_ref, slice(units, 2 * units)), (keep_ref, slice(0, units))):
        target[0:units, :] = (
            contract(ffn_own_ref[...], gate_own_ref[:, lanes], 0, 0)
            + contract(ffn_far_ref[...], gate_far_ref[:, lanes], 0, 0)
        ).astype(BF)
        target[units : 2 * units, :] = (
            contract(middle_own_ref[:, lanes], upstream_own_ref[...], 0, 0)
            + contract(middle_far_ref[:, lanes], upstream_far_ref[...], 0, 0)
        ).astype(BF)
    back_ref[...] = contract(gate_own_ref[...], up_ref[...], 1, 1)
    out_far_ref[...] = contract(middle_far_ref[...], down_ref[...], 1, 0).astype(BF)
    out_own_ref[...] = contract(middle_own_ref[...], down_ref[...], 1, 0)


def memory_weights_kernel(
    grad_kv_ref, came_kv_ref, normed_ref, k0, v0, near_ref, keep_ref, give_ref, normed_grad_ref
):
    step = k0.shape[0]
    grad_kv = (grad_kv_ref[...] + came_kv_ref[...].astype(F32)).astype(BF)
    put_blocks(keep_ref, give_ref, 0, step, contract(grad_kv, normed_ref[...], 0, 0))
    normed_grad_ref[...] = contract(grad_kv, kv_blocks(k0, v0, near_ref), 1, 0)


def self_weights_kernel(grad_qkv_ref, self_in_ref, keep_ref, give_ref):
    step = keep_ref.shape[0] // 3
    for index in range(3):
        lanes = slice(2 * index * step, 2 * (index + 1) * step)
        put_blocks(
            keep_ref, give_ref, index, step, contract(grad_qkv_ref[:, lanes], self_in_ref[...], 0, 0)
        )


def flip_over(axis, bit):
    def send(block):
        size = lax.axis_size(axis)
        return lax.ppermute(block, axis, [(i, i ^ bit) for i in range(size)])

    return send


def mate(block):
    return flip_over("mp", 1)(block)


def peer(block):
    return flip_over("mp", 2)(block)


def cut(block, index, size, axis=0):
    return lax.dynamic_slice_in_dim(block, index * size, size, axis)


def dot_right(left, right):
    return contract(left, right, 1, 1)


def dot_left(left, right):
    return contract(left, right, 0, 0)


def dot(left, right):
    return contract(left, right, 1, 0)


def batch_bits():
    size = lax.axis_size("batch")
    bits = []
    while (1 << len(bits)) < size:
        bits.append(1 << len(bits))
    return bits


def mixed_bits(bits, order):
    return [bits[i] for i in order if i < len(bits)] + bits[len(order) :]


def pack_small(parts):
    flat = jnp.concatenate([part.reshape(-1) for part in parts])
    size = -(-flat.shape[0] // (8 * LANES)) * 8 * LANES
    return jnp.pad(flat, (0, size - flat.shape[0])).reshape(-1, LANES)


def unpack_small(packed, shapes):
    flat = packed.reshape(-1)
    parts, start = [], 0
    for shape in shapes:
        size = 1
        for extent in shape:
            size *= extent
        parts.append(flat[start : start + size].reshape(shape))
        start += size
    return parts


def shape_of(shape, dtype):
    return jax.ShapeDtypeStruct(shape, dtype)


def pieces_of(values):
    high = lax.reduce_precision(values, 8, 7)
    middle = lax.reduce_precision(values - high, 8, 7)
    return [high.astype(BF), middle.astype(BF), (values - high - middle).astype(BF)]


def tie(*arrays):
    return lax.optimization_barrier(arrays)


def two_of(index, own, other):
    return jnp.where(index == 0, own, other), jnp.where(index == 0, other, own)


def in_order(index, own, other):
    return jnp.concatenate(two_of(index, own, other), 0)


class Summing:
    def __init__(self, blocks, bits):
        self.blocks = blocks
        self.bits = bits
        self.todo = [("halve", bit) for bit in bits] + [("double", bit) for bit in reversed(bits)]
        self.start = None
        self.size = blocks[0].shape[0]
        self.terms = []
        self.block = None
        self.came = None

    def part(self, start, size):
        total = lax.dynamic_slice_in_dim(self.base, start, size).astype(F32)
        for offset, came in self.terms:
            total = total + lax.dynamic_slice_in_dim(came, start - offset, size).astype(F32)
        return total.astype(BF)

    def prepare(self):
        kind, bit = self.todo.pop(0)
        index = (lax.axis_index("batch") // bit) % 2
        self.kind, self.index, self.bit = kind, index, bit
        if kind == "halve" and self.start is None:
            first, second = self.blocks
            self.base = jnp.where(index == 0, first, second)
            self.give = jnp.where(index == 0, second, first)
            self.start = jnp.int32(0)
        elif kind == "halve":
            self.size = self.size // 2
            self.give = self.part(self.start + (1 - index) * self.size, self.size)
            self.start = self.start + index * self.size
        else:
            if self.block is None:
                self.block = self.part(self.start, self.size)
            self.give = self.block

    def land(self):
        if self.kind == "halve":
            self.terms.append((self.start, self.came))
        elif self.todo:
            self.block = in_order(self.index, self.block, self.came)
        else:
            self.block = two_of(self.index, self.block, self.came)
        self.came = None

    def blocks_of(self, rows):
        whole = jnp.concatenate(self.block, 0)
        return [whole[i : i + rows].astype(F32) for i in range(0, whole.shape[0], rows)]


def advance(flows, *others):
    for flow in flows:
        if flow.came is not None:
            flow.land()
    going = [flow for flow in flows if flow.todo]
    for flow in going:
        flow.prepare()
    ready = tie(*[flow.give for flow in going], *others) if going or others else ()
    for flow, give in zip(going, ready):
        flow.give = give
        flow.came = flip_over("batch", flow.bit)(give)
    return ready[len(going) :]


def finish(flows):
    while any(flow.came is not None for flow in flows):
        advance(flows)


def cost_of(micros):
    return pl.CostEstimate(flops=0, bytes_accessed=int(micros * 3.0e6), transcendentals=0)


def on_device(
    tokens,
    segment_ids,
    bucket_ids,
    memory,
    memory_mask,
    cotangent,
    self_gain,
    self_bias,
    query_weight,
    key_weight,
    value_weight,
    rel_table,
    head_scale,
    output_weight,
    after_gain,
    after_bias,
    cross_gain,
    cross_bias,
    batch_gain,
    batch_bias,
    cross_query,
    cross_key,
    cross_value,
    cross_output,
    crossout_gain,
    crossout_bias,
    ffn_gain,
    ffn_bias,
    up_weight,
    middle_gain,
    middle_bias,
    down_weight,
):
    place = lax.axis_index("mp")
    core, side = place % 2, place // 2
    batch = lax.axis_size("batch")
    bits = batch_bits()
    quarter, _, width = tokens.shape
    length = 4 * quarter
    half = 2 * quarter
    heads = 2 * rel_table.shape[1]
    lanes = heads * HEAD_DIM
    step = lanes // 2
    units = up_weight.shape[1]
    all_hidden = 4 * units
    mem_rows = memory.shape[0]
    positions = mem_rows * batch

    def call(kernel, shapes, micros, late=(), scratch=(), name=None):
        def run(*args):
            taken = list(scratch)
            specs = [pl.BlockSpec(memory_space=pltpu.VMEM)] * len(args)
            wrapped = kernel
            if late:
                for index in late:
                    specs[index] = pl.BlockSpec(memory_space=pltpu.HBM)
                    taken.append(pltpu.VMEM(args[index].shape, args[index].dtype))
                taken.append(pltpu.SemaphoreType.DMA((len(late),)))
                wrapped = with_late(kernel, len(args), late)
            return pl.pallas_call(
                wrapped,
                out_shape=shapes,
                in_specs=specs,
                scratch_shapes=taken,
                compiler_params=kernel_params(late),
                cost_estimate=cost_of(micros),
                name=name,
            )(*args)

        return run

    def rows_of(array):
        return tuple(
            lax.dynamic_index_in_dim(array, index, 1, keepdims=False) for index in (core, 1 - core)
        )

    keep_tokens, give_tokens = rows_of(tokens)
    keep_tokens, give_tokens, memory = tie(keep_tokens, give_tokens, memory)
    far_keep, far_give = peer(keep_tokens), flip_over("mp", 3)(give_tokens)
    near_tokens = mate(give_tokens)

    query_t, key_t, value_t = query_weight.T, key_weight.T, value_weight.T
    own_trio = [output_weight, cross_query.T, cross_output]
    key_c, value_c = cross_key.T, cross_value.T
    all_blocks = [query_t, key_t, value_t, key_c, value_c, *own_trio]
    anywhere = pl.BlockSpec(memory_space=pl.ANY)
    own_first, trio = pl.pallas_call(
        pack_kernel,
        out_shape=tuple(shape_of((count * step, width), BF) for count in (5, 3)),
        in_specs=[anywhere] * len(all_blocks),
        out_specs=(anywhere,) * 2,
        scratch_shapes=[pltpu.SemaphoreType.DMA((len(all_blocks),))],
        compiler_params=pltpu.CompilerParams(vmem_limit_bytes=1024 * 1024),
        cost_estimate=cost_of(3),
        name="pack",
    )(*all_blocks)
    near_first = mate(own_first)
    far_keep, far_give, trio = tie(far_keep, far_give, trio)
    far_trio = peer(trio)
    near_small = unpack_small(
        mate(pack_small([rel_table.T, head_scale, middle_gain, middle_bias])),
        [(heads // 2, rel_table.shape[0]), (heads // 2,), (units,), (units,)],
    )
    both_scale = jnp.concatenate([head_scale, near_small[1]])
    gain_pair = jnp.concatenate([middle_gain, near_small[2]])
    bias_pair = jnp.concatenate([middle_bias, near_small[3]])
    gains = jnp.stack(
        [
            after_gain,
            after_bias,
            cross_gain,
            cross_bias,
            crossout_gain,
            crossout_bias,
            ffn_gain,
            ffn_bias,
            batch_gain,
            batch_bias,
            self_gain,
            self_bias,
        ]
    )

    blocks = -(-length // LANES)
    span = blocks * LANES
    split = length - 1 - (blocks - 1) * LANES
    ids = jnp.concatenate(
        [
            bucket_ids[split:length],
            jnp.full((span - length,), -1, bucket_ids.dtype),
            bucket_ids[:split],
        ]
    )[None, :]
    table = jnp.concatenate([rel_table.T, near_small[0]], 0)
    table = jnp.pad(table, ((0, -heads % 8), (0, 0)))
    ext = call(bias_kernel, shape_of((heads // 2, 2 * LANES, span), F32), 2, name="bias")(ids, table)

    mem_float = memory.astype(F32)
    sums = [jnp.sum(mem_float, (0, 1)), jnp.sum(mem_float * mem_float, (0, 1))]
    extra = jnp.stack([piece for total in sums for piece in pieces_of(total)])
    extra = jnp.broadcast_to(jnp.pad(extra, ((0, 10), (0, 0)))[None], (batch, 16, width))
    rows_here = memory.reshape(mem_rows, batch, 2, width)
    my_rows = jnp.where(core == 0, rows_here[:, :, 0], rows_here[:, :, 1])
    outgoing = jnp.concatenate([jnp.swapaxes(my_rows, 0, 1), extra], 1)
    gathered = lax.all_to_all(outgoing, "batch", split_axis=0, concat_axis=0, tiled=True)
    count = positions * memory.shape[1]
    own_tokens = in_order(core, keep_tokens, near_tokens)
    row_tokens = in_order(side, own_tokens, in_order(core, far_keep, far_give))
    self_in, qkv, qkv_weight = call(
        project_kernel,
        (
            shape_of((length, width), BF),
            shape_of((length, 3 * lanes), BF),
            shape_of((3 * lanes, width), BF),
        ),
        5,
        name="project",
    )(row_tokens, gains, query_t, key_t, value_t, near_first)
    keep_cotangent, give_cotangent = rows_of(cotangent)
    segment = lax.dynamic_index_in_dim(segment_ids, core, 0, keepdims=False)
    seg_col, seg_row = segment[:, None], segment[None, :]
    scale_lanes = jnp.repeat(both_scale, HEAD_DIM)[None, :]
    qkv, gathered = tie(qkv, gathered)
    normed, own_kv, mem_stats = call(
        functools.partial(memory_kernel, count=count),
        (
            shape_of((positions, width), BF),
            shape_of((positions, width), BF),
            shape_of((2, width), F32),
        ),
        0,
        name="memory",
    )(gathered, key_c, value_c, near_first, gains)
    far_kv = peer(own_kv)
    qkv, own_kv, give_cotangent, up_give, down_give, trio = tie(
        qkv, own_kv, give_cotangent, up_weight, down_weight, trio
    )
    near_trio = mate(trio)
    near_cotangent = mate(give_cotangent)
    scaled, stats = call(
        self_forward_kernel,
        (shape_of((length, lanes), BF), shape_of((length, LANES), F32)),
        16,
        name="self_forward",
    )(qkv, ext, seg_col, seg_row, scale_lanes)
    scaled, far_kv, far_trio, near_cotangent = tie(scaled, far_kv, far_trio, near_cotangent)
    keep_scaled, far_scaled = cut(scaled, side, half), peer(cut(scaled, 1 - side, half))
    across_trio = mate(far_trio)
    own_cotangent = in_order(core, keep_cotangent, near_cotangent)
    up_pair = jnp.concatenate([up_weight, mate(up_give)], 1)
    down_pair = jnp.concatenate([down_weight, mate(down_give)], 0)
    far_scaled, own_cotangent, up_pair, down_pair, across_trio = tie(
        far_scaled, own_cotangent, up_pair, down_pair, across_trio
    )
    far_cotangent = peer(own_cotangent)
    trio_args = [*own_trio, near_trio, far_trio, across_trio]

    valid = lax.dynamic_index_in_dim(memory_mask, core, 0, keepdims=True)
    wide, narrow = shape_of((half, width), F32), shape_of((half, width), BF)
    attn, first, cross_in, cross_queries, cross_mixed, cross_attn, second, ffn_own, cross_stats = call(
        mid_forward_kernel,
        (wide, wide, narrow, narrow, narrow, wide, wide, narrow, shape_of((half, LANES), F32)),
        10,
        name="mid_forward",
    )(keep_scaled, far_scaled, own_tokens, *trio_args, own_kv, far_kv, valid, gains)

    ffn_own, far_cotangent = tie(ffn_own, far_cotangent)
    ffn_far = peer(ffn_own)

    def ffn_start(values, grad_middle):
        gate = dot(values, up_pair)
        active = gate * (0.5 * (1.0 + lax.erf(gate * (0.5**0.5))))
        leaned = grad_middle * gain_pair
        sums = jnp.stack(
            [
                jnp.sum(active, -1),
                jnp.sum(active * active, -1),
                jnp.sum(leaned, -1),
                jnp.sum(leaned * active, -1),
            ]
        )
        return gate, sums

    grad_middle_own = dot_right(own_cotangent, down_pair)
    grad_middle_far = dot_right(far_cotangent, down_pair)
    gate_own, sums_own = ffn_start(ffn_own, grad_middle_own)
    ffn_far, grad_middle_far, gate_own, sums_own = tie(ffn_far, grad_middle_far, gate_own, sums_own)
    gate_far, sums_far = ffn_start(ffn_far, grad_middle_far)
    scale_row = jnp.pad(both_scale, (0, half - heads))[None, :]
    came_sums = peer(jnp.concatenate([sums_far, sums_own, scale_row], 0))
    sums_own = (sums_own + came_sums[:4]) / all_hidden
    sums_far = (sums_far + came_sums[4:8]) / all_hidden
    all_scale = jnp.concatenate([both_scale, came_sums[8, :heads]])

    def ffn_end(gate, grad_middle, sums):
        chance = 0.5 * (1.0 + lax.erf(gate * (0.5**0.5)))
        active = gate * chance
        leaned = grad_middle * gain_pair
        act_mean = sums[0][:, None]
        act_scale = lax.rsqrt(sums[1][:, None] - act_mean * act_mean + EPSILON)
        act_hat = (active - act_mean) * act_scale
        middle = (act_hat * gain_pair + bias_pair).astype(BF)
        leaned_mean = sums[2][:, None]
        leaned_hat = act_scale * (sums[3][:, None] - act_mean * leaned_mean)
        grad_active = act_scale * (leaned - leaned_mean - act_hat * leaned_hat)
        density = jnp.exp(-0.5 * gate * gate) * ((2.0 * jnp.pi) ** -0.5)
        grad_gate = (grad_active * (chance + gate * density)).astype(BF)
        return middle, grad_gate, jnp.sum(grad_middle * act_hat, 0), jnp.sum(grad_middle, 0)

    middle_far, gate_grad_far, mid_gain_far, mid_bias_far = ffn_end(
        gate_far, grad_middle_far, sums_far
    )
    back_far = dot_right(gate_grad_far, up_pair).astype(BF)
    back_far, gate_own, grad_middle_own, sums_own = tie(
        back_far, gate_own, grad_middle_own, sums_own
    )
    back_came = peer(back_far)
    middle_own, gate_grad_own, mid_gain_own, mid_bias_own = ffn_end(
        gate_own, grad_middle_own, sums_own
    )
    grad_mid_gain = mid_gain_own + mid_gain_far
    grad_mid_bias = mid_bias_own + mid_bias_far

    wide, narrow = shape_of((half, width), F32), shape_of((half, width), BF)
    both_grads = shape_of((width + units, width), BF)
    keep_ffn, give_ffn, back_own, out_part, out_far = call(
        ffn_weights_kernel,
        (both_grads, both_grads, wide, wide, narrow),
        0,
        name="ffn_weights",
    )(
        ffn_own,
        ffn_far,
        gate_grad_own,
        gate_grad_far,
        middle_own,
        middle_far,
        own_cotangent,
        far_cotangent,
        up_pair,
        down_pair,
    )
    back_came, back_own, give_ffn, out_far = tie(back_came, back_own, give_ffn, out_far)
    part_ffn = (keep_ffn.astype(F32) + mate(give_ffn).astype(F32)).astype(BF)
    back_came, part_ffn = tie(back_came, part_ffn)
    ffn_chunk = lax.psum_scatter(part_ffn, "batch", scatter_dimension=0, tiled=True)

    six = shape_of((6 * step, width), BF)
    (
        grad_first,
        keep_mixed,
        give_mixed,
        grad_kv,
        give_kv,
        norms,
        keep_cross,
        give_cross,
    ) = call(
        mid_backward_kernel,
        (
            wide,
            shape_of((half, lanes), BF),
            shape_of((half, lanes), BF),
            shape_of((positions, width), F32),
            shape_of((positions, width), BF),
            shape_of((8, width), F32),
            six,
            six,
        ),
        16,
        late=(3, 2, 4, 11, 12, 13, 14, 7, 8, 15, 16, 10, 5, 6, 9, 20, 21, 22, 23),
        scratch=[pltpu.VMEM((half, width), BF), pltpu.VMEM((half, width), BF)],
        name="mid_backward",
    )(
        back_own,
        back_came,
        own_cotangent,
        second,
        cross_attn,
        first,
        attn,
        cross_queries,
        cross_stats,
        *trio_args,
        own_kv,
        far_kv,
        valid,
        gains,
        jnp.repeat(all_scale, HEAD_DIM)[None, :],
        keep_scaled,
        far_scaled,
        cross_mixed,
        cross_in,
    )
    came_mixed = peer(give_mixed)
    near_cross = mate(give_cross)
    near_cross, give_kv = tie(near_cross, give_kv)
    came_kv = peer(give_kv)
    far_cross = (keep_cross[3 * step :].astype(F32) + near_cross[3 * step :].astype(F32)).astype(BF)
    grad_mixed = in_order(side, keep_mixed, came_mixed)
    grad_mixed, far_cross = tie(grad_mixed, far_cross)
    came_cross = peer(far_cross)
    grad_qkv, grad_table, grad_heads = call(
        self_backward_kernel,
        (
            shape_of((length, 3 * lanes), BF),
            shape_of(table.shape, F32),
            shape_of((8, LANES), F32),
        ),
        22,
        scratch=[
            pltpu.VMEM((length, lanes), F32),
            pltpu.VMEM((length, lanes), F32),
            pltpu.VMEM(ext.shape, F32),
        ],
        name="self_backward",
    )(qkv, grad_mixed, ext, seg_col, seg_row, stats, ids)
    grad_qkv, came_kv = tie(grad_qkv, came_kv)
    far_in = dot(cut(grad_qkv, 1 - side, half), qkv_weight).astype(BF)
    came_in = peer(far_in)
    grad_qkv, came_kv, far_in = tie(grad_qkv, came_kv, far_in)
    keep_last, give_last = call(
        self_weights_kernel,
        (shape_of((3 * step, width), BF), shape_of((3 * step, width), BF)),
        4,
        name="self_weights",
    )(grad_qkv, self_in)
    near_last = mate(give_last)
    keep_mem, give_mem, normed_grad = call(
        memory_weights_kernel,
        (
            shape_of((2 * step, width), BF),
            shape_of((2 * step, width), BF),
            shape_of((positions, width), F32),
        ),
        2,
        late=(0, 1, 2, 3, 4, 5),
        name="memory_weights",
    )(grad_kv, came_kv, normed, key_c, value_c, near_first)
    near_mem = mate(give_mem)

    def add_up(*terms):
        total = terms[0].astype(F32)
        for term in terms[1:]:
            total = total + term.astype(F32)
        return total.astype(BF)

    part_last = add_up(keep_last, near_last)
    some = 3 * step // 2
    last_sum = Summing((part_last[:some], part_last[some:]), mixed_bits(bits, (1, 0, 2)))
    part_cross = jnp.concatenate(
        [add_up(keep_cross[: 3 * step], near_cross[: 3 * step], came_cross), add_up(keep_mem, near_mem)],
        0,
    )
    some = 5 * step // 2
    cross_sum = Summing((part_cross[:some], part_cross[some:]), bits)
    last_flows = [last_sum, cross_sum]
    half_cols = width // 2
    give_normed = cut(normed_grad, 1 - side, half_cols, 1).astype(BF)
    grad_qkv, give_normed = advance(last_flows, grad_qkv, give_normed)
    came_half = peer(give_normed)
    def by_quarter(own):
        keep = cut(own, core, quarter)
        came = mate(cut(own, 1 - core, quarter))
        return jnp.stack([jnp.where(core == 0, keep, came), jnp.where(core == 0, came, keep)], 1)

    channels = width // 4
    half_normed = cut(normed_grad, side, half_cols, 1) + came_half.astype(F32)
    keep_normed = cut(half_normed, core, channels, 1)
    give_part = cut(half_normed, 1 - core, channels, 1).astype(BF)
    back_in = dot(cut(grad_qkv, side, half), qkv_weight)
    back_in, came_in, give_part, out_far, ffn_chunk = advance(
        last_flows, back_in, came_in, give_part, out_far, ffn_chunk
    )
    sum_ffn = lax.all_gather(ffn_chunk, "batch", axis=0, tiled=True)
    came_normed = mate(give_part).astype(F32)
    out_came = peer(out_far)
    grad_self_in = back_in + came_in.astype(F32)
    back_tokens, grad_self_gain, grad_self_bias = norm_back(
        own_tokens.astype(F32), self_gain, grad_self_in
    )
    own_grad_tokens = grad_first + back_tokens
    both_normed = jnp.stack(
        [
            jnp.where(core == 0, keep_normed, came_normed),
            jnp.where(core == 0, came_normed, keep_normed),
        ],
        1,
    ).astype(BF)

    own_heads = heads // 2

    def small_of(index):
        mine = slice(index * own_heads, (index + 1) * own_heads)
        some = slice(index * units, (index + 1) * units)
        return pack_small(
            [
                grad_table[mine],
                grad_heads[mine, 0] / both_scale[mine],
                grad_mid_gain[some],
                grad_mid_bias[some],
            ]
        )

    shared = pack_small([norms, grad_self_gain, grad_self_bias])
    keep_small = small_of(0)
    here = shared.shape[0]
    give_small = jnp.concatenate([shared, small_of(1)], 0)
    own_grad_tokens, both_normed, give_small, out_came = advance(
        last_flows, own_grad_tokens, both_normed, give_small, out_came
    )
    came_small = mate(give_small)
    grad_normed = lax.all_to_all(
        both_normed, "batch", split_axis=0, concat_axis=1, tiled=True
    ).astype(F32)
    grad_tokens = by_quarter(own_grad_tokens)
    out_own = (second + out_part + out_came.astype(F32)).astype(BF)
    output = by_quarter(out_own)
    shared = shared + came_small[:here]
    shared = shared + peer(shared)
    shared, grad_normed, grad_tokens, output = advance(
        last_flows, shared, grad_normed, grad_tokens, output
    )
    mean_slice = cut(mem_stats[0], place, channels)
    gain_slice = cut(batch_gain, place, channels)
    scale_slice = cut(mem_stats[1], place, channels)
    hat_slice = (cut(memory, place, channels, 2).astype(F32) - mean_slice) * scale_slice
    shift_term = jnp.sum(grad_normed, (0, 1))
    scale_term = jnp.sum(grad_normed * hat_slice, (0, 1))
    mem_small = pack_small([shift_term, scale_term])
    total = jnp.concatenate([shared, keep_small + came_small[here:], mem_small], 0)
    sum_up, sum_down = call(
        widen_kernel,
        (shape_of((width, width), F32), shape_of((units, width), F32)),
        0,
        name="widen",
    )(sum_ffn)
    for place, bit in enumerate(bits):
        total = total + flip_over("batch", bit)(total)
        if place == 0:
            total, sum_up, sum_down = advance(last_flows, total, sum_up, sum_down)
        else:
            (total,) = advance(last_flows, total)
    finish(last_flows)
    sum_output, sum_coutput, sum_cquery, sum_ckey, sum_cvalue = cross_sum.blocks_of(step)
    sum_query, sum_key, sum_value = last_sum.blocks_of(step)
    there = here + keep_small.shape[0]
    norm_totals = unpack_small(total[:here], [(width,)] * 10)
    sum_table, sum_scale, sum_mid_gain, sum_mid_bias = unpack_small(
        total[here:there], [(own_heads, table.shape[1]), (own_heads,), (units,), (units,)]
    )
    shift_total, scale_total = unpack_small(total[there:], [(channels,), (channels,)])
    grad_memory = (
        gain_slice
        * scale_slice
        * (grad_normed - shift_total / count - hat_slice * scale_total / count)
    )
    return (
        output,
        grad_tokens,
        grad_memory,
        norm_totals[8],
        norm_totals[9],
        sum_query.T,
        sum_key.T,
        sum_value.T,
        sum_table.T,
        sum_scale,
        sum_output,
        norm_totals[0],
        norm_totals[1],
        norm_totals[2],
        norm_totals[3],
        scale_total,
        shift_total,
        sum_cquery.T,
        sum_ckey.T,
        sum_cvalue.T,
        sum_coutput,
        norm_totals[4],
        norm_totals[5],
        norm_totals[6],
        norm_totals[7],
        sum_up,
        sum_mid_gain,
        sum_mid_bias,
        sum_down,
    )


def solution(mesh):
    in_specs = (
        P("mp", "batch", None),
        P("batch", None),
        P(),
        P("batch", None, None),
        P("batch", None),
        P("mp", "batch", None),
        P(),
        P(),
        P(None, "mp"),
        P(None, "mp"),
        P(None, "mp"),
        P(None, "mp"),
        P("mp"),
        P("mp", None),
        P(),
        P(),
        P(),
        P(),
        P(),
        P(),
        P(None, "mp"),
        P(None, "mp"),
        P(None, "mp"),
        P("mp", None),
        P(),
        P(),
        P(),
        P(),
        P(None, "mp"),
        P("mp"),
        P("mp"),
        P("mp", None),
    )
    out_specs = (
        P("mp", "batch", None),
        P("mp", "batch", None),
        P("batch", None, "mp"),
        P(),
        P(),
        P(None, "mp"),
        P(None, "mp"),
        P(None, "mp"),
        P(None, "mp"),
        P("mp"),
        P("mp", None),
        P(),
        P(),
        P(),
        P(),
        P("mp"),
        P("mp"),
        P(None, "mp"),
        P(None, "mp"),
        P(None, "mp"),
        P("mp", None),
        P(),
        P(),
        P(),
        P(),
        P(None, "mp"),
        P("mp"),
        P("mp"),
        P("mp", None),
    )
    return jax.shard_map(
        on_device, mesh=mesh, in_specs=in_specs, out_specs=out_specs, check_vma=False
    )
```
